512 devices in a mesh: blk: 64 (over x_lo, z, core), tp: 8 (over y, x_hi).
Axes of the slice: x: 4 (x_hi: 2, x_lo: 2; x = x_hi * 2 + x_lo), y: 4, z: 16, core: 2. Of those that a mesh axis runs over, the one named last changes fastest.
Arguments:
- params: float32 [64, 4096, 1024], P('blk', None, 'tp'), may hold values from -6 to 6
- warm: float32 [64, 8, 1024], P('blk', None, 'tp'), may hold values from -6 to 6
Outputs:
- new_params: float32 [64, 4096, 1024], P('blk', None, 'tp')
- next_warm: float32 [64, 8, 1024], P('blk', None, 'tp')
The draws below stay inside these ranges and needn't reach their ends.
All inputs are finite; a program needn't handle non-finite values.
Results may differ from the reference program's by a relative error of at most 0.0003.
Values sent between devices are 32-bit elements; how exact they have to be, the bound alone decides.
No kernel may reach another device: no remote copies, remote signals or barrier semaphores. Data moves between devices by JAX's collectives and lax.ppermute only.
A program may use at most 64 MiB of HBM per device.

```python
import jax
import jax.numpy as jnp
from jax import lax

D = 4096
KV = 1024
R = 8
STEPS = 2
REPLICAS = 64


def level_of(rng, extent, cuts, smallest, largest):
    factor_of, own = 1.0, jax.random.fold_in(rng, 6)
    for dim, parts in cuts:
        draws = jnp.exp(jax.random.uniform(jax.random.fold_in(own, dim), (parts,), jnp.float32, smallest / len(cuts), largest / len(cuts)))
        factor_of = factor_of * jnp.repeat(draws, extent[dim] // parts).reshape([-1 if axis == dim else 1 for axis in range(len(extent))])
    return factor_of


def centred(stream_key, extent, deviation, bound, split=(), kind=jnp.bfloat16):
    level = level_of(stream_key, extent, split, -0.22, 0.18) if split else 1.0
    values = jax.random.normal(stream_key, extent, jnp.float32) * deviation * level
    return jnp.minimum(jnp.maximum(values, -bound), bound).astype(kind)


def setup_inputs(seed: int = 0) -> dict:
    arg_keys = jax.random.split(jax.random.key(seed), 3)
    params = centred(arg_keys[0], (REPLICAS, D, KV), 1.0, 6.0, ((0, 64), (2, 8)), jnp.float32)
    warm = centred(arg_keys[1], (REPLICAS, R, KV), 1.0, 6.0, ((0, 64), (2, 8)), jnp.float32)
    return dict(params=params, warm=warm)


gossip_rate = 0.5

def orth(rows):
    gram = jnp.dot(rows, rows.T, precision=lax.Precision.HIGHEST)
    lower = jnp.linalg.cholesky(gram)
    return jax.scipy.linalg.solve_triangular(lower, rows, lower=True)

def edge(first, second, start):
    factor = start
    left = None
    for step in range(STEPS):
        left = orth(jnp.dot(factor, first.T, precision=lax.Precision.HIGHEST) - jnp.dot(factor, second.T, precision=lax.Precision.HIGHEST))
        factor = jnp.dot(left, first, precision=lax.Precision.HIGHEST) - jnp.dot(left, second, precision=lax.Precision.HIGHEST)
    return (left, factor)

def reference(params, warm):
    count = params.shape[0]
    order = jnp.arange(count, dtype=jnp.int32)

    def one_edge(index):
        after = ((index + 1) % count).astype(jnp.int32)
        return edge(params[index], params[after], warm[index])
    lefts, rights = lax.map(one_edge, order)

    def update(index):
        before = ((index + count - 1) % count).astype(jnp.int32)
        gain = jnp.dot(lefts[before].T, rights[before], precision=lax.Precision.HIGHEST)
        loss = jnp.dot(lefts[index].T, rights[index], precision=lax.Precision.HIGHEST)
        return params[index] + gossip_rate * (gain - loss)
    new_params = lax.map(update, order)
    return (new_params, rights)
```

```python
import jax
import jax.numpy as jnp
from jax import lax
from jax.experimental import pallas as pl
from jax.experimental.pallas import tpu as pltpu
from jax.sharding import PartitionSpec as P

GOSSIP_RATE = 0.5
HIGHEST = lax.Precision.HIGHEST


def kernel_call(body, out_shape, flops, moved):
    return pl.pallas_call(
        body,
        out_shape=out_shape,
        compiler_params=pltpu.CompilerParams(vmem_limit_bytes=24 << 20),
        cost_estimate=pl.CostEstimate(flops=flops, bytes_accessed=moved, transcendentals=0),
    )


def times_transposed(rows, matrix):
    return lax.dot_general(
        rows, matrix, (((1,), (1,)), ((), ())), precision=HIGHEST,
        preferred_element_type=jnp.float32,
    )


def times(rows, matrix):
    return lax.dot_general(
        rows, matrix, (((1,), (0,)), ((), ())), precision=HIGHEST,
        preferred_element_type=jnp.float32,
    )


def forward_eliminate(gram, columns):
    rank = gram.shape[0]
    row_index = lax.broadcasted_iota(jnp.int32, (rank, 1), 0)
    pivots = jnp.ones((rank, 1), jnp.float32)
    columns = list(columns)
    for k in range(rank):
        pivot = gram[k:k + 1, k:k + 1]
        pivots = jnp.where(row_index == k, pivot, pivots)
        if k + 1 < rank:
            ratio = jnp.where(row_index > k, gram[:, k:k + 1] / pivot, 0.0)
            columns = [c - ratio * c[k:k + 1, :] for c in columns]
            gram = gram - ratio * gram[k:k + 1, :]
    scale = 1.0 / jnp.sqrt(pivots)
    return [c * scale for c in columns]


def first_product(q_ref, mine_ref, next_ref, delta_ref, parts_ref):
    delta = mine_ref[0] - next_ref[0]
    delta_ref[...] = delta
    part = times_transposed(q_ref[0], delta)
    for peer in range(parts_ref.shape[0]):
        parts_ref[peer] = part


def middle_step(parts_ref, delta_ref, out_ref):
    value = parts_ref[0]
    for peer in range(1, parts_ref.shape[0]):
        value = value + parts_ref[peer]
    delta = delta_ref[...]
    gram = times_transposed(value, value)
    image = times(value, delta)
    (factor,) = forward_eliminate(gram, [image])
    part = times_transposed(factor, delta)
    count, _, width = out_ref.shape
    for peer in range(count):
        out_ref[peer] = part[:, peer * width:(peer + 1) * width]


def sum_and_spread(parts_ref, out_ref):
    value = parts_ref[0]
    for peer in range(1, parts_ref.shape[0]):
        value = value + parts_ref[peer]
    for peer in range(out_ref.shape[0]):
        out_ref[peer] = value


def last_step(slices_ref, delta_ref, packed_ref, factor_ref):
    count, rank, width = slices_ref.shape
    for peer in range(count):
        packed_ref[:, peer * width:(peer + 1) * width] = slices_ref[peer]
    value = packed_ref[:, :count * width]
    gram = times_transposed(value, value)
    image = times(value, delta_ref[...])
    unit = (
        lax.broadcasted_iota(jnp.int32, (rank, rank), 0)
        == lax.broadcasted_iota(jnp.int32, (rank, rank), 1)
    ).astype(jnp.float32)
    factor, inverse = forward_eliminate(gram, [image, unit])
    factor_ref[0] = factor
    packed_ref[:, count * width:] = lax.dot_general(
        inverse, factor, (((0,), (0,)), ((), ())), precision=HIGHEST,
        preferred_element_type=jnp.float32,
    )


def update(mine_ref, own_ref, left_ref, new_ref):
    rows = mine_ref.shape[1]
    values = jnp.concatenate([left_ref[:, :rows], own_ref[:, :rows]], axis=0)
    weights = jnp.concatenate([left_ref[:, rows:], -own_ref[:, rows:]], axis=0)
    change = lax.dot_general(
        values, weights, (((0,), (0,)), ((), ())), precision=HIGHEST,
        preferred_element_type=jnp.float32,
    )
    new_ref[0] = mine_ref[0] + GOSSIP_RATE * change


def per_device(params, warm):
    _, rows, columns = params.shape
    rank = warm.shape[1]
    peers = lax.axis_size("tp")
    count = lax.axis_size("blk")
    width = rows // peers
    one = rank * rows * columns * 2
    block = rows * columns * 4
    f32 = jnp.float32

    following = lax.ppermute(params, "blk", [(i, (i - 1) % count) for i in range(count)])
    delta, parts = kernel_call(
        first_product,
        (jax.ShapeDtypeStruct((rows, columns), f32), jax.ShapeDtypeStruct((peers, rank, rows), f32)),
        6 * one, 4 * block,
    )(warm, params, following)
    parts = lax.all_to_all(parts, "tp", 0, 0)
    slices = kernel_call(
        middle_step, jax.ShapeDtypeStruct((peers, rank, width), f32), 12 * one, 2 * block
    )(parts, delta)
    slices = lax.all_to_all(slices, "tp", 0, 0)
    slices = kernel_call(
        sum_and_spread, jax.ShapeDtypeStruct((peers, rank, width), f32), one // 64, block // 8
    )(slices)
    slices = lax.all_to_all(slices, "tp", 0, 0)
    packed, factor = kernel_call(
        last_step,
        (jax.ShapeDtypeStruct((rank, rows + columns), f32), jax.ShapeDtypeStruct((1, rank, columns), f32)),
        6 * one, block,
    )(slices, delta)
    left = lax.ppermute(packed, "blk", [(i, (i + 1) % count) for i in range(count)])
    new_params = kernel_call(
        update, jax.ShapeDtypeStruct((1, rows, columns), f32), 12 * one, 2 * block
    )(params, packed, left)
    return new_params, factor


def solution(mesh):
    spec = P("blk", None, "tp")
    return jax.shard_map(
        per_device, mesh=mesh, in_specs=(spec, spec), out_specs=(spec, spec), check_vma=False
    )
```

```python
import jax
import jax.numpy as jnp
from jax import lax
from jax.experimental import pallas as pl
from jax.experimental.pallas import tpu as pltpu
from jax.sharding import PartitionSpec as P

GOSSIP_RATE = 0.5
HIGHEST = lax.Precision.HIGHEST


def kernel_call(body, out_shape, flops, moved, **blocks):
    return pl.pallas_call(
        body,
        out_shape=out_shape,
        **blocks,
        compiler_params=pltpu.CompilerParams(vmem_limit_bytes=24 << 20),
        cost_estimate=pl.CostEstimate(flops=flops, bytes_accessed=moved, transcendentals=0),
    )


def three_parts(value):
    high = value.astype(jnp.bfloat16)
    rest = value - high.astype(jnp.float32)
    middle = rest.astype(jnp.bfloat16)
    low = (rest - middle.astype(jnp.float32)).astype(jnp.bfloat16)
    return high, middle, low


def stack(parts):
    return jnp.concatenate([p.astype(jnp.float32) for p in parts], axis=0).astype(jnp.bfloat16)


def bf16_dot(a, b, a_dim, b_dim):
    return lax.dot_general(
        a, b, (((a_dim,), (b_dim,)), ((), ())), preferred_element_type=jnp.float32
    )


def split_product(rows, parts, contract):
    rank = rows.shape[0]
    stacked = stack(three_parts(rows))
    total = None
    for taken, part in reversed(list(zip((3, 2, 1), parts))):
        products = bf16_dot(stacked[:taken * rank], part, 1, contract)
        for index in reversed(range(taken)):
            term = products[index * rank:(index + 1) * rank]
            total = term if total is None else total + term
    return total


def gram_of(rows):
    rank = rows.shape[0]
    stacked = stack(three_parts(rows))
    products = bf16_dot(stacked, stacked, 1, 1)
    total = None
    for i, j in ((1, 1), (0, 2), (2, 0), (0, 1), (1, 0), (0, 0)):
        term = products[i * rank:(i + 1) * rank, j * rank:(j + 1) * rank]
        total = term if total is None else total + term
    return total


def outer_product(values, weights):
    left, right = three_parts(values), three_parts(weights)
    pairs = ((1, 1), (0, 2), (2, 0), (0, 1), (1, 0), (0, 0))
    return bf16_dot(stack([left[i] for i, _ in pairs]), stack([right[j] for _, j in pairs]), 0, 0)


def forward_eliminate(gram, columns):
    rank = gram.shape[0]
    row_index = lax.broadcasted_iota(jnp.int32, (rank, 1), 0)
    pivots = jnp.ones((rank, 1), jnp.float32)
    columns = list(columns)
    for k in range(rank):
        pivot = gram[k:k + 1, k:k + 1]
        pivots = jnp.where(row_index == k, pivot, pivots)
        if k + 1 < rank:
            ratio = jnp.where(row_index > k, gram[:, k:k + 1] / pivot, 0.0)
            columns = [c - ratio * c[k:k + 1, :] for c in columns]
            gram = gram - ratio * gram[k:k + 1, :]
    scale = 1.0 / jnp.sqrt(pivots)
    return [c * scale for c in columns]


def own_product(q_ref, matrix_ref, packed_ref, parts_ref):
    rows = matrix_ref.shape[1]
    parts = three_parts(matrix_ref[0])
    for index, part in enumerate(parts):
        parts_ref[index] = part
    packed_ref[:, :rows] = split_product(q_ref[0], parts, 1)
    packed_ref[:, rows:] = q_ref[0]


def spread_first(packed_ref, parts_ref, out_ref):
    rows = parts_ref.shape[1]
    mine = split_product(packed_ref[:, rows:], [parts_ref[i] for i in range(3)], 1)
    part = packed_ref[:, :rows] - mine
    for peer in range(out_ref.shape[0]):
        out_ref[peer] = part


def total_of(parts_ref):
    value = parts_ref[0]
    for peer in range(1, parts_ref.shape[0]):
        value = value + parts_ref[peer]
    return value


def middle_step(sums_ref, mine_ref, left_ref, delta_ref, out_ref):
    value = total_of(sums_ref)
    delta = three_parts(left_ref[0] - mine_ref[0])
    for index, part in enumerate(delta):
        delta_ref[index] = part
    image = split_product(value, delta, 0)
    (factor,) = forward_eliminate(gram_of(value), [image])
    part = split_product(factor, delta, 1)
    for peer in range(out_ref.shape[0]):
        out_ref[peer] = part


def last_step(sums_ref, delta_ref, packed_ref):
    _, rank, rows = sums_ref.shape
    columns = delta_ref.shape[2]
    value = total_of(sums_ref)
    packed_ref[:, :rows] = value
    image = split_product(value, [delta_ref[i] for i in range(3)], 0)
    unit = (
        lax.broadcasted_iota(jnp.int32, (rank, rank), 0)
        == lax.broadcasted_iota(jnp.int32, (rank, rank), 1)
    ).astype(jnp.float32)
    factor, inverse = forward_eliminate(gram_of(value), [image, unit])
    packed_ref[:, rows:rows + columns] = lax.dot_general(
        inverse, factor, (((0,), (0,)), ((), ())), precision=HIGHEST,
        preferred_element_type=jnp.float32,
    )
    packed_ref[:, rows + columns:] = factor


def update_left(matrix_ref, values_ref, weights_ref, new_ref):
    change = outer_product(values_ref[...], GOSSIP_RATE * weights_ref[...])
    new_ref[0] = matrix_ref[0] + change


def update_right(matrix_ref, values_ref, weights_ref, factor_ref, new_ref, warm_ref):
    change = outer_product(values_ref[...], -GOSSIP_RATE * weights_ref[...])
    new_ref[0] = matrix_ref[0] + change
    warm_ref[0] = factor_ref[...]


def per_device(params, warm):
    _, rows, columns = params.shape
    rank = warm.shape[1]
    peers = lax.axis_size("tp")
    count = lax.axis_size("blk")
    one = rank * rows * columns * 2
    block = rows * columns * 4
    f32 = jnp.float32
    to_right = [(i, (i + 1) % count) for i in range(count)]
    to_left = [(i, (i - 1) % count) for i in range(count)]
    spread = jax.ShapeDtypeStruct((peers, rank, rows), f32)
    split = jax.ShapeDtypeStruct((3, rows, columns), jnp.bfloat16)
    matrix = jax.ShapeDtypeStruct((1, rows, columns), f32)

    left_params = lax.ppermute(params, "blk", to_right)
    packed, parts = kernel_call(
        own_product, (jax.ShapeDtypeStruct((rank, rows + columns), f32), split), 6 * one, 2 * block
    )(warm, params)
    packed = lax.ppermute(packed, "blk", to_right)
    sums = kernel_call(spread_first, spread, 6 * one, block)(packed, parts)
    sums = lax.all_to_all(sums, "tp", 0, 0)
    delta, sums = kernel_call(middle_step, (split, spread), 12 * one, 4 * block)(
        sums, params, left_params
    )
    sums = lax.all_to_all(sums, "tp", 0, 0)
    own = kernel_call(
        last_step, jax.ShapeDtypeStruct((rank, rows + 2 * columns), f32), 6 * one, 2 * block
    )(sums, delta)
    right = lax.ppermute(own, "blk", to_left)

    tiles = 4
    tile = rows // tiles
    matrix_spec = pl.BlockSpec((1, tile, columns), lambda i: (0, i, 0))
    values_spec = pl.BlockSpec((rank, tile), lambda i: (0, i))
    weights_spec = pl.BlockSpec((rank, columns), lambda i: (0, rows // columns))
    factor_spec = pl.BlockSpec((rank, columns), lambda i: (0, rows // columns + 1))
    half = kernel_call(
        update_left, matrix, 6 * one, 2 * block, grid=(tiles,),
        in_specs=[matrix_spec, values_spec, weights_spec], out_specs=matrix_spec,
    )(params, own, own)
    new_params, next_warm = kernel_call(
        update_right, (matrix, jax.ShapeDtypeStruct(warm.shape, f32)), 6 * one, 2 * block, grid=(tiles,),
        in_specs=[matrix_spec, values_spec, weights_spec, factor_spec],
        out_specs=(matrix_spec, pl.BlockSpec((1, rank, columns), lambda i: (0, 0, 0))),
    )(half, right, right, right)
    return new_params, next_warm


def solution(mesh):
    spec = P("blk", None, "tp")
    return jax.shard_map(
        per_device, mesh=mesh, in_specs=(spec, spec), out_specs=(spec, spec), check_vma=False
    )
```

```python
import jax
import jax.numpy as jnp
from jax import lax
from jax.experimental import pallas as pl
from jax.experimental.pallas import tpu as pltpu
from jax.sharding import PartitionSpec as P

GOSSIP_RATE = 0.5
TILES = 4
HIGHEST = lax.Precision.HIGHEST


def kernel_call(body, out_shape, flops, moved, **blocks):
    return pl.pallas_call(
        body,
        out_shape=out_shape,
        **blocks,
        compiler_params=pltpu.CompilerParams(vmem_limit_bytes=24 << 20),
        cost_estimate=pl.CostEstimate(flops=flops, bytes_accessed=moved, transcendentals=0),
    )


def three_parts(value):
    high = value.astype(jnp.bfloat16)
    rest = value - high.astype(jnp.float32)
    middle = rest.astype(jnp.bfloat16)
    low = (rest - middle.astype(jnp.float32)).astype(jnp.bfloat16)
    return high, middle, low


def stack(parts):
    return jnp.concatenate([p.astype(jnp.float32) for p in parts], axis=0).astype(jnp.bfloat16)


def bf16_dot(a, b, a_dim, b_dim):
    return lax.dot_general(
        a, b, (((a_dim,), (b_dim,)), ((), ())), preferred_element_type=jnp.float32
    )


def split_product(rows, parts, contract):
    rank = rows.shape[0]
    stacked = stack(three_parts(rows))
    total = None
    for taken, part in reversed(list(zip((3, 2, 1), parts))):
        products = bf16_dot(stacked[:taken * rank], part, 1, contract)
        for index in reversed(range(taken)):
            term = products[index * rank:(index + 1) * rank]
            total = term if total is None else total + term
    return total


def gram_of(rows):
    rank = rows.shape[0]
    stacked = stack(three_parts(rows))
    products = bf16_dot(stacked, stacked, 1, 1)
    total = None
    for i, j in ((1, 1), (0, 2), (2, 0), (0, 1), (1, 0), (0, 0)):
        term = products[i * rank:(i + 1) * rank, j * rank:(j + 1) * rank]
        total = term if total is None else total + term
    return total


def outer_product(values, weights):
    left, right = three_parts(values), three_parts(weights)
    pairs = ((1, 1), (0, 2), (2, 0), (0, 1), (1, 0), (0, 0))
    return bf16_dot(stack([left[i] for i, _ in pairs]), stack([right[j] for _, j in pairs]), 0, 0)


def forward_eliminate(gram, columns):
    rank = gram.shape[0]
    row_index = lax.broadcasted_iota(jnp.int32, (rank, 1), 0)
    pivots = jnp.ones((rank, 1), jnp.float32)
    columns = list(columns)
    for k in range(rank):
        pivot = gram[k:k + 1, k:k + 1]
        pivots = jnp.where(row_index == k, pivot, pivots)
        if k + 1 < rank:
            ratio = jnp.where(row_index > k, gram[:, k:k + 1] / pivot, 0.0)
            columns = [c - ratio * c[k:k + 1, :] for c in columns]
            gram = gram - ratio * gram[k:k + 1, :]
    scale = 1.0 / jnp.sqrt(pivots)
    return [c * scale for c in columns]


def own_product(q_hbm, matrix_hbm, packed_ref, parts_ref, matrix_vmem, q_vmem, sems):
    rows = matrix_vmem.shape[0]
    tile = rows // TILES
    copies = [pltpu.make_async_copy(q_hbm.at[0], q_vmem, sems.at[TILES])]
    for index in range(TILES):
        piece = pl.ds(index * tile, tile)
        copies.append(pltpu.make_async_copy(
            matrix_hbm.at[0, piece], matrix_vmem.at[piece], sems.at[index]
        ))
    for copy in copies:
        copy.start()
    copies[0].wait()
    q = q_vmem[...]
    packed_ref[:, rows:] = q
    for index in range(TILES):
        copies[index + 1].wait()
        piece = pl.ds(index * tile, tile)
        parts = three_parts(matrix_vmem[piece])
        for number, part in enumerate(parts):
            parts_ref[number, piece] = part
        packed_ref[:, piece] = split_product(q, parts, 1)


def spread_first(packed_ref, parts_ref, out_ref):
    rows = parts_ref.shape[1]
    mine = split_product(packed_ref[:, rows:], [parts_ref[i] for i in range(3)], 1)
    part = packed_ref[:, :rows] - mine
    for peer in range(out_ref.shape[0]):
        out_ref[peer] = part


def total_of(parts_ref):
    value = parts_ref[0]
    for peer in range(1, parts_ref.shape[0]):
        value = value + parts_ref[peer]
    return value


def middle_step(sums_ref, mine_ref, left_ref, delta_ref, out_ref):
    value = total_of(sums_ref)
    delta = three_parts(left_ref[0] - mine_ref[...])
    for index, part in enumerate(delta):
        delta_ref[index] = part
    image = split_product(value, delta, 0)
    (factor,) = forward_eliminate(gram_of(value), [image])
    part = split_product(factor, delta, 1)
    for peer in range(out_ref.shape[0]):
        out_ref[peer] = part


def last_step(sums_ref, delta_ref, packed_ref):
    _, rank, rows = sums_ref.shape
    columns = delta_ref.shape[2]
    value = total_of(sums_ref)
    packed_ref[:, :rows] = value
    image = split_product(value, [delta_ref[i] for i in range(3)], 0)
    unit = (
        lax.broadcasted_iota(jnp.int32, (rank, rank), 0)
        == lax.broadcasted_iota(jnp.int32, (rank, rank), 1)
    ).astype(jnp.float32)
    factor, inverse = forward_eliminate(gram_of(value), [image, unit])
    packed_ref[:, rows:rows + columns] = lax.dot_general(
        inverse, factor, (((0,), (0,)), ((), ())), precision=HIGHEST,
        preferred_element_type=jnp.float32,
    )
    packed_ref[:, rows + columns:] = factor


def update_left(matrix_ref, packed_ref, new_ref):
    rows, columns = matrix_ref.shape
    weights = GOSSIP_RATE * packed_ref[:, rows:rows + columns]
    new_ref[...] = matrix_ref[...] + outer_product(packed_ref[:, :rows], weights)


def update_right(matrix_ref, packed_ref, new_hbm, warm_hbm, new_vmem, warm_vmem, sems):
    rows, columns = matrix_ref.shape
    tile = rows // TILES
    warm_vmem[...] = packed_ref[:, rows + columns:]
    copies = [pltpu.make_async_copy(warm_vmem, warm_hbm.at[0], sems.at[TILES])]
    copies[0].start()
    weights = -GOSSIP_RATE * packed_ref[:, rows:rows + columns]
    for index in range(TILES):
        piece = pl.ds(index * tile, tile)
        new_vmem[piece] = matrix_ref[piece] + outer_product(packed_ref[:, piece], weights)
        copy = pltpu.make_async_copy(new_vmem.at[piece], new_hbm.at[0, piece], sems.at[index])
        copy.start()
        copies.append(copy)
    for copy in copies:
        copy.wait()


def per_device(params, warm):
    _, rows, columns = params.shape
    rank = warm.shape[1]
    peers = lax.axis_size("tp")
    count = lax.axis_size("blk")
    one = rank * rows * columns * 2
    block = rows * columns * 4
    f32 = jnp.float32
    to_right = [(i, (i + 1) % count) for i in range(count)]
    to_left = [(i, (i - 1) % count) for i in range(count)]
    spread = jax.ShapeDtypeStruct((peers, rank, rows), f32)
    split = jax.ShapeDtypeStruct((3, rows, columns), jnp.bfloat16)
    matrix = jax.ShapeDtypeStruct((1, rows, columns), f32)

    hbm = pl.BlockSpec(memory_space=pltpu.HBM)
    scratch = [
        pltpu.VMEM((rank, columns), f32), pltpu.VMEM((rows, columns), f32),
        pltpu.SemaphoreType.DMA((TILES + 1,)),
    ]

    packed, parts, mine = kernel_call(
        own_product,
        (jax.ShapeDtypeStruct((rank, rows + columns), f32), split, jax.ShapeDtypeStruct((rows, columns), f32)),
        6 * one, 2 * block, in_specs=[hbm, hbm], scratch_shapes=[scratch[0], scratch[2]],
    )(warm, params)
    packed = lax.ppermute(packed, "blk", to_right)
    later_params, packed = lax.optimization_barrier((params, packed))
    left_params = lax.ppermute(later_params, "blk", to_right)
    sums = kernel_call(spread_first, spread, 6 * one, block)(packed, parts)
    sums = lax.all_to_all(sums, "tp", 0, 0)
    delta, sums = kernel_call(middle_step, (split, spread), 12 * one, 4 * block)(
        sums, mine, left_params
    )
    sums = lax.all_to_all(sums, "tp", 0, 0)
    own = kernel_call(
        last_step, jax.ShapeDtypeStruct((rank, rows + 2 * columns), f32), 6 * one, 2 * block
    )(sums, delta)
    right = lax.ppermute(own, "blk", to_left)

    half = kernel_call(update_left, jax.ShapeDtypeStruct((rows, columns), f32), 6 * one, 2 * block)(mine, own)
    new_params, next_warm = kernel_call(
        update_right, (matrix, jax.ShapeDtypeStruct(warm.shape, f32)), 6 * one, 2 * block,
        out_specs=(hbm, hbm), scratch_shapes=[scratch[1], scratch[0], scratch[2]],
    )(half, right)
    return new_params, next_warm


def solution(mesh):
    spec = P("blk", None, "tp")
    return jax.shard_map(
        per_device, mesh=mesh, in_specs=(spec, spec), out_specs=(spec, spec), check_vma=False
    )
```

```python
import jax
import jax.numpy as jnp
from jax import lax
from jax.experimental import pallas as pl
from jax.experimental.pallas import tpu as pltpu
from jax.sharding import PartitionSpec as P

GOSSIP_RATE = 0.5
TILES = 4
HIGHEST = lax.Precision.HIGHEST


def kernel_call(body, out_shape, flops, moved, **blocks):
    return pl.pallas_call(
        body,
        out_shape=out_shape,
        **blocks,
        compiler_params=pltpu.CompilerParams(vmem_limit_bytes=24 << 20),
        cost_estimate=pl.CostEstimate(flops=flops, bytes_accessed=moved, transcendentals=0),
    )


def three_parts(value):
    high = value.astype(jnp.bfloat16)
    rest = value - high.astype(jnp.float32)
    middle = rest.astype(jnp.bfloat16)
    low = (rest - middle.astype(jnp.float32)).astype(jnp.bfloat16)
    return high, middle, low


def stack(parts):
    return jnp.concatenate([p.astype(jnp.float32) for p in parts], axis=0).astype(jnp.bfloat16)


def bf16_dot(a, b, a_dim, b_dim):
    return lax.dot_general(
        a, b, (((a_dim,), (b_dim,)), ((), ())), preferred_element_type=jnp.float32
    )


def split_product(rows, parts, contract):
    rank = rows.shape[0]
    stacked = stack(three_parts(rows))
    total = None
    for taken, part in reversed(list(zip((3, 2, 1), parts))):
        products = bf16_dot(stacked[:taken * rank], part, 1, contract)
        for index in reversed(range(taken)):
            term = products[index * rank:(index + 1) * rank]
            total = term if total is None else total + term
    return total


def gram_of(rows):
    rank = rows.shape[0]
    stacked = stack(three_parts(rows))
    products = bf16_dot(stacked, stacked, 1, 1)
    total = None
    for i, j in ((1, 1), (0, 2), (2, 0), (0, 1), (1, 0), (0, 0)):
        term = products[i * rank:(i + 1) * rank, j * rank:(j + 1) * rank]
        total = term if total is None else total + term
    return total


def outer_product(values, weights):
    left, right = three_parts(values), three_parts(weights)
    pairs = ((1, 1), (0, 2), (2, 0), (0, 1), (1, 0), (0, 0))
    return bf16_dot(stack([left[i] for i, _ in pairs]), stack([right[j] for _, j in pairs]), 0, 0)


def forward_eliminate(gram, columns):
    rank = gram.shape[0]
    row_index = lax.broadcasted_iota(jnp.int32, (rank, 1), 0)
    pivots = jnp.ones((rank, 1), jnp.float32)
    columns = list(columns)
    for k in range(rank):
        pivot = gram[k:k + 1, k:k + 1]
        pivots = jnp.where(row_index == k, pivot, pivots)
        if k + 1 < rank:
            ratio = jnp.where(row_index > k, gram[:, k:k + 1] / pivot, 0.0)
            columns = [c - ratio * c[k:k + 1, :] for c in columns]
            gram = gram - ratio * gram[k:k + 1, :]
    scale = 1.0 / jnp.sqrt(pivots)
    return [c * scale for c in columns]


def own_product(q_hbm, matrix_hbm, packed_ref, parts_ref, mine_ref, q_vmem, sems):
    rows = mine_ref.shape[0]
    tile = rows // TILES
    copies = [pltpu.make_async_copy(q_hbm.at[0], q_vmem, sems.at[TILES])]
    for index in range(TILES):
        piece = pl.ds(index * tile, tile)
        copies.append(pltpu.make_async_copy(
            matrix_hbm.at[0, piece], mine_ref.at[piece], sems.at[index]
        ))
    for copy in copies:
        copy.start()
    copies[0].wait()
    q = q_vmem[...]
    packed_ref[:, rows:] = q
    for index in range(TILES):
        copies[index + 1].wait()
        piece = pl.ds(index * tile, tile)
        parts = three_parts(mine_ref[piece])
        for number, part in enumerate(parts):
            parts_ref[number, piece] = part
        packed_ref[:, piece] = split_product(q, parts, 1)


def spread_first(packed_ref, parts_ref, out_ref):
    rows = parts_ref.shape[1]
    mine = split_product(packed_ref[:, rows:], [parts_ref[i] for i in range(3)], 1)
    part = packed_ref[:, :rows] - mine
    for peer in range(out_ref.shape[0]):
        out_ref[peer] = part


def total_of(sums_ref):
    value = sums_ref[0]
    for peer in range(1, sums_ref.shape[0]):
        value = value + sums_ref[peer]
    return value


def add_up(sums_ref, out_ref):
    out_ref[...] = total_of(sums_ref)


def middle_step(sum_ref, other_ref, mine_ref, left_ref, delta_ref, out_ref):
    value = sum_ref[...] + other_ref[...]
    delta = three_parts(left_ref[0] - mine_ref[...])
    for index, part in enumerate(delta):
        delta_ref[index] = part
    image = split_product(value, delta, 0)
    (factor,) = forward_eliminate(gram_of(value), [image])
    part = split_product(factor, delta, 1)
    for peer in range(out_ref.shape[0]):
        out_ref[peer] = part


def last_step(sum_ref, other_ref, delta_ref, packed_ref):
    rank, rows = sum_ref.shape
    columns = delta_ref.shape[2]
    value = sum_ref[...] + other_ref[...]
    packed_ref[:, :rows] = value
    image = split_product(value, [delta_ref[i] for i in range(3)], 0)
    unit = (
        lax.broadcasted_iota(jnp.int32, (rank, rank), 0)
        == lax.broadcasted_iota(jnp.int32, (rank, rank), 1)
    ).astype(jnp.float32)
    factor, inverse = forward_eliminate(gram_of(value), [image, unit])
    packed_ref[:, rows:rows + columns] = lax.dot_general(
        inverse, factor, (((0,), (0,)), ((), ())), precision=HIGHEST,
        preferred_element_type=jnp.float32,
    )
    packed_ref[:, rows + columns:] = factor


def update_left(matrix_ref, packed_ref, new_ref):
    rows, columns = matrix_ref.shape
    weights = GOSSIP_RATE * packed_ref[:, rows:rows + columns]
    new_ref[...] = matrix_ref[...] + outer_product(packed_ref[:, :rows], weights)


def update_right(matrix_ref, packed_ref, new_hbm, warm_hbm, new_vmem, warm_vmem, sems):
    rows, columns = matrix_ref.shape
    tile = rows // TILES
    warm_vmem[...] = packed_ref[:, rows + columns:]
    copies = [pltpu.make_async_copy(warm_vmem, warm_hbm.at[0], sems.at[TILES])]
    copies[0].start()
    weights = -GOSSIP_RATE * packed_ref[:, rows:rows + columns]
    for index in range(TILES):
        piece = pl.ds(index * tile, tile)
        new_vmem[piece] = matrix_ref[piece] + outer_product(packed_ref[:, piece], weights)
        copy = pltpu.make_async_copy(new_vmem.at[piece], new_hbm.at[0, piece], sems.at[index])
        copy.start()
        copies.append(copy)
    for copy in copies:
        copy.wait()


def sum_over_tp(spread):
    peers = lax.axis_size("tp")
    groups = [list(range(start, peers, 2)) for start in range(2)]
    spread = lax.all_to_all(spread, "tp", 0, 0, axis_index_groups=groups)
    _, rank, rows = spread.shape
    total = kernel_call(
        add_up, jax.ShapeDtypeStruct((rank, rows), jnp.float32), spread.size, 4 * spread.size
    )(spread)
    other = lax.ppermute(total, "tp", [(i, i ^ 1) for i in range(peers)])
    return total, other


def per_device(params, warm):
    _, rows, columns = params.shape
    rank = warm.shape[1]
    peers = lax.axis_size("tp")
    count = lax.axis_size("blk")
    one = rank * rows * columns * 2
    block = rows * columns * 4
    f32 = jnp.float32
    to_right = [(i, (i + 1) % count) for i in range(count)]
    to_left = [(i, (i - 1) % count) for i in range(count)]
    spread = jax.ShapeDtypeStruct((peers // 2, rank, rows), f32)
    split = jax.ShapeDtypeStruct((3, rows, columns), jnp.bfloat16)
    matrix = jax.ShapeDtypeStruct((rows, columns), f32)
    hbm = pl.BlockSpec(memory_space=pltpu.HBM)
    factor_scratch = pltpu.VMEM((rank, columns), f32)
    sems = pltpu.SemaphoreType.DMA((TILES + 1,))

    packed, parts, mine = kernel_call(
        own_product, (jax.ShapeDtypeStruct((rank, rows + columns), f32), split, matrix),
        6 * one, 2 * block, in_specs=[hbm, hbm], scratch_shapes=[factor_scratch, sems],
    )(warm, params)
    packed = lax.ppermute(packed, "blk", to_right)
    later_params, packed = lax.optimization_barrier((params, packed))
    left_params = lax.ppermute(later_params, "blk", to_right)
    sums = kernel_call(spread_first, spread, 6 * one, block)(packed, parts)
    total, other = sum_over_tp(sums)
    delta, sums = kernel_call(middle_step, (split, spread), 12 * one, 4 * block)(
        total, other, mine, left_params
    )
    total, other = sum_over_tp(sums)
    own = kernel_call(
        last_step, jax.ShapeDtypeStruct((rank, rows + 2 * columns), f32), 6 * one, 2 * block
    )(total, other, delta)
    right = lax.ppermute(own, "blk", to_left)
    left_done = kernel_call(update_left, matrix, 6 * one, 2 * block)(mine, own)
    new_params, next_warm = kernel_call(
        update_right,
        (jax.ShapeDtypeStruct(params.shape, f32), jax.ShapeDtypeStruct(warm.shape, f32)),
        6 * one, 2 * block, out_specs=(hbm, hbm),
        scratch_shapes=[pltpu.VMEM(matrix.shape, f32), factor_scratch, sems],
    )(left_done, right)
    return new_params, next_warm


def solution(mesh):
    spec = P("blk", None, "tp")
    return jax.shard_map(
        per_device, mesh=mesh, in_specs=(spec, spec), out_specs=(spec, spec), check_vma=False
    )
```

```python
import jax
import jax.numpy as jnp
from jax import lax
from jax.experimental import pallas as pl
from jax.experimental.pallas import tpu as pltpu
from jax.sharding import PartitionSpec as P

GOSSIP_RATE = 0.5
TILES = 4
HIGHEST = lax.Precision.HIGHEST


def kernel_call(body, out_shape, flops, moved, **blocks):
    return pl.pallas_call(
        body,
        out_shape=out_shape,
        **blocks,
        compiler_params=pltpu.CompilerParams(vmem_limit_bytes=24 << 20),
        cost_estimate=pl.CostEstimate(flops=flops, bytes_accessed=moved, transcendentals=0),
    )


def three_parts(value):
    high = value.astype(jnp.bfloat16)
    rest = value - high.astype(jnp.float32)
    middle = rest.astype(jnp.bfloat16)
    low = (rest - middle.astype(jnp.float32)).astype(jnp.bfloat16)
    return high, middle, low


def stack(parts):
    return jnp.concatenate([p.astype(jnp.float32) for p in parts], axis=0).astype(jnp.bfloat16)


def bf16_dot(a, b, a_dim, b_dim):
    return lax.dot_general(
        a, b, (((a_dim,), (b_dim,)), ((), ())), preferred_element_type=jnp.float32
    )


def split_product(rows, parts, contract):
    rank = rows.shape[0]
    stacked = stack(three_parts(rows))
    total = None
    for taken, part in reversed(list(zip((3, 2, 1), parts))):
        products = bf16_dot(stacked[:taken * rank], part, 1, contract)
        for index in reversed(range(taken)):
            term = products[index * rank:(index + 1) * rank]
            total = term if total is None else total + term
    return total


def gram_of(rows):
    rank = rows.shape[0]
    stacked = stack(three_parts(rows))
    products = bf16_dot(stacked, stacked, 1, 1)
    total = None
    for i, j in ((1, 1), (0, 2), (2, 0), (0, 1), (1, 0), (0, 0)):
        term = products[i * rank:(i + 1) * rank, j * rank:(j + 1) * rank]
        total = term if total is None else total + term
    return total


def outer_product(values, weights):
    left, right = three_parts(values), three_parts(weights)
    pairs = ((1, 1), (0, 2), (2, 0), (0, 1), (1, 0), (0, 0))
    return bf16_dot(stack([left[i] for i, _ in pairs]), stack([right[j] for _, j in pairs]), 0, 0)


def forward_eliminate(gram, columns):
    rank = gram.shape[0]
    row_index = lax.broadcasted_iota(jnp.int32, (rank, 1), 0)
    pivots = jnp.ones((rank, 1), jnp.float32)
    columns = list(columns)
    for k in range(rank):
        pivot = gram[k:k + 1, k:k + 1]
        pivots = jnp.where(row_index == k, pivot, pivots)
        if k + 1 < rank:
            ratio = jnp.where(row_index > k, gram[:, k:k + 1] / pivot, 0.0)
            columns = [c - ratio * c[k:k + 1, :] for c in columns]
            gram = gram - ratio * gram[k:k + 1, :]
    scale = 1.0 / jnp.sqrt(pivots)
    return [c * scale for c in columns]


def own_product(q_hbm, matrix_hbm, packed_ref, parts_ref, mine_ref, q_vmem, sems):
    rows = mine_ref.shape[0]
    tile = rows // TILES
    copies = [pltpu.make_async_copy(q_hbm.at[0], q_vmem, sems.at[TILES])]
    for index in range(TILES):
        piece = pl.ds(index * tile, tile)
        copies.append(pltpu.make_async_copy(
            matrix_hbm.at[0, piece], mine_ref.at[piece], sems.at[index]
        ))
    for copy in copies:
        copy.start()
    copies[0].wait()
    q = q_vmem[...]
    packed_ref[:, rows:] = q
    for index in range(TILES):
        copies[index + 1].wait()
        piece = pl.ds(index * tile, tile)
        parts = three_parts(mine_ref[piece])
        for number, part in enumerate(parts):
            parts_ref[number, piece] = part
        packed_ref[:, piece] = split_product(q, parts, 1)


def spread_first(packed_ref, parts_ref, out_ref):
    rows = parts_ref.shape[1]
    mine = split_product(packed_ref[:, rows:], [parts_ref[i] for i in range(3)], 1)
    part = packed_ref[:, :rows] - mine
    for peer in range(out_ref.shape[0]):
        out_ref[peer] = part


def total_of(sums_ref):
    value = sums_ref[0]
    for peer in range(1, sums_ref.shape[0]):
        value = value + sums_ref[peer]
    return value


def add_up(sums_ref, out_ref):
    out_ref[...] = total_of(sums_ref)


def middle_step(sum_ref, other_ref, mine_ref, left_ref, delta_ref, out_ref):
    value = sum_ref[...] + other_ref[...]
    delta = three_parts(left_ref[0] - mine_ref[...])
    for index, part in enumerate(delta):
        delta_ref[index] = part
    image = split_product(value, delta, 0)
    (factor,) = forward_eliminate(gram_of(value), [image])
    part = split_product(factor, delta, 1)
    for peer in range(out_ref.shape[0]):
        out_ref[peer] = part


def last_step(sum_ref, other_ref, delta_ref, packed_ref):
    rank, rows = sum_ref.shape
    columns = delta_ref.shape[2]
    value = sum_ref[...] + other_ref[...]
    packed_ref[:, :rows] = value
    image = split_product(value, [delta_ref[i] for i in range(3)], 0)
    unit = (
        lax.broadcasted_iota(jnp.int32, (rank, rank), 0)
        == lax.broadcasted_iota(jnp.int32, (rank, rank), 1)
    ).astype(jnp.float32)
    factor, inverse = forward_eliminate(gram_of(value), [image, unit])
    packed_ref[:, rows:rows + columns] = lax.dot_general(
        inverse, factor, (((0,), (0,)), ((), ())), precision=HIGHEST,
        preferred_element_type=jnp.float32,
    )
    packed_ref[:, rows + columns:] = factor


def update_left(matrix_ref, packed_ref, new_ref):
    rows, columns = matrix_ref.shape
    weights = GOSSIP_RATE * packed_ref[:, rows:rows + columns]
    new_ref[...] = matrix_ref[...] + outer_product(packed_ref[:, :rows], weights)


def update_right(matrix_ref, packed_ref, new_hbm, warm_hbm, new_vmem, warm_vmem, sems):
    rows, columns = matrix_ref.shape
    tile = rows // TILES
    warm_vmem[...] = packed_ref[:, rows + columns:]
    copies = [pltpu.make_async_copy(warm_vmem, warm_hbm.at[0], sems.at[TILES])]
    copies[0].start()
    weights = -GOSSIP_RATE * packed_ref[:, rows:rows + columns]
    for index in range(TILES):
        piece = pl.ds(index * tile, tile)
        new_vmem[piece] = matrix_ref[piece] + outer_product(packed_ref[:, piece], weights)
        copy = pltpu.make_async_copy(new_vmem.at[piece], new_hbm.at[0, piece], sems.at[index])
        copy.start()
        copies.append(copy)
    for copy in copies:
        copy.wait()


def sum_over_tp(spread):
    peers = lax.axis_size("tp")
    groups = [list(range(start, peers, 2)) for start in range(2)]
    spread = lax.all_to_all(spread, "tp", 0, 0, axis_index_groups=groups)
    _, rank, rows = spread.shape
    total = kernel_call(
        add_up, jax.ShapeDtypeStruct((rank, rows), jnp.float32), spread.size, 4 * spread.size
    )(spread)
    other = lax.ppermute(total, "tp", [(i, i ^ 1) for i in range(peers)])
    return total, other


def per_device(params, warm):
    _, rows, columns = params.shape
    rank = warm.shape[1]
    peers = lax.axis_size("tp")
    count = lax.axis_size("blk")
    one = rank * rows * columns * 2
    block = rows * columns * 4
    f32 = jnp.float32
    to_right = [(i, (i + 1) % count) for i in range(count)]
    to_left = [(i, (i - 1) % count) for i in range(count)]
    spread = jax.ShapeDtypeStruct((peers // 2, rank, rows), f32)
    split = jax.ShapeDtypeStruct((3, rows, columns), jnp.bfloat16)
    matrix = jax.ShapeDtypeStruct((rows, columns), f32)
    hbm = pl.BlockSpec(memory_space=pltpu.HBM)
    factor_scratch = pltpu.VMEM((rank, columns), f32)
    sems = pltpu.SemaphoreType.DMA((TILES + 1,))

    packed, parts, mine = kernel_call(
        own_product, (jax.ShapeDtypeStruct((rank, rows + columns), f32), split, matrix),
        6 * one, 2 * block, in_specs=[hbm, hbm], scratch_shapes=[factor_scratch, sems],
    )(warm, params)
    packed = lax.ppermute(packed, "blk", to_right)
    left_params = lax.ppermute(params, "blk", to_right)
    sums = kernel_call(spread_first, spread, 4000 * one, block)(packed, parts)
    total, other = sum_over_tp(sums)
    delta, sums = kernel_call(middle_step, (split, spread), 12 * one, 4 * block)(
        total, other, mine, left_params
    )
    total, other = sum_over_tp(sums)
    own = kernel_call(
        last_step, jax.ShapeDtypeStruct((rank, rows + 2 * columns), f32), 6 * one, 2 * block
    )(total, other, delta)
    right = lax.ppermute(own, "blk", to_left)
    left_done = kernel_call(update_left, matrix, 6 * one, 2 * block)(mine, own)
    new_params, next_warm = kernel_call(
        update_right,
        (jax.ShapeDtypeStruct(params.shape, f32), jax.ShapeDtypeStruct(warm.shape, f32)),
        6 * one, 2 * block, out_specs=(hbm, hbm),
        scratch_shapes=[pltpu.VMEM(matrix.shape, f32), factor_scratch, sems],
    )(left_done, right)
    return new_params, next_warm


def solution(mesh):
    spec = P("blk", None, "tp")
    return jax.shard_map(
        per_device, mesh=mesh, in_specs=(spec, spec), out_specs=(spec, spec), check_vma=False
    )
```

```python
import jax
import jax.numpy as jnp
from jax import lax
from jax.experimental import pallas as pl
from jax.experimental.pallas import tpu as pltpu
from jax.sharding import PartitionSpec as P

GOSSIP_RATE = 0.5
TILES = 8
EARLY = 2
HIGHEST = lax.Precision.HIGHEST


def kernel_call(body, out_shape, flops, moved, **blocks):
    return pl.pallas_call(
        body,
        out_shape=out_shape,
        **blocks,
        compiler_params=pltpu.CompilerParams(vmem_limit_bytes=24 << 20),
        cost_estimate=pl.CostEstimate(flops=flops, bytes_accessed=moved, transcendentals=0),
    )


def three_parts(value):
    high = value.astype(jnp.bfloat16)
    rest = value - high.astype(jnp.float32)
    middle = rest.astype(jnp.bfloat16)
    low = (rest - middle.astype(jnp.float32)).astype(jnp.bfloat16)
    return high, middle, low


def stack(parts):
    return jnp.concatenate([p.astype(jnp.float32) for p in parts], axis=0).astype(jnp.bfloat16)


def bf16_dot(a, b, a_dim, b_dim):
    return lax.dot_general(
        a, b, (((a_dim,), (b_dim,)), ((), ())), preferred_element_type=jnp.float32
    )


def split_product(rows, parts, contract):
    rank = rows.shape[0]
    stacked = stack(three_parts(rows))
    total = None
    for taken, part in reversed(list(zip((3, 2, 1), parts))):
        products = bf16_dot(stacked[:taken * rank], part, 1, contract)
        for index in reversed(range(taken)):
            term = products[index * rank:(index + 1) * rank]
            total = term if total is None else total + term
    return total


def gram_of(rows):
    rank = rows.shape[0]
    stacked = stack(three_parts(rows))
    products = bf16_dot(stacked, stacked, 1, 1)
    total = None
    for i, j in ((1, 1), (0, 2), (2, 0), (0, 1), (1, 0), (0, 0)):
        term = products[i * rank:(i + 1) * rank, j * rank:(j + 1) * rank]
        total = term if total is None else total + term
    return total


def outer_product(values, weights):
    left, right = three_parts(values), three_parts(weights)
    pairs = ((1, 1), (0, 2), (2, 0), (0, 1), (1, 0), (0, 0))
    return bf16_dot(stack([left[i] for i, _ in pairs]), stack([right[j] for _, j in pairs]), 0, 0)


def forward_eliminate(gram, columns):
    rank = gram.shape[0]
    row_index = lax.broadcasted_iota(jnp.int32, (rank, 1), 0)
    pivots = jnp.ones((rank, 1), jnp.float32)
    columns = list(columns)
    for k in range(rank):
        pivot = gram[k:k + 1, k:k + 1]
        pivots = jnp.where(row_index == k, pivot, pivots)
        if k + 1 < rank:
            ratio = jnp.where(row_index > k, gram[:, k:k + 1] / pivot, 0.0)
            columns = [c - ratio * c[k:k + 1, :] for c in columns]
            gram = gram - ratio * gram[k:k + 1, :]
    scale = 1.0 / jnp.sqrt(pivots)
    return [c * scale for c in columns]


def own_product(q_ref, matrix_ref, packed_ref, parts_ref, rest_ref):
    rows = parts_ref.shape[1]
    early = rows - rest_ref.shape[0]
    parts = three_parts(matrix_ref[0])
    for index, part in enumerate(parts):
        parts_ref[index] = part
    packed_ref[:, :rows] = split_product(q_ref[0], parts, 1)
    packed_ref[:, rows:] = q_ref[0]
    rest_ref[...] = matrix_ref[0, early:]


def spread_first(packed_ref, parts_ref, mine_ref, left_ref, out_ref, delta_ref):
    rows = parts_ref.shape[1]
    for index, part in enumerate(three_parts(left_ref[...] - mine_ref[...])):
        delta_ref[index] = part
    mine = split_product(packed_ref[:, rows:], [parts_ref[i] for i in range(3)], 1)
    part = packed_ref[:, :rows] - mine
    for peer in range(out_ref.shape[0]):
        out_ref[peer] = part


def total_of(sums_ref):
    value = sums_ref[0]
    for peer in range(1, sums_ref.shape[0]):
        value = value + sums_ref[peer]
    return value


def add_up(sums_ref, out_ref):
    out_ref[...] = total_of(sums_ref)


def middle_step(sum_ref, other_ref, mine_ref, left_ref, first_ref, rest_ref, out_ref):
    value = sum_ref[...] + other_ref[...]
    rest = three_parts(left_ref[...] - mine_ref[...])
    for index, part in enumerate(rest):
        rest_ref[index] = part
    delta = [jnp.concatenate([first_ref[index], part], axis=0) for index, part in enumerate(rest)]
    image = split_product(value, delta, 0)
    (factor,) = forward_eliminate(gram_of(value), [image])
    part = split_product(factor, delta, 1)
    for peer in range(out_ref.shape[0]):
        out_ref[peer] = part


def last_step(sums_ref, first_ref, rest_ref, packed_ref):
    _, rank, rows = sums_ref.shape
    columns = rest_ref.shape[2]
    value = total_of(sums_ref)
    packed_ref[:, :rows] = value
    image = split_product(
        value, [jnp.concatenate([first_ref[i], rest_ref[i]], axis=0) for i in range(3)], 0
    )
    unit = (
        lax.broadcasted_iota(jnp.int32, (rank, rank), 0)
        == lax.broadcasted_iota(jnp.int32, (rank, rank), 1)
    ).astype(jnp.float32)
    factor, inverse = forward_eliminate(gram_of(value), [image, unit])
    packed_ref[:, rows:rows + columns] = lax.dot_general(
        inverse, factor, (((0,), (0,)), ((), ())), precision=HIGHEST,
        preferred_element_type=jnp.float32,
    )
    packed_ref[:, rows + columns:] = factor


def update_left(first_ref, rest_ref, packed_ref, new_ref):
    rows, columns = new_ref.shape
    weights = GOSSIP_RATE * packed_ref[:, rows:rows + columns]
    start = 0
    for matrix_ref in (first_ref, rest_ref):
        piece = pl.ds(start, matrix_ref.shape[0])
        new_ref[piece] = matrix_ref[...] + outer_product(packed_ref[:, piece], weights)
        start += matrix_ref.shape[0]


def update_right(matrix_ref, packed_ref, new_hbm, warm_hbm, new_vmem, warm_vmem, sems):
    rows, columns = matrix_ref.shape
    tile = rows // TILES
    warm_vmem[...] = packed_ref[:, rows + columns:]
    copies = [pltpu.make_async_copy(warm_vmem, warm_hbm.at[0], sems.at[TILES])]
    copies[0].start()
    weights = -GOSSIP_RATE * packed_ref[:, rows:rows + columns]
    for index in range(TILES):
        piece = pl.ds(index * tile, tile)
        new_vmem[piece] = matrix_ref[piece] + outer_product(packed_ref[:, piece], weights)
        copy = pltpu.make_async_copy(new_vmem.at[piece], new_hbm.at[0, piece], sems.at[index])
        copy.start()
        copies.append(copy)
    for copy in copies:
        copy.wait()


def sum_over_tp(spread):
    peers = lax.axis_size("tp")
    groups = [list(range(start, peers, 2)) for start in range(2)]
    spread = lax.all_to_all(spread, "tp", 0, 0, axis_index_groups=groups)
    _, rank, rows = spread.shape
    total = kernel_call(
        add_up, jax.ShapeDtypeStruct((rank, rows), jnp.float32), spread.size, 4 * spread.size
    )(spread)
    other = lax.ppermute(total, "tp", [(i, i ^ 1) for i in range(peers)])
    return total, other


def per_device(params, warm):
    _, rows, columns = params.shape
    rank = warm.shape[1]
    peers = lax.axis_size("tp")
    count = lax.axis_size("blk")
    one = rank * rows * columns * 2
    block = rows * columns * 4
    f32 = jnp.float32
    to_right = [(i, (i + 1) % count) for i in range(count)]
    to_left = [(i, (i - 1) % count) for i in range(count)]
    early = rows // TILES * EARLY

    def spread(peers):
        return jax.ShapeDtypeStruct((peers, rank, rows), f32)

    def split(rows):
        return jax.ShapeDtypeStruct((3, rows, columns), jnp.bfloat16)

    matrix = jax.ShapeDtypeStruct((rows, columns), f32)
    hbm = pl.BlockSpec(memory_space=pltpu.HBM)
    factor_scratch = pltpu.VMEM((rank, columns), f32)
    sems = pltpu.SemaphoreType.DMA((TILES + 1,))

    first = params[0, :early]
    left_first = lax.ppermute(first, "blk", to_right)
    packed, parts, rest = kernel_call(
        own_product,
        (
            jax.ShapeDtypeStruct((rank, rows + columns), f32), split(rows),
            jax.ShapeDtypeStruct((rows - early, columns), f32),
        ),
        6 * one, 2 * block,
    )(warm, params)
    packed = lax.ppermute(packed, "blk", to_right)
    left_rest = lax.ppermute(rest, "blk", to_right)
    sums, delta_first = kernel_call(spread_first, (spread(peers // 2), split(early)), 4000 * one, block)(
        packed, parts, first, left_first
    )
    total, other = sum_over_tp(sums)
    delta_rest, sums = kernel_call(middle_step, (split(rows - early), spread(peers)), 12 * one, 4 * block)(
        total, other, rest, left_rest, delta_first
    )
    sums = lax.all_to_all(sums, "tp", 0, 0)
    own = kernel_call(
        last_step, jax.ShapeDtypeStruct((rank, rows + 2 * columns), f32), 6 * one, 2 * block
    )(sums, delta_first, delta_rest)
    right = lax.ppermute(own, "blk", to_left)
    left_done = kernel_call(update_left, matrix, 6 * one, 2 * block)(first, rest, own)
    new_params, next_warm = kernel_call(
        update_right,
        (jax.ShapeDtypeStruct(params.shape, f32), jax.ShapeDtypeStruct(warm.shape, f32)),
        6 * one, 2 * block, out_specs=(hbm, hbm),
        scratch_shapes=[pltpu.VMEM(matrix.shape, f32), factor_scratch, sems],
    )(left_done, right)
    return new_params, next_warm


def solution(mesh):
    spec = P("blk", None, "tp")
    return jax.shard_map(
        per_device, mesh=mesh, in_specs=(spec, spec), out_specs=(spec, spec), check_vma=False
    )
```

```python
import jax
import jax.numpy as jnp
from jax import lax
from jax.experimental import pallas as pl
from jax.experimental.pallas import tpu as pltpu
from jax.sharding import PartitionSpec as P

GOSSIP_RATE = 0.5
TILES = 8
LATE = 2
RUNS = 2
HIGHEST = lax.Precision.HIGHEST


def kernel_call(body, out_shape, flops, moved, **blocks):
    return pl.pallas_call(
        body,
        out_shape=out_shape,
        **blocks,
        compiler_params=pltpu.CompilerParams(vmem_limit_bytes=24 << 20),
        cost_estimate=pl.CostEstimate(flops=flops, bytes_accessed=moved, transcendentals=0),
    )


def three_parts(value):
    high = value.astype(jnp.bfloat16)
    rest = value - high.astype(jnp.float32)
    middle = rest.astype(jnp.bfloat16)
    low = (rest - middle.astype(jnp.float32)).astype(jnp.bfloat16)
    return high, middle, low


def stack(parts):
    return jnp.concatenate([p.astype(jnp.float32) for p in parts], axis=0).astype(jnp.bfloat16)


def bf16_dot(a, b, a_dim, b_dim):
    return lax.dot_general(
        a, b, (((a_dim,), (b_dim,)), ((), ())), preferred_element_type=jnp.float32
    )


def split_product(rows, parts, contract):
    rank = rows.shape[0]
    stacked = stack(three_parts(rows))
    total = None
    for taken, part in reversed(list(zip((3, 2, 1), parts))):
        products = bf16_dot(stacked[:taken * rank], part, 1, contract)
        for index in reversed(range(taken)):
            term = products[index * rank:(index + 1) * rank]
            total = term if total is None else total + term
    return total


def gram_of(rows):
    rank = rows.shape[0]
    stacked = stack(three_parts(rows))
    products = bf16_dot(stacked, stacked, 1, 1)
    total = None
    for i, j in ((1, 1), (0, 2), (2, 0), (0, 1), (1, 0), (0, 0)):
        term = products[i * rank:(i + 1) * rank, j * rank:(j + 1) * rank]
        total = term if total is None else total + term
    return total


def outer_product(values, weights):
    left, right = three_parts(values), three_parts(weights)
    pairs = ((1, 1), (0, 2), (2, 0), (0, 1), (1, 0), (0, 0))
    return bf16_dot(stack([left[i] for i, _ in pairs]), stack([right[j] for _, j in pairs]), 0, 0)


def forward_eliminate(gram, columns):
    rank = gram.shape[0]
    row_index = lax.broadcasted_iota(jnp.int32, (rank, 1), 0)
    pivots = jnp.ones((rank, 1), jnp.float32)
    columns = list(columns)
    for k in range(rank):
        pivot = gram[k:k + 1, k:k + 1]
        pivots = jnp.where(row_index == k, pivot, pivots)
        if k + 1 < rank:
            ratio = jnp.where(row_index > k, gram[:, k:k + 1] / pivot, 0.0)
            columns = [c - ratio * c[k:k + 1, :] for c in columns]
            gram = gram - ratio * gram[k:k + 1, :]
    scale = 1.0 / jnp.sqrt(pivots)
    return [c * scale for c in columns]


def own_product(q_ref, matrix_ref, packed_ref, parts_ref, main_ref, late_ref):
    rows = parts_ref.shape[1]
    split = main_ref.shape[0]
    parts = three_parts(matrix_ref[0])
    for index, part in enumerate(parts):
        parts_ref[index] = part
    packed_ref[:, :rows] = split_product(q_ref[0], parts, 1)
    packed_ref[:, rows:] = q_ref[0]
    main_ref[...] = matrix_ref[0, :split]
    late_ref[...] = matrix_ref[0, split:]


def spread_first(packed_ref, parts_ref, out_ref):
    rows = parts_ref.shape[1]
    mine = split_product(packed_ref[:, rows:], [parts_ref[i] for i in range(3)], 1)
    part = packed_ref[:, :rows] - mine
    for peer in range(out_ref.shape[0]):
        out_ref[peer] = part


def total_of(sums_ref):
    value = sums_ref[0]
    for peer in range(1, sums_ref.shape[0]):
        value = value + sums_ref[peer]
    return value


def add_up(sums_ref, out_ref):
    out_ref[...] = total_of(sums_ref)


def middle_main(sum_ref, other_ref, mine_ref, left_ref, value_ref, gram_ref, image_ref, main_ref):
    split = mine_ref.shape[0]
    value = sum_ref[...] + other_ref[...]
    value_ref[...] = value
    delta = three_parts(left_ref[...] - mine_ref[...])
    for index, part in enumerate(delta):
        main_ref[index] = part
    image_ref[...] = split_product(value[:, :split], delta, 0)
    gram_ref[...] = gram_of(value)


def middle_late(value_ref, gram_ref, image_ref, main_ref, mine_ref, left_ref, late_ref, out_ref):
    split = main_ref.shape[1]
    late = three_parts(left_ref[...] - mine_ref[...])
    for index, part in enumerate(late):
        late_ref[index] = part
    image = image_ref[...] + split_product(value_ref[:, split:], late, 0)
    (factor,) = forward_eliminate(gram_ref[...], [image])
    main = split_product(factor, [main_ref[i] for i in range(3)], 1)
    last = split_product(factor, late, 1)
    for peer in range(out_ref.shape[0]):
        out_ref[peer, :, :split] = main
        out_ref[peer, :, split:] = last


def last_step(sums_ref, main_ref, late_ref, packed_ref):
    _, rank, rows = sums_ref.shape
    columns = main_ref.shape[2]
    value = total_of(sums_ref)
    packed_ref[:, :rows] = value
    image = split_product(
        value, [jnp.concatenate([main_ref[i], late_ref[i]], axis=0) for i in range(3)], 0
    )
    unit = (
        lax.broadcasted_iota(jnp.int32, (rank, rank), 0)
        == lax.broadcasted_iota(jnp.int32, (rank, rank), 1)
    ).astype(jnp.float32)
    factor, inverse = forward_eliminate(gram_of(value), [image, unit])
    packed_ref[:, rows:rows + columns] = lax.dot_general(
        inverse, factor, (((0,), (0,)), ((), ())), precision=HIGHEST,
        preferred_element_type=jnp.float32,
    )
    packed_ref[:, rows + columns:] = factor


def update_left(main_ref, late_ref, packed_ref, new_ref):
    rows, columns = new_ref.shape
    weights = GOSSIP_RATE * packed_ref[:, rows:rows + columns]
    start = 0
    for matrix_ref in (main_ref, late_ref):
        piece = pl.ds(start, matrix_ref.shape[0])
        new_ref[piece] = matrix_ref[...] + outer_product(packed_ref[:, piece], weights)
        start += matrix_ref.shape[0]


def update_right(matrix_ref, packed_ref, new_hbm, warm_hbm, new_vmem, warm_vmem, sems):
    rows, columns = matrix_ref.shape
    tile = rows // TILES
    warm_vmem[...] = packed_ref[:, rows + columns:]
    copies = [pltpu.make_async_copy(warm_vmem, warm_hbm.at[0], sems.at[TILES])]
    copies[0].start()
    weights = -GOSSIP_RATE * packed_ref[:, rows:rows + columns]
    for index in range(TILES):
        piece = pl.ds(index * tile, tile)
        new_vmem[piece] = matrix_ref[piece] + outer_product(packed_ref[:, piece], weights)
        copy = pltpu.make_async_copy(new_vmem.at[piece], new_hbm.at[0, piece], sems.at[index])
        copy.start()
        copies.append(copy)
    for copy in copies:
        copy.wait()


def sum_over_y(spread):
    peers = lax.axis_size("tp")
    groups = [list(range(start, peers, 2)) for start in range(2)]
    spread = lax.all_to_all(spread, "tp", 0, 0, axis_index_groups=groups)
    _, rank, rows = spread.shape
    return kernel_call(
        add_up, jax.ShapeDtypeStruct((rank, rows), jnp.float32), spread.size, 4 * spread.size
    )(spread)


def per_device(params, warm):
    _, rows, columns = params.shape
    rank = warm.shape[1]
    peers = lax.axis_size("tp")
    count = lax.axis_size("blk")
    one = rank * rows * columns * 2
    block = rows * columns * 4
    f32 = jnp.float32
    to_right = [(i, (i + 1) % count) for i in range(count)]
    to_left = [(i, (i - 1) % count) for i in range(count)]
    split_at = rows - rows // TILES * LATE
    run = count // RUNS
    ends = [run * (i + 1) - 1 for i in range(RUNS)]
    swap_ends = [(i, i) for i in range(count) if i not in ends]
    swap_ends += [(end, ends[index - 1]) for index, end in enumerate(ends)]
    in_run = [(i, i // run * run + (i + 1) % run) for i in range(count)]

    def spread(peers):
        return jax.ShapeDtypeStruct((peers, rank, rows), f32)

    def split(rows):
        return jax.ShapeDtypeStruct((3, rows, columns), jnp.bfloat16)

    matrix = jax.ShapeDtypeStruct((rows, columns), f32)
    hbm = pl.BlockSpec(memory_space=pltpu.HBM)
    factor_scratch = pltpu.VMEM((rank, columns), f32)
    sems = pltpu.SemaphoreType.DMA((TILES + 1,))

    packed, parts, main, late = kernel_call(
        own_product,
        (
            jax.ShapeDtypeStruct((rank, rows + columns), f32), split(rows),
            jax.ShapeDtypeStruct((split_at, columns), f32),
            jax.ShapeDtypeStruct((rows - split_at, columns), f32),
        ),
        6 * one, 2 * block,
    )(warm, params)
    packed = lax.ppermute(packed, "blk", to_right)
    left_main = lax.ppermute(main, "blk", to_right)
    carried = lax.ppermute(late, "blk", swap_ends)
    sums = kernel_call(spread_first, spread(peers // 2), 4000 * one, block)(packed, parts)
    sums = sum_over_y(sums)
    carried, sums = lax.optimization_barrier((carried, sums))
    left_late = lax.ppermute(carried, "blk", in_run)
    other = lax.ppermute(sums, "tp", [(i, i ^ 1) for i in range(peers)])
    value, gram, image, delta_main = kernel_call(
        middle_main,
        (
            jax.ShapeDtypeStruct((rank, rows), f32), jax.ShapeDtypeStruct((rank, rank), f32),
            jax.ShapeDtypeStruct((rank, columns), f32), split(split_at),
        ),
        4000 * one, 2 * block,
    )(sums, other, main, left_main)
    delta_late, sums = kernel_call(middle_late, (split(rows - split_at), spread(peers)), 6 * one, block)(
        value, gram, image, delta_main, late, left_late
    )
    sums = lax.all_to_all(sums, "tp", 0, 0)
    own = kernel_call(
        last_step, jax.ShapeDtypeStruct((rank, rows + 2 * columns), f32), 6 * one, 2 * block
    )(sums, delta_main, delta_late)
    right = lax.ppermute(own, "blk", to_left)
    left_done = kernel_call(update_left, matrix, 6 * one, 2 * block)(main, late, own)
    new_params, next_warm = kernel_call(
        update_right,
        (jax.ShapeDtypeStruct(params.shape, f32), jax.ShapeDtypeStruct(warm.shape, f32)),
        6 * one, 2 * block, out_specs=(hbm, hbm),
        scratch_shapes=[pltpu.VMEM(matrix.shape, f32), factor_scratch, sems],
    )(left_done, right)
    return new_params, next_warm


def solution(mesh):
    spec = P("blk", None, "tp")
    return jax.shard_map(
        per_device, mesh=mesh, in_specs=(spec, spec), out_specs=(spec, spec), check_vma=False
    )
```

```python
import jax
import jax.numpy as jnp
from jax import lax
from jax.experimental import pallas as pl
from jax.experimental.pallas import tpu as pltpu
from jax.sharding import PartitionSpec as P

GOSSIP_RATE = 0.5
TILES = 8
LATE = 2
RUNS = 2


def kernel_call(body, out_shape, flops, moved, **blocks):
    return pl.pallas_call(
        body,
        out_shape=out_shape,
        **blocks,
        compiler_params=pltpu.CompilerParams(vmem_limit_bytes=24 << 20),
        cost_estimate=pl.CostEstimate(flops=flops, bytes_accessed=moved, transcendentals=0),
    )


def three_parts(value):
    high = value.astype(jnp.bfloat16)
    rest = value - high.astype(jnp.float32)
    middle = rest.astype(jnp.bfloat16)
    low = (rest - middle.astype(jnp.float32)).astype(jnp.bfloat16)
    return high, middle, low


def stack(parts):
    return jnp.concatenate([p.astype(jnp.float32) for p in parts], axis=0).astype(jnp.bfloat16)


def bf16_dot(a, b, a_dim, b_dim):
    return lax.dot_general(
        a, b, (((a_dim,), (b_dim,)), ((), ())), preferred_element_type=jnp.float32
    )


def split_product(rows, parts, contract):
    rank = rows.shape[0]
    stacked = stack(three_parts(rows))
    total = None
    for taken, part in reversed(list(zip((3, 2, 1), parts))):
        products = bf16_dot(stacked[:taken * rank], part, 1, contract)
        for index in reversed(range(taken)):
            term = products[index * rank:(index + 1) * rank]
            total = term if total is None else total + term
    return total


def gram_of(rows):
    rank = rows.shape[0]
    stacked = stack(three_parts(rows))
    products = bf16_dot(stacked, stacked, 1, 1)
    total = None
    for i, j in ((1, 1), (0, 2), (2, 0), (0, 1), (1, 0), (0, 0)):
        term = products[i * rank:(i + 1) * rank, j * rank:(j + 1) * rank]
        total = term if total is None else total + term
    return total


def outer_product(values, weights):
    left, right = three_parts(values), three_parts(weights)
    pairs = ((1, 1), (0, 2), (2, 0), (0, 1), (1, 0), (0, 0))
    return bf16_dot(stack([left[i] for i, _ in pairs]), stack([right[j] for _, j in pairs]), 0, 0)


def eliminate(gram, image):
    rank = gram.shape[0]
    row_index = lax.broadcasted_iota(jnp.int32, image.shape, 0)
    columns = [jnp.broadcast_to(gram[:, k:k + 1], image.shape) for k in range(rank)]
    pivots = jnp.ones_like(image)
    ratios = []
    for k in range(rank):
        pivot = columns[k][k:k + 1, :]
        pivots = jnp.where(row_index == k, pivot, pivots)
        if k + 1 < rank:
            ratio = jnp.where(row_index > k, columns[k] * (1.0 / pivot), 0.0)
            ratios.append(ratio)
            for j in range(k + 1, rank):
                columns[j] = columns[j] - ratio * columns[j][k:k + 1, :]
            image = image - ratio * image[k:k + 1, :]
    return image, pivots, ratios


def back_substitute(ratios, value):
    row_index = lax.broadcasted_iota(jnp.int32, value.shape, 0)
    for k in reversed(range(len(ratios))):
        below = jnp.sum(ratios[k] * value, axis=0, keepdims=True)
        value = jnp.where(row_index == k, value - below, value)
    return value


def own_product(q_hbm, matrix_hbm, packed_ref, parts_ref, main_ref, late_ref, q_vmem, sems):
    rows = parts_ref.shape[1]
    tile = rows // TILES
    places = [
        ref.at[pl.ds(start, tile)]
        for ref in (main_ref, late_ref) for start in range(0, ref.shape[0], tile)
    ]
    copies = [pltpu.make_async_copy(q_hbm.at[0], q_vmem, sems.at[TILES])]
    for index, place in enumerate(places):
        piece = pl.ds(index * tile, tile)
        copies.append(pltpu.make_async_copy(matrix_hbm.at[0, piece], place, sems.at[index]))
    for copy in copies:
        copy.start()
    copies[0].wait()
    q = q_vmem[...]
    packed_ref[:, rows:] = q
    for index, place in enumerate(places):
        copies[index + 1].wait()
        piece = pl.ds(index * tile, tile)
        parts = three_parts(place[...])
        for number, part in enumerate(parts):
            parts_ref[number, piece] = part
        packed_ref[:, piece] = split_product(q, parts, 1)


def spread_first(packed_ref, parts_ref, out_ref):
    rows = parts_ref.shape[1]
    mine = split_product(packed_ref[:, rows:], [parts_ref[i] for i in range(3)], 1)
    part = packed_ref[:, :rows] - mine
    for peer in range(out_ref.shape[0]):
        out_ref[peer] = part


def total_of(sums_ref):
    value = sums_ref[0]
    for peer in range(1, sums_ref.shape[0]):
        value = value + sums_ref[peer]
    return value


def add_up(sums_ref, out_ref):
    out_ref[...] = total_of(sums_ref)


def middle_main(sum_ref, other_ref, mine_ref, left_ref, value_ref, gram_ref, image_ref, main_ref):
    split = mine_ref.shape[0]
    value = sum_ref[...] + other_ref[...]
    value_ref[...] = value
    delta = three_parts(left_ref[...] - mine_ref[...])
    for index, part in enumerate(delta):
        main_ref[index] = part
    image_ref[...] = split_product(value[:, :split], delta, 0)
    gram_ref[...] = gram_of(value)


def middle_late(value_ref, gram_ref, image_ref, main_ref, mine_ref, left_ref, late_ref, out_ref):
    split = main_ref.shape[1]
    late = three_parts(left_ref[...] - mine_ref[...])
    for index, part in enumerate(late):
        late_ref[index] = part
    image = image_ref[...] + split_product(value_ref[:, split:], late, 0)
    image, pivots, _ = eliminate(gram_ref[...], image)
    factor = image * (1.0 / jnp.sqrt(pivots))
    main = split_product(factor, [main_ref[i] for i in range(3)], 1)
    last = split_product(factor, late, 1)
    for peer in range(out_ref.shape[0]):
        out_ref[peer, :, :split] = main
        out_ref[peer, :, split:] = last


def last_step(sums_ref, main_ref, late_ref, packed_ref):
    _, rank, rows = sums_ref.shape
    columns = main_ref.shape[2]
    value = total_of(sums_ref)
    packed_ref[:, :rows] = value
    image = split_product(
        value, [jnp.concatenate([main_ref[i], late_ref[i]], axis=0) for i in range(3)], 0
    )
    image, pivots, ratios = eliminate(gram_of(value), image)
    packed_ref[:, rows:rows + columns] = back_substitute(ratios, image * (1.0 / pivots))
    packed_ref[:, rows + columns:] = image * (1.0 / jnp.sqrt(pivots))


def update_left(main_ref, late_ref, packed_ref, new_ref):
    rows, columns = new_ref.shape
    weights = GOSSIP_RATE * packed_ref[:, rows:rows + columns]
    start = 0
    for matrix_ref in (main_ref, late_ref):
        piece = pl.ds(start, matrix_ref.shape[0])
        new_ref[piece] = matrix_ref[...] + outer_product(packed_ref[:, piece], weights)
        start += matrix_ref.shape[0]


def update_right(matrix_ref, packed_ref, new_hbm, warm_hbm, new_vmem, warm_vmem, sems):
    rows, columns = matrix_ref.shape
    tile = rows // TILES
    warm_vmem[...] = packed_ref[:, rows + columns:]
    copies = [pltpu.make_async_copy(warm_vmem, warm_hbm.at[0], sems.at[TILES])]
    copies[0].start()
    weights = -GOSSIP_RATE * packed_ref[:, rows:rows + columns]
    for index in range(TILES):
        piece = pl.ds(index * tile, tile)
        new_vmem[piece] = matrix_ref[piece] + outer_product(packed_ref[:, piece], weights)
        copy = pltpu.make_async_copy(new_vmem.at[piece], new_hbm.at[0, piece], sems.at[index])
        copy.start()
        copies.append(copy)
    for copy in copies:
        copy.wait()


def sum_over_y(spread):
    peers = lax.axis_size("tp")
    groups = [list(range(start, peers, 2)) for start in range(2)]
    spread = lax.all_to_all(spread, "tp", 0, 0, axis_index_groups=groups)
    _, rank, rows = spread.shape
    return kernel_call(
        add_up, jax.ShapeDtypeStruct((rank, rows), jnp.float32), spread.size, 4 * spread.size
    )(spread)


def per_device(params, warm):
    _, rows, columns = params.shape
    rank = warm.shape[1]
    peers = lax.axis_size("tp")
    count = lax.axis_size("blk")
    one = rank * rows * columns * 2
    block = rows * columns * 4
    f32 = jnp.float32
    to_right = [(i, (i + 1) % count) for i in range(count)]
    to_left = [(i, (i - 1) % count) for i in range(count)]
    split_at = rows - rows // TILES * LATE
    run = count // RUNS
    ends = [run * (i + 1) - 1 for i in range(RUNS)]
    swap_ends = [(i, i) for i in range(count) if i not in ends]
    swap_ends += [(end, ends[index - 1]) for index, end in enumerate(ends)]
    in_run = [(i, i // run * run + (i + 1) % run) for i in range(count)]

    def spread(peers):
        return jax.ShapeDtypeStruct((peers, rank, rows), f32)

    def split(rows):
        return jax.ShapeDtypeStruct((3, rows, columns), jnp.bfloat16)

    matrix = jax.ShapeDtypeStruct((rows, columns), f32)
    hbm = pl.BlockSpec(memory_space=pltpu.HBM)
    factor_scratch = pltpu.VMEM((rank, columns), f32)
    sems = pltpu.SemaphoreType.DMA((TILES + 1,))

    packed, parts, main, late = kernel_call(
        own_product,
        (
            jax.ShapeDtypeStruct((rank, rows + columns), f32), split(rows),
            jax.ShapeDtypeStruct((split_at, columns), f32),
            jax.ShapeDtypeStruct((rows - split_at, columns), f32),
        ),
        6 * one, 2 * block, in_specs=[hbm, hbm], scratch_shapes=[factor_scratch, sems],
    )(pltpu.with_memory_space_constraint(warm, pltpu.HBM), pltpu.with_memory_space_constraint(params, pltpu.HBM))
    packed = lax.ppermute(packed, "blk", to_right)
    left_main = lax.ppermute(main, "blk", to_right)
    carried = lax.ppermute(late, "blk", swap_ends)
    sums = kernel_call(spread_first, spread(peers // 2), 4000 * one, block)(packed, parts)
    sums = sum_over_y(sums)
    carried, sums = lax.optimization_barrier((carried, sums))
    left_late = lax.ppermute(carried, "blk", in_run)
    other = lax.ppermute(sums, "tp", [(i, i ^ 1) for i in range(peers)])
    value, gram, image, delta_main = kernel_call(
        middle_main,
        (
            jax.ShapeDtypeStruct((rank, rows), f32), jax.ShapeDtypeStruct((rank, rank), f32),
            jax.ShapeDtypeStruct((rank, columns), f32), split(split_at),
        ),
        4000 * one, 2 * block,
    )(sums, other, main, left_main)
    delta_late, sums = kernel_call(middle_late, (split(rows - split_at), spread(peers)), 6 * one, block)(
        value, gram, image, delta_main, late, left_late
    )
    sums = lax.all_to_all(sums, "tp", 0, 0)
    own = kernel_call(
        last_step, jax.ShapeDtypeStruct((rank, rows + 2 * columns), f32), 6 * one, 2 * block
    )(sums, delta_main, delta_late)
    right = lax.ppermute(own, "blk", to_left)
    left_done = kernel_call(update_left, matrix, 6 * one, 2 * block)(main, late, own)
    new_params, next_warm = kernel_call(
        update_right,
        (jax.ShapeDtypeStruct(params.shape, f32), jax.ShapeDtypeStruct(warm.shape, f32)),
        6 * one, 2 * block, out_specs=(hbm, hbm),
        scratch_shapes=[pltpu.VMEM(matrix.shape, f32), factor_scratch, sems],
    )(left_done, right)
    return new_params, next_warm


def solution(mesh):
    spec = P("blk", None, "tp")
    return jax.shard_map(
        per_device, mesh=mesh, in_specs=(spec, spec), out_specs=(spec, spec), check_vma=False
    )
```

```python
import jax
import jax.numpy as jnp
from jax import lax
from jax.experimental import pallas as pl
from jax.experimental.pallas import tpu as pltpu
from jax.sharding import PartitionSpec as P

GOSSIP_RATE = 0.5
TILES = 4
LATE = 1
RUNS = 2


def kernel_call(body, out_shape, flops, moved, **blocks):
    return pl.pallas_call(
        body,
        out_shape=out_shape,
        **blocks,
        compiler_params=pltpu.CompilerParams(vmem_limit_bytes=24 << 20),
        cost_estimate=pl.CostEstimate(flops=flops, bytes_accessed=moved, transcendentals=0),
    )


def three_parts(value):
    high = value.astype(jnp.bfloat16)
    rest = value - high.astype(jnp.float32)
    middle = rest.astype(jnp.bfloat16)
    low = (rest - middle.astype(jnp.float32)).astype(jnp.bfloat16)
    return high, middle, low


def stack(parts):
    return jnp.concatenate([p.astype(jnp.float32) for p in parts], axis=0).astype(jnp.bfloat16)


def bf16_dot(a, b, a_dim, b_dim):
    return lax.dot_general(
        a, b, (((a_dim,), (b_dim,)), ((), ())), preferred_element_type=jnp.float32
    )


def split_product(rows, parts, contract):
    rank = rows.shape[0]
    stacked = stack(three_parts(rows))
    total = None
    for taken, part in reversed(list(zip((3, 2, 1), parts))):
        products = bf16_dot(stacked[:taken * rank], part, 1, contract)
        for index in reversed(range(taken)):
            term = products[index * rank:(index + 1) * rank]
            total = term if total is None else total + term
    return total


def gram_of(rows):
    rank = rows.shape[0]
    stacked = stack(three_parts(rows))
    products = bf16_dot(stacked, stacked, 1, 1)
    total = None
    for i, j in ((1, 1), (0, 2), (2, 0), (0, 1), (1, 0), (0, 0)):
        term = products[i * rank:(i + 1) * rank, j * rank:(j + 1) * rank]
        total = term if total is None else total + term
    return total


def outer_product(values, weights):
    left, right = three_parts(values), three_parts(weights)
    pairs = ((1, 1), (0, 2), (2, 0), (0, 1), (1, 0), (0, 0))
    return bf16_dot(stack([left[i] for i, _ in pairs]), stack([right[j] for _, j in pairs]), 0, 0)


def eliminate(gram, image):
    rank = gram.shape[0]
    row_index = lax.broadcasted_iota(jnp.int32, image.shape, 0)
    columns = [jnp.broadcast_to(gram[:, k:k + 1], image.shape) for k in range(rank)]
    pivots = jnp.ones_like(image)
    ratios = []
    for k in range(rank):
        pivot = columns[k][k:k + 1, :]
        pivots = jnp.where(row_index == k, pivot, pivots)
        if k + 1 < rank:
            ratio = jnp.where(row_index > k, columns[k] * (1.0 / pivot), 0.0)
            ratios.append(ratio)
            for j in range(k + 1, rank):
                columns[j] = columns[j] - ratio * columns[j][k:k + 1, :]
            image = image - ratio * image[k:k + 1, :]
    return image, pivots, ratios


def back_substitute(ratios, value):
    row_index = lax.broadcasted_iota(jnp.int32, value.shape, 0)
    for k in reversed(range(len(ratios))):
        below = jnp.sum(ratios[k] * value, axis=0, keepdims=True)
        value = jnp.where(row_index == k, value - below, value)
    return value


def own_product(q_hbm, matrix_hbm, packed_ref, parts_ref, main_ref, late_ref, q_vmem, sems):
    rows = parts_ref.shape[1]
    tile = rows // TILES
    places = [
        ref.at[pl.ds(start, tile)]
        for ref in (main_ref, late_ref) for start in range(0, ref.shape[0], tile)
    ]
    copies = [pltpu.make_async_copy(q_hbm.at[0], q_vmem, sems.at[TILES])]
    for index, place in enumerate(places):
        piece = pl.ds(index * tile, tile)
        copies.append(pltpu.make_async_copy(matrix_hbm.at[0, piece], place, sems.at[index]))
    for copy in copies:
        copy.start()
    copies[0].wait()
    q = q_vmem[...]
    packed_ref[:, rows:] = q
    for index, place in enumerate(places):
        copies[index + 1].wait()
        piece = pl.ds(index * tile, tile)
        parts = three_parts(place[...])
        for number, part in enumerate(parts):
            parts_ref[number, piece] = part
        packed_ref[:, piece] = split_product(q, parts, 1)


def spread_first(packed_ref, parts_ref, out_ref):
    rows = parts_ref.shape[1]
    mine = split_product(packed_ref[:, rows:], [parts_ref[i] for i in range(3)], 1)
    part = packed_ref[:, :rows] - mine
    for peer in range(out_ref.shape[0]):
        out_ref[peer] = part


def total_of(sums_ref):
    value = sums_ref[0]
    for peer in range(1, sums_ref.shape[0]):
        value = value + sums_ref[peer]
    return value


def add_up(sums_ref, out_ref):
    out_ref[...] = total_of(sums_ref)


def middle_main(sum_ref, other_ref, mine_ref, left_ref, value_ref, gram_ref, image_ref, main_ref):
    split = mine_ref.shape[0]
    value = sum_ref[...] + other_ref[...]
    value_ref[...] = value
    delta = three_parts(left_ref[...] - mine_ref[...])
    for index, part in enumerate(delta):
        main_ref[index] = part
    image_ref[...] = split_product(value[:, :split], delta, 0)
    gram_ref[...] = gram_of(value)


def middle_late(value_ref, gram_ref, image_ref, main_ref, mine_ref, left_ref, late_ref, out_ref):
    split = main_ref.shape[1]
    late = three_parts(left_ref[...] - mine_ref[...])
    for index, part in enumerate(late):
        late_ref[index] = part
    image = image_ref[...] + split_product(value_ref[:, split:], late, 0)
    image, pivots, _ = eliminate(gram_ref[...], image)
    factor = image * (1.0 / jnp.sqrt(pivots))
    main = split_product(factor, [main_ref[i] for i in range(3)], 1)
    last = split_product(factor, late, 1)
    for peer in range(out_ref.shape[0]):
        out_ref[peer, :, :split] = main
        out_ref[peer, :, split:] = last


def last_step(sums_ref, main_ref, late_ref, packed_ref):
    _, rank, rows = sums_ref.shape
    columns = main_ref.shape[2]
    value = total_of(sums_ref)
    packed_ref[:, :rows] = value
    image = split_product(
        value, [jnp.concatenate([main_ref[i], late_ref[i]], axis=0) for i in range(3)], 0
    )
    image, pivots, ratios = eliminate(gram_of(value), image)
    packed_ref[:, rows:rows + columns] = back_substitute(ratios, image * (1.0 / pivots))
    packed_ref[:, rows + columns:] = image * (1.0 / jnp.sqrt(pivots))


def update_left(main_ref, late_ref, packed_ref, new_ref):
    rows, columns = new_ref.shape
    weights = GOSSIP_RATE * packed_ref[:, rows:rows + columns]
    start = 0
    for matrix_ref in (main_ref, late_ref):
        piece = pl.ds(start, matrix_ref.shape[0])
        new_ref[piece] = matrix_ref[...] + outer_product(packed_ref[:, piece], weights)
        start += matrix_ref.shape[0]


def update_right(matrix_ref, packed_ref, new_hbm, warm_hbm, new_vmem, warm_vmem, sems):
    rows, columns = matrix_ref.shape
    tile = rows // TILES
    warm_vmem[...] = packed_ref[:, rows + columns:]
    copies = [pltpu.make_async_copy(warm_vmem, warm_hbm.at[0], sems.at[TILES])]
    copies[0].start()
    weights = -GOSSIP_RATE * packed_ref[:, rows:rows + columns]
    for index in range(TILES):
        piece = pl.ds(index * tile, tile)
        new_vmem[piece] = matrix_ref[piece] + outer_product(packed_ref[:, piece], weights)
        copy = pltpu.make_async_copy(new_vmem.at[piece], new_hbm.at[0, piece], sems.at[index])
        copy.start()
        copies.append(copy)
    for copy in copies:
        copy.wait()


def sum_over_y(spread):
    peers = lax.axis_size("tp")
    groups = [list(range(start, peers, 2)) for start in range(2)]
    spread = lax.all_to_all(spread, "tp", 0, 0, axis_index_groups=groups)
    _, rank, rows = spread.shape
    return kernel_call(
        add_up, jax.ShapeDtypeStruct((rank, rows), jnp.float32), spread.size, 4 * spread.size
    )(spread)


def per_device(params, warm):
    _, rows, columns = params.shape
    rank = warm.shape[1]
    peers = lax.axis_size("tp")
    count = lax.axis_size("blk")
    one = rank * rows * columns * 2
    block = rows * columns * 4
    f32 = jnp.float32
    to_right = [(i, (i + 1) % count) for i in range(count)]
    to_left = [(i, (i - 1) % count) for i in range(count)]
    split_at = rows - rows // TILES * LATE
    run = count // RUNS
    ends = [run * (i + 1) - 1 for i in range(RUNS)]
    swap_ends = [(i, i) for i in range(count) if i not in ends]
    swap_ends += [(end, ends[index - 1]) for index, end in enumerate(ends)]
    in_run = [(i, i // run * run + (i + 1) % run) for i in range(count)]

    def spread(peers):
        return jax.ShapeDtypeStruct((peers, rank, rows), f32)

    def split(rows):
        return jax.ShapeDtypeStruct((3, rows, columns), jnp.bfloat16)

    matrix = jax.ShapeDtypeStruct((rows, columns), f32)
    hbm = pl.BlockSpec(memory_space=pltpu.HBM)
    factor_scratch = pltpu.VMEM((rank, columns), f32)
    sems = pltpu.SemaphoreType.DMA((TILES + 1,))

    packed, parts, main, late = kernel_call(
        own_product,
        (
            jax.ShapeDtypeStruct((rank, rows + columns), f32), split(rows),
            jax.ShapeDtypeStruct((split_at, columns), f32),
            jax.ShapeDtypeStruct((rows - split_at, columns), f32),
        ),
        6 * one, 2 * block, in_specs=[hbm, hbm], scratch_shapes=[factor_scratch, sems],
    )(pltpu.with_memory_space_constraint(warm, pltpu.HBM), pltpu.with_memory_space_constraint(params, pltpu.HBM))
    packed = lax.ppermute(packed, "blk", to_right)
    left_main = lax.ppermute(main, "blk", to_right)
    carried = lax.ppermute(late, "blk", swap_ends)
    sums = kernel_call(spread_first, spread(peers // 2), 1250 * one, block)(packed, parts)
    sums = sum_over_y(sums)
    carried, sums = lax.optimization_barrier((carried, sums))
    left_late = lax.ppermute(carried, "blk", in_run)
    other = lax.ppermute(sums, "tp", [(i, i ^ 1) for i in range(peers)])
    value, gram, image, delta_main = kernel_call(
        middle_main,
        (
            jax.ShapeDtypeStruct((rank, rows), f32), jax.ShapeDtypeStruct((rank, rank), f32),
            jax.ShapeDtypeStruct((rank, columns), f32), split(split_at),
        ),
        4000 * one, 2 * block,
    )(sums, other, main, left_main)
    delta_late, sums = kernel_call(middle_late, (split(rows - split_at), spread(peers)), 6 * one, block)(
        value, gram, image, delta_main, late, left_late
    )
    sums = lax.all_to_all(sums, "tp", 0, 0)
    own = kernel_call(
        last_step, jax.ShapeDtypeStruct((rank, rows + 2 * columns), f32), 6 * one, 2 * block
    )(sums, delta_main, delta_late)
    right = lax.ppermute(own, "blk", to_left)
    left_done = kernel_call(update_left, matrix, 6 * one, 2 * block)(main, late, own)
    new_params, next_warm = kernel_call(
        update_right,
        (jax.ShapeDtypeStruct(params.shape, f32), jax.ShapeDtypeStruct(warm.shape, f32)),
        6 * one, 2 * block, out_specs=(hbm, hbm),
        scratch_shapes=[pltpu.VMEM(matrix.shape, f32), factor_scratch, sems],
    )(left_done, right)
    return new_params, next_warm


def solution(mesh):
    spec = P("blk", None, "tp")
    return jax.shard_map(
        per_device, mesh=mesh, in_specs=(spec, spec), out_specs=(spec, spec), check_vma=False
    )
```

```python
import jax
import jax.numpy as jnp
from jax import lax
from jax.experimental import pallas as pl
from jax.experimental.pallas import tpu as pltpu
from jax.sharding import PartitionSpec as P

GOSSIP_RATE = 0.5
TILES = 4
LATE = 1
RUNS = 2


def kernel_call(body, out_shape, flops, moved, **blocks):
    return pl.pallas_call(
        body,
        out_shape=out_shape,
        **blocks,
        compiler_params=pltpu.CompilerParams(vmem_limit_bytes=24 << 20),
        cost_estimate=pl.CostEstimate(flops=flops, bytes_accessed=moved, transcendentals=0),
    )


def three_parts(value):
    high = value.astype(jnp.bfloat16)
    rest = value - high.astype(jnp.float32)
    middle = rest.astype(jnp.bfloat16)
    low = (rest - middle.astype(jnp.float32)).astype(jnp.bfloat16)
    return high, middle, low


def stack(parts):
    return jnp.concatenate([p.astype(jnp.float32) for p in parts], axis=0).astype(jnp.bfloat16)


def bf16_dot(a, b, a_dim, b_dim):
    return lax.dot_general(
        a, b, (((a_dim,), (b_dim,)), ((), ())), preferred_element_type=jnp.float32
    )


def split_product(rows, parts, contract):
    rank = rows.shape[0]
    stacked = stack(three_parts(rows))
    total = None
    for taken, part in reversed(list(zip((3, 2, 1), parts))):
        products = bf16_dot(stacked[:taken * rank], part, 1, contract)
        for index in reversed(range(taken)):
            term = products[index * rank:(index + 1) * rank]
            total = term if total is None else total + term
    return total


def gram_of(rows):
    rank = rows.shape[0]
    stacked = stack(three_parts(rows))
    products = bf16_dot(stacked, stacked, 1, 1)
    total = None
    for i, j in ((1, 1), (0, 2), (2, 0), (0, 1), (1, 0), (0, 0)):
        term = products[i * rank:(i + 1) * rank, j * rank:(j + 1) * rank]
        total = term if total is None else total + term
    return total


def outer_product(values, weights):
    left, right = three_parts(values), three_parts(weights)
    pairs = ((1, 1), (0, 2), (2, 0), (0, 1), (1, 0), (0, 0))
    return bf16_dot(stack([left[i] for i, _ in pairs]), stack([right[j] for _, j in pairs]), 0, 0)


def eliminate(gram, image):
    rank = gram.shape[0]
    row_index = lax.broadcasted_iota(jnp.int32, image.shape, 0)
    columns = [jnp.broadcast_to(gram[:, k:k + 1], image.shape) for k in range(rank)]
    pivots = jnp.ones_like(image)
    ratios = []
    for k in range(rank):
        pivot = columns[k][k:k + 1, :]
        pivots = jnp.where(row_index == k, pivot, pivots)
        if k + 1 < rank:
            ratio = jnp.where(row_index > k, columns[k] * (1.0 / pivot), 0.0)
            ratios.append(ratio)
            for j in range(k + 1, rank):
                columns[j] = columns[j] - ratio * columns[j][k:k + 1, :]
            image = image - ratio * image[k:k + 1, :]
    return image, pivots, ratios


def back_substitute(ratios, value):
    row_index = lax.broadcasted_iota(jnp.int32, value.shape, 0)
    for k in reversed(range(len(ratios))):
        below = jnp.sum(ratios[k] * value, axis=0, keepdims=True)
        value = jnp.where(row_index == k, value - below, value)
    return value


def own_product(q_hbm, matrix_hbm, packed_ref, parts_ref, main_ref, late_ref, q_vmem, sems):
    rows = parts_ref.shape[1]
    tile = rows // TILES
    places = [
        ref.at[pl.ds(start, tile)]
        for ref in (main_ref, late_ref) for start in range(0, ref.shape[0], tile)
    ]
    copies = [pltpu.make_async_copy(q_hbm.at[0], q_vmem, sems.at[TILES])]
    for index, place in enumerate(places):
        piece = pl.ds(index * tile, tile)
        copies.append(pltpu.make_async_copy(matrix_hbm.at[0, piece], place, sems.at[index]))
    for copy in copies:
        copy.start()
    copies[0].wait()
    q = q_vmem[...]
    packed_ref[:, rows:] = q
    for index, place in enumerate(places):
        copies[index + 1].wait()
        piece = pl.ds(index * tile, tile)
        parts = three_parts(place[...])
        for number, part in enumerate(parts):
            parts_ref[number, piece] = part
        packed_ref[:, piece] = split_product(q, parts, 1)


def spread_first(packed_ref, parts_ref, out_ref):
    rows = parts_ref.shape[1]
    mine = split_product(packed_ref[:, rows:], [parts_ref[i] for i in range(3)], 1)
    part = packed_ref[:, :rows] - mine
    for peer in range(out_ref.shape[0]):
        out_ref[peer] = part


def total_of(sums_ref):
    value = sums_ref[0]
    for peer in range(1, sums_ref.shape[0]):
        value = value + sums_ref[peer]
    return value


def add_up(sums_ref, out_ref):
    out_ref[...] = total_of(sums_ref)


def split_difference(mine_ref, left_ref, delta_ref):
    for index, part in enumerate(three_parts(left_ref[...] - mine_ref[...])):
        delta_ref[index] = part


def middle_step(sum_ref, other_ref, main_ref, mine_ref, left_ref, late_ref, out_ref):
    split = main_ref.shape[1]
    value = sum_ref[...] + other_ref[...]
    main = [main_ref[i] for i in range(3)]
    late = three_parts(left_ref[...] - mine_ref[...])
    for index, part in enumerate(late):
        late_ref[index] = part
    image = split_product(value[:, :split], main, 0) + split_product(value[:, split:], late, 0)
    image, pivots, _ = eliminate(gram_of(value), image)
    factor = image * (1.0 / jnp.sqrt(pivots))
    first = split_product(factor, main, 1)
    last = split_product(factor, late, 1)
    for peer in range(out_ref.shape[0]):
        out_ref[peer, :, :split] = first
        out_ref[peer, :, split:] = last


def last_step(sums_ref, main_ref, late_ref, packed_ref):
    _, rank, rows = sums_ref.shape
    columns = main_ref.shape[2]
    value = total_of(sums_ref)
    packed_ref[:, :rows] = value
    image = split_product(
        value, [jnp.concatenate([main_ref[i], late_ref[i]], axis=0) for i in range(3)], 0
    )
    image, pivots, ratios = eliminate(gram_of(value), image)
    packed_ref[:, rows:rows + columns] = back_substitute(ratios, image * (1.0 / pivots))
    packed_ref[:, rows + columns:] = image * (1.0 / jnp.sqrt(pivots))


def update_left(main_ref, late_ref, packed_ref, new_ref):
    rows, columns = new_ref.shape
    weights = GOSSIP_RATE * packed_ref[:, rows:rows + columns]
    start = 0
    for matrix_ref in (main_ref, late_ref):
        piece = pl.ds(start, matrix_ref.shape[0])
        new_ref[piece] = matrix_ref[...] + outer_product(packed_ref[:, piece], weights)
        start += matrix_ref.shape[0]


def update_right(matrix_ref, packed_ref, new_hbm, warm_hbm, new_vmem, warm_vmem, sems):
    rows, columns = matrix_ref.shape
    tile = rows // TILES
    warm_vmem[...] = packed_ref[:, rows + columns:]
    copies = [pltpu.make_async_copy(warm_vmem, warm_hbm.at[0], sems.at[TILES])]
    copies[0].start()
    weights = -GOSSIP_RATE * packed_ref[:, rows:rows + columns]
    for index in range(TILES):
        piece = pl.ds(index * tile, tile)
        new_vmem[piece] = matrix_ref[piece] + outer_product(packed_ref[:, piece], weights)
        copy = pltpu.make_async_copy(new_vmem.at[piece], new_hbm.at[0, piece], sems.at[index])
        copy.start()
        copies.append(copy)
    for copy in copies:
        copy.wait()


def sum_over_y(spread):
    peers = lax.axis_size("tp")
    groups = [list(range(start, peers, 2)) for start in range(2)]
    spread = lax.all_to_all(spread, "tp", 0, 0, axis_index_groups=groups)
    _, rank, rows = spread.shape
    return kernel_call(
        add_up, jax.ShapeDtypeStruct((rank, rows), jnp.float32), spread.size, 4 * spread.size
    )(spread)


def per_device(params, warm):
    _, rows, columns = params.shape
    rank = warm.shape[1]
    peers = lax.axis_size("tp")
    count = lax.axis_size("blk")
    one = rank * rows * columns * 2
    block = rows * columns * 4
    f32 = jnp.float32
    to_right = [(i, (i + 1) % count) for i in range(count)]
    to_left = [(i, (i - 1) % count) for i in range(count)]
    split_at = rows - rows // TILES * LATE
    run = count // RUNS
    ends = [run * (i + 1) - 1 for i in range(RUNS)]
    swap_ends = [(i, i) for i in range(count) if i not in ends]
    swap_ends += [(end, ends[index - 1]) for index, end in enumerate(ends)]
    in_run = [(i, i // run * run + (i + 1) % run) for i in range(count)]

    def spread(peers):
        return jax.ShapeDtypeStruct((peers, rank, rows), f32)

    def split(rows):
        return jax.ShapeDtypeStruct((3, rows, columns), jnp.bfloat16)

    matrix = jax.ShapeDtypeStruct((rows, columns), f32)
    hbm = pl.BlockSpec(memory_space=pltpu.HBM)
    factor_scratch = pltpu.VMEM((rank, columns), f32)
    sems = pltpu.SemaphoreType.DMA((TILES + 1,))

    packed, parts, main, late = kernel_call(
        own_product,
        (
            jax.ShapeDtypeStruct((rank, rows + columns), f32), split(rows),
            jax.ShapeDtypeStruct((split_at, columns), f32),
            jax.ShapeDtypeStruct((rows - split_at, columns), f32),
        ),
        6 * one, 2 * block, in_specs=[hbm, hbm], scratch_shapes=[factor_scratch, sems],
    )(pltpu.with_memory_space_constraint(warm, pltpu.HBM), pltpu.with_memory_space_constraint(params, pltpu.HBM))
    packed = lax.ppermute(packed, "blk", to_right)
    left_main = lax.ppermute(main, "blk", to_right)
    carried = lax.ppermute(late, "blk", swap_ends)
    sums = kernel_call(spread_first, spread(peers // 2), 750 * one, block)(packed, parts)
    sums = sum_over_y(sums)
    carried, sums = lax.optimization_barrier((carried, sums))
    left_late = lax.ppermute(carried, "blk", in_run)
    other = lax.ppermute(sums, "tp", [(i, i ^ 1) for i in range(peers)])
    delta_main = kernel_call(split_difference, split(split_at), one // 64, 3 * block)(main, left_main)
    delta_late, sums = kernel_call(middle_step, (split(rows - split_at), spread(peers)), 12 * one, 3 * block)(
        sums, other, delta_main, late, left_late
    )
    sums = lax.all_to_all(sums, "tp", 0, 0)
    own = kernel_call(
        last_step, jax.ShapeDtypeStruct((rank, rows + 2 * columns), f32), 6 * one, 2 * block
    )(sums, delta_main, delta_late)
    right = lax.ppermute(own, "blk", to_left)
    left_done = kernel_call(update_left, matrix, 6 * one, 2 * block)(main, late, own)
    new_params, next_warm = kernel_call(
        update_right,
        (jax.ShapeDtypeStruct(params.shape, f32), jax.ShapeDtypeStruct(warm.shape, f32)),
        6 * one, 2 * block, out_specs=(hbm, hbm),
        scratch_shapes=[pltpu.VMEM(matrix.shape, f32), factor_scratch, sems],
    )(left_done, right)
    return new_params, next_warm


def solution(mesh):
    spec = P("blk", None, "tp")
    return jax.shard_map(
        per_device, mesh=mesh, in_specs=(spec, spec), out_specs=(spec, spec), check_vma=False
    )
```

```python
import jax
import jax.numpy as jnp
from jax import lax
from jax.experimental import pallas as pl
from jax.experimental.pallas import tpu as pltpu
from jax.sharding import PartitionSpec as P

GOSSIP_RATE = 0.5
TILES = 4
LATE = 1
RUNS = 2


def kernel_call(body, out_shape, flops, moved, **blocks):
    return pl.pallas_call(
        body,
        out_shape=out_shape,
        **blocks,
        compiler_params=pltpu.CompilerParams(vmem_limit_bytes=24 << 20),
        cost_estimate=pl.CostEstimate(flops=flops, bytes_accessed=moved, transcendentals=0),
    )


def three_parts(value):
    high = value.astype(jnp.bfloat16)
    rest = value - high.astype(jnp.float32)
    middle = rest.astype(jnp.bfloat16)
    low = (rest - middle.astype(jnp.float32)).astype(jnp.bfloat16)
    return high, middle, low


def stack(parts):
    return jnp.concatenate([p.astype(jnp.float32) for p in parts], axis=0).astype(jnp.bfloat16)


def bf16_dot(a, b, a_dim, b_dim):
    return lax.dot_general(
        a, b, (((a_dim,), (b_dim,)), ((), ())), preferred_element_type=jnp.float32
    )


def split_product(rows, parts, contract):
    rank = rows.shape[0]
    stacked = stack(three_parts(rows))
    total = None
    for taken, part in reversed(list(zip((3, 2, 1), parts))):
        products = bf16_dot(stacked[:taken * rank], part, 1, contract)
        for index in reversed(range(taken)):
            term = products[index * rank:(index + 1) * rank]
            total = term if total is None else total + term
    return total


def gram_of(rows):
    rank = rows.shape[0]
    stacked = stack(three_parts(rows))
    products = bf16_dot(stacked, stacked, 1, 1)
    total = None
    for i, j in ((1, 1), (0, 2), (2, 0), (0, 1), (1, 0), (0, 0)):
        term = products[i * rank:(i + 1) * rank, j * rank:(j + 1) * rank]
        total = term if total is None else total + term
    return total


def outer_product(values, weights):
    left, right = three_parts(values), three_parts(weights)
    pairs = ((1, 1), (0, 2), (2, 0), (0, 1), (1, 0), (0, 0))
    return bf16_dot(stack([left[i] for i, _ in pairs]), stack([right[j] for _, j in pairs]), 0, 0)


def eliminate(gram, image):
    rank = gram.shape[0]
    row_index = lax.broadcasted_iota(jnp.int32, image.shape, 0)
    columns = [jnp.broadcast_to(gram[:, k:k + 1], image.shape) for k in range(rank)]
    pivots = jnp.ones_like(image)
    ratios = []
    for k in range(rank):
        pivot = columns[k][k:k + 1, :]
        pivots = jnp.where(row_index == k, pivot, pivots)
        if k + 1 < rank:
            ratio = jnp.where(row_index > k, columns[k] * (1.0 / pivot), 0.0)
            ratios.append(ratio)
            for j in range(k + 1, rank):
                columns[j] = columns[j] - ratio * columns[j][k:k + 1, :]
            image = image - ratio * image[k:k + 1, :]
    return image, pivots, ratios


def back_substitute(ratios, value):
    row_index = lax.broadcasted_iota(jnp.int32, value.shape, 0)
    for k in reversed(range(len(ratios))):
        below = jnp.sum(ratios[k] * value, axis=0, keepdims=True)
        value = jnp.where(row_index == k, value - below, value)
    return value


def own_product(q_hbm, matrix_hbm, packed_ref, parts_ref, main_ref, late_ref, q_vmem, sems):
    split = main_ref.shape[0]
    half, rows = split // 2, split + late_ref.shape[0]
    pieces = [(0, half), (half, split), (split, rows)]
    places = [main_ref.at[pl.ds(0, half)], main_ref.at[pl.ds(half, half)], late_ref]
    copies = [pltpu.make_async_copy(q_hbm.at[0], q_vmem, sems.at[TILES])]
    for index, (start, end) in enumerate(pieces):
        piece = pl.ds(start, end - start)
        copies.append(pltpu.make_async_copy(matrix_hbm.at[0, piece], places[index], sems.at[index]))
    for copy in copies:
        copy.start()
    copies[0].wait()
    q = q_vmem[...]
    packed_ref[:, rows:] = q
    for index, (start, end) in enumerate(pieces):
        copies[index + 1].wait()
        parts = three_parts(places[index][...].T)
        for number, part in enumerate(parts):
            parts_ref[number, :, start:end] = part
        packed_ref[:, start:end] = split_product(q, parts, 0)


def spread_first(packed_ref, parts_ref, out_ref):
    rows = parts_ref.shape[2]
    mine = split_product(packed_ref[:, rows:], [parts_ref[i] for i in range(3)], 0)
    part = packed_ref[:, :rows] - mine
    for peer in range(out_ref.shape[0]):
        out_ref[peer] = part


def total_of(sums_ref):
    value = sums_ref[0]
    for peer in range(1, sums_ref.shape[0]):
        value = value + sums_ref[peer]
    return value


def add_up(sums_ref, out_ref):
    out_ref[...] = total_of(sums_ref)


def split_difference(mine_ref, left_ref, delta_ref, turned_ref):
    difference = left_ref[...] - mine_ref[...]
    for index, part in enumerate(three_parts(difference)):
        delta_ref[index] = part
    for index, part in enumerate(three_parts(difference.T)):
        turned_ref[index] = part


def middle_step(sum_ref, other_ref, main_ref, turned_ref, mine_ref, left_ref, late_ref, out_ref):
    split = main_ref.shape[1]
    value = sum_ref[...] + other_ref[...]
    late = three_parts(left_ref[...] - mine_ref[...])
    for index, part in enumerate(late):
        late_ref[index] = part
    image = split_product(value[:, :split], [main_ref[i] for i in range(3)], 0)
    image = image + split_product(value[:, split:], late, 0)
    image, pivots, _ = eliminate(gram_of(value), image)
    factor = image * (1.0 / jnp.sqrt(pivots))
    first = split_product(factor, [turned_ref[i] for i in range(3)], 0)
    last = split_product(factor, late, 1)
    for peer in range(out_ref.shape[0]):
        out_ref[peer, :, :split] = first
        out_ref[peer, :, split:] = last


def last_step(sums_ref, main_ref, late_ref, packed_ref):
    _, rank, rows = sums_ref.shape
    columns = main_ref.shape[2]
    value = total_of(sums_ref)
    packed_ref[:, :rows] = value
    image = split_product(
        value, [jnp.concatenate([main_ref[i], late_ref[i]], axis=0) for i in range(3)], 0
    )
    image, pivots, ratios = eliminate(gram_of(value), image)
    packed_ref[:, rows:rows + columns] = back_substitute(ratios, image * (1.0 / pivots))
    packed_ref[:, rows + columns:] = image * (1.0 / jnp.sqrt(pivots))


def update_left(main_ref, late_ref, packed_ref, new_ref):
    rows, columns = new_ref.shape
    weights = GOSSIP_RATE * packed_ref[:, rows:rows + columns]
    start = 0
    for matrix_ref in (main_ref, late_ref):
        piece = pl.ds(start, matrix_ref.shape[0])
        new_ref[piece] = matrix_ref[...] + outer_product(packed_ref[:, piece], weights)
        start += matrix_ref.shape[0]


def update_right(matrix_ref, packed_ref, new_hbm, warm_hbm, new_vmem, warm_vmem, sems):
    rows, columns = matrix_ref.shape
    tile = rows // TILES
    warm_vmem[...] = packed_ref[:, rows + columns:]
    copies = [pltpu.make_async_copy(warm_vmem, warm_hbm.at[0], sems.at[TILES])]
    copies[0].start()
    weights = -GOSSIP_RATE * packed_ref[:, rows:rows + columns]
    for index in range(TILES):
        piece = pl.ds(index * tile, tile)
        new_vmem[piece] = matrix_ref[piece] + outer_product(packed_ref[:, piece], weights)
        copy = pltpu.make_async_copy(new_vmem.at[piece], new_hbm.at[0, piece], sems.at[index])
        copy.start()
        copies.append(copy)
    for copy in copies:
        copy.wait()


def sum_over_y(spread):
    peers = lax.axis_size("tp")
    groups = [list(range(start, peers, 2)) for start in range(2)]
    spread = lax.all_to_all(spread, "tp", 0, 0, axis_index_groups=groups)
    _, rank, rows = spread.shape
    return kernel_call(
        add_up, jax.ShapeDtypeStruct((rank, rows), jnp.float32), spread.size, 4 * spread.size
    )(spread)


def per_device(params, warm):
    _, rows, columns = params.shape
    rank = warm.shape[1]
    peers = lax.axis_size("tp")
    count = lax.axis_size("blk")
    one = rank * rows * columns * 2
    block = rows * columns * 4
    f32 = jnp.float32
    to_right = [(i, (i + 1) % count) for i in range(count)]
    to_left = [(i, (i - 1) % count) for i in range(count)]
    split_at = rows - rows // TILES * LATE
    run = count // RUNS
    ends = [run * (i + 1) - 1 for i in range(RUNS)]
    swap_ends = [(i, i) for i in range(count) if i not in ends]
    swap_ends += [(end, ends[index - 1]) for index, end in enumerate(ends)]
    in_run = [(i, i // run * run + (i + 1) % run) for i in range(count)]

    def spread(peers):
        return jax.ShapeDtypeStruct((peers, rank, rows), f32)

    def split(rows):
        return jax.ShapeDtypeStruct((3, rows, columns), jnp.bfloat16)

    def turned(rows):
        return jax.ShapeDtypeStruct((3, columns, rows), jnp.bfloat16)

    matrix = jax.ShapeDtypeStruct((rows, columns), f32)
    hbm = pl.BlockSpec(memory_space=pltpu.HBM)
    factor_scratch = pltpu.VMEM((rank, columns), f32)
    sems = pltpu.SemaphoreType.DMA((TILES + 1,))

    packed, parts, main, late = kernel_call(
        own_product,
        (
            jax.ShapeDtypeStruct((rank, rows + columns), f32), turned(rows),
            jax.ShapeDtypeStruct((split_at, columns), f32),
            jax.ShapeDtypeStruct((rows - split_at, columns), f32),
        ),
        6 * one, 2 * block, in_specs=[hbm, hbm], scratch_shapes=[factor_scratch, sems],
    )(pltpu.with_memory_space_constraint(warm, pltpu.HBM), pltpu.with_memory_space_constraint(params, pltpu.HBM))
    packed = lax.ppermute(packed, "blk", to_right)
    left_main = lax.ppermute(main, "blk", to_right)
    carried = lax.ppermute(late, "blk", swap_ends)
    sums = kernel_call(spread_first, spread(peers // 2), 750 * one, block)(packed, parts)
    sums = sum_over_y(sums)
    carried, sums = lax.optimization_barrier((carried, sums))
    left_late = lax.ppermute(carried, "blk", in_run)
    other = lax.ppermute(sums, "tp", [(i, i ^ 1) for i in range(peers)])
    delta_main, delta_turned = kernel_call(
        split_difference, (split(split_at), turned(split_at)), one // 64, 3 * block
    )(main, left_main)
    delta_late, sums = kernel_call(middle_step, (split(rows - split_at), spread(peers)), 12 * one, 3 * block)(
        sums, other, delta_main, delta_turned, late, left_late
    )
    sums = lax.all_to_all(sums, "tp", 0, 0)
    own = kernel_call(
        last_step, jax.ShapeDtypeStruct((rank, rows + 2 * columns), f32), 6 * one, 2 * block
    )(sums, delta_main, delta_late)
    right = lax.ppermute(own, "blk", to_left)
    left_done = kernel_call(update_left, matrix, 6 * one, 2 * block)(main, late, own)
    new_params, next_warm = kernel_call(
        update_right,
        (jax.ShapeDtypeStruct(params.shape, f32), jax.ShapeDtypeStruct(warm.shape, f32)),
        6 * one, 2 * block, out_specs=(hbm, hbm),
        scratch_shapes=[pltpu.VMEM(matrix.shape, f32), factor_scratch, sems],
    )(left_done, right)
    return new_params, next_warm


def solution(mesh):
    spec = P("blk", None, "tp")
    return jax.shard_map(
        per_device, mesh=mesh, in_specs=(spec, spec), out_specs=(spec, spec), check_vma=False
    )
```

```python
import jax
import jax.numpy as jnp
from jax import lax
from jax.experimental import pallas as pl
from jax.experimental.pallas import tpu as pltpu
from jax.sharding import PartitionSpec as P

GOSSIP_RATE = 0.5
TILES = 4
COPIES = 16
LATE = 1
RUNS = 2


def kernel_call(body, out_shape, flops, moved, **blocks):
    return pl.pallas_call(
        body,
        out_shape=out_shape,
        **blocks,
        compiler_params=pltpu.CompilerParams(vmem_limit_bytes=24 << 20),
        cost_estimate=pl.CostEstimate(flops=flops, bytes_accessed=moved, transcendentals=0),
    )


def three_parts(value):
    high = value.astype(jnp.bfloat16)
    rest = value - high.astype(jnp.float32)
    middle = rest.astype(jnp.bfloat16)
    low = (rest - middle.astype(jnp.float32)).astype(jnp.bfloat16)
    return high, middle, low


def stack(parts):
    return jnp.concatenate([p.astype(jnp.float32) for p in parts], axis=0).astype(jnp.bfloat16)


def bf16_dot(a, b, a_dim, b_dim):
    return lax.dot_general(
        a, b, (((a_dim,), (b_dim,)), ((), ())), preferred_element_type=jnp.float32
    )


def split_product(rows, parts, contract):
    rank = rows.shape[0]
    stacked = stack(three_parts(rows))
    total = None
    for taken, part in reversed(list(zip((3, 2, 1), parts))):
        products = bf16_dot(stacked[:taken * rank], part, 1, contract)
        for index in reversed(range(taken)):
            term = products[index * rank:(index + 1) * rank]
            total = term if total is None else total + term
    return total


def gram_of(rows):
    rank = rows.shape[0]
    stacked = stack(three_parts(rows))
    products = bf16_dot(stacked, stacked, 1, 1)
    total = None
    for i, j in ((1, 1), (0, 2), (2, 0), (0, 1), (1, 0), (0, 0)):
        term = products[i * rank:(i + 1) * rank, j * rank:(j + 1) * rank]
        total = term if total is None else total + term
    return total


def outer_product(values, weights):
    left, right = three_parts(values), three_parts(weights)
    pairs = ((1, 1), (0, 2), (2, 0), (0, 1), (1, 0), (0, 0))
    return bf16_dot(stack([left[i] for i, _ in pairs]), stack([right[j] for _, j in pairs]), 0, 0)


def eliminate(gram, image):
    rank = gram.shape[0]
    row_index = lax.broadcasted_iota(jnp.int32, image.shape, 0)
    columns = [jnp.broadcast_to(gram[:, k:k + 1], image.shape) for k in range(rank)]
    pivots = jnp.ones_like(image)
    ratios = []
    for k in range(rank):
        pivot = columns[k][k:k + 1, :]
        pivots = jnp.where(row_index == k, pivot, pivots)
        if k + 1 < rank:
            ratio = jnp.where(row_index > k, columns[k] * (1.0 / pivot), 0.0)
            ratios.append(ratio)
            for j in range(k + 1, rank):
                columns[j] = columns[j] - ratio * columns[j][k:k + 1, :]
            image = image - ratio * image[k:k + 1, :]
    return image, pivots, ratios


def back_substitute(ratios, value):
    row_index = lax.broadcasted_iota(jnp.int32, value.shape, 0)
    for k in reversed(range(len(ratios))):
        below = jnp.sum(ratios[k] * value, axis=0, keepdims=True)
        value = jnp.where(row_index == k, value - below, value)
    return value


def own_product(q_hbm, matrix_hbm, packed_ref, parts_ref, main_ref, late_ref, q_vmem, sems):
    split = main_ref.shape[0]
    half, rows = split // 2, split + late_ref.shape[0]
    step = rows // COPIES
    pieces = [(0, half), (half, split), (split, rows)]
    first = pltpu.make_async_copy(q_hbm.at[0], q_vmem, sems.at[COPIES])
    first.start()
    copies = []
    for start in range(0, rows, step):
        place = main_ref.at[pl.ds(start, step)] if start < split else late_ref.at[pl.ds(start - split, step)]
        copy = pltpu.make_async_copy(matrix_hbm.at[0, pl.ds(start, step)], place, sems.at[start // step])
        copy.start()
        copies.append(copy)
    first.wait()
    q = q_vmem[...]
    packed_ref[:, rows:] = q
    for start, end in pieces:
        for copy in copies[start // step:end // step]:
            copy.wait()
        piece = main_ref[start:end] if end <= split else late_ref[...]
        parts = three_parts(piece.T)
        for number, part in enumerate(parts):
            parts_ref[number, :, start:end] = part
        packed_ref[:, start:end] = split_product(q, parts, 0)


def spread_first(packed_ref, parts_ref, out_ref):
    rows = parts_ref.shape[2]
    mine = split_product(packed_ref[:, rows:], [parts_ref[i] for i in range(3)], 0)
    part = packed_ref[:, :rows] - mine
    for peer in range(out_ref.shape[0]):
        out_ref[peer] = part


def total_of(sums_ref):
    value = sums_ref[0]
    for peer in range(1, sums_ref.shape[0]):
        value = value + sums_ref[peer]
    return value


def add_up(sums_ref, out_ref):
    out_ref[...] = total_of(sums_ref)


def split_difference(mine_ref, left_ref, delta_ref, turned_ref):
    difference = left_ref[...] - mine_ref[...]
    for index, part in enumerate(three_parts(difference)):
        delta_ref[index] = part
    for index, part in enumerate(three_parts(difference.T)):
        turned_ref[index] = part


def middle_step(sum_ref, other_ref, main_ref, turned_ref, mine_ref, left_ref, late_ref, out_ref):
    split = main_ref.shape[1]
    value = sum_ref[...] + other_ref[...]
    late = three_parts(left_ref[...] - mine_ref[...])
    for index, part in enumerate(late):
        late_ref[index] = part
    image = split_product(value[:, :split], [main_ref[i] for i in range(3)], 0)
    image = image + split_product(value[:, split:], late, 0)
    image, pivots, _ = eliminate(gram_of(value), image)
    factor = image * (1.0 / jnp.sqrt(pivots))
    first = split_product(factor, [turned_ref[i] for i in range(3)], 0)
    last = split_product(factor, late, 1)
    for peer in range(out_ref.shape[0]):
        out_ref[peer, :, :split] = first
        out_ref[peer, :, split:] = last


def last_step(sums_ref, main_ref, late_ref, packed_ref):
    _, rank, rows = sums_ref.shape
    columns = main_ref.shape[2]
    value = total_of(sums_ref)
    packed_ref[:, :rows] = value
    image = split_product(
        value, [jnp.concatenate([main_ref[i], late_ref[i]], axis=0) for i in range(3)], 0
    )
    image, pivots, ratios = eliminate(gram_of(value), image)
    packed_ref[:, rows:rows + columns] = back_substitute(ratios, image * (1.0 / pivots))
    packed_ref[:, rows + columns:] = image * (1.0 / jnp.sqrt(pivots))


def update_left(main_ref, late_ref, packed_ref, new_ref):
    rows, columns = new_ref.shape
    weights = GOSSIP_RATE * packed_ref[:, rows:rows + columns]
    start = 0
    for matrix_ref in (main_ref, late_ref):
        piece = pl.ds(start, matrix_ref.shape[0])
        new_ref[piece] = matrix_ref[...] + outer_product(packed_ref[:, piece], weights)
        start += matrix_ref.shape[0]


def update_right(matrix_ref, packed_ref, new_hbm, warm_hbm, new_vmem, warm_vmem, sems):
    rows, columns = matrix_ref.shape
    tile, step = rows // TILES, rows // COPIES
    warm_vmem[...] = packed_ref[:, rows + columns:]
    copies = [pltpu.make_async_copy(warm_vmem, warm_hbm.at[0], sems.at[COPIES])]
    copies[0].start()
    weights = -GOSSIP_RATE * packed_ref[:, rows:rows + columns]
    for index in range(TILES):
        piece = pl.ds(index * tile, tile)
        new_vmem[piece] = matrix_ref[piece] + outer_product(packed_ref[:, piece], weights)
        for start in range(index * tile, (index + 1) * tile, step):
            part = pl.ds(start, step)
            copy = pltpu.make_async_copy(new_vmem.at[part], new_hbm.at[0, part], sems.at[start // step])
            copy.start()
            copies.append(copy)
    for copy in copies:
        copy.wait()


def sum_over_y(spread):
    peers = lax.axis_size("tp")
    groups = [list(range(start, peers, 2)) for start in range(2)]
    spread = lax.all_to_all(spread, "tp", 0, 0, axis_index_groups=groups)
    _, rank, rows = spread.shape
    return kernel_call(
        add_up, jax.ShapeDtypeStruct((rank, rows), jnp.float32), spread.size, 4 * spread.size
    )(spread)


def per_device(params, warm):
    _, rows, columns = params.shape
    rank = warm.shape[1]
    peers = lax.axis_size("tp")
    count = lax.axis_size("blk")
    one = rank * rows * columns * 2
    block = rows * columns * 4
    f32 = jnp.float32
    to_right = [(i, (i + 1) % count) for i in range(count)]
    to_left = [(i, (i - 1) % count) for i in range(count)]
    split_at = rows - rows // TILES * LATE
    run = count // RUNS
    ends = [run * (i + 1) - 1 for i in range(RUNS)]
    swap_ends = [(i, i) for i in range(count) if i not in ends]
    swap_ends += [(end, ends[index - 1]) for index, end in enumerate(ends)]
    in_run = [(i, i // run * run + (i + 1) % run) for i in range(count)]

    def spread(peers):
        return jax.ShapeDtypeStruct((peers, rank, rows), f32)

    def split(rows):
        return jax.ShapeDtypeStruct((3, rows, columns), jnp.bfloat16)

    def turned(rows):
        return jax.ShapeDtypeStruct((3, columns, rows), jnp.bfloat16)

    matrix = jax.ShapeDtypeStruct((rows, columns), f32)
    hbm = pl.BlockSpec(memory_space=pltpu.HBM)
    factor_scratch = pltpu.VMEM((rank, columns), f32)
    sems = pltpu.SemaphoreType.DMA((COPIES + 1,))

    packed, parts, main, late = kernel_call(
        own_product,
        (
            jax.ShapeDtypeStruct((rank, rows + columns), f32), turned(rows),
            jax.ShapeDtypeStruct((split_at, columns), f32),
            jax.ShapeDtypeStruct((rows - split_at, columns), f32),
        ),
        6 * one, 2 * block, in_specs=[hbm, hbm], scratch_shapes=[factor_scratch, sems],
    )(pltpu.with_memory_space_constraint(warm, pltpu.HBM), pltpu.with_memory_space_constraint(params, pltpu.HBM))
    packed = lax.ppermute(packed, "blk", to_right)
    left_main = lax.ppermute(main, "blk", to_right)
    carried = lax.ppermute(late, "blk", swap_ends)
    sums = kernel_call(spread_first, spread(peers // 2), 750 * one, block)(packed, parts)
    sums = sum_over_y(sums)
    carried, sums = lax.optimization_barrier((carried, sums))
    left_late = lax.ppermute(carried, "blk", in_run)
    other = lax.ppermute(sums, "tp", [(i, i ^ 1) for i in range(peers)])
    delta_main, delta_turned = kernel_call(
        split_difference, (split(split_at), turned(split_at)), one // 64, 3 * block
    )(main, left_main)
    delta_late, sums = kernel_call(middle_step, (split(rows - split_at), spread(peers)), 12 * one, 3 * block)(
        sums, other, delta_main, delta_turned, late, left_late
    )
    sums = lax.all_to_all(sums, "tp", 0, 0)
    own = kernel_call(
        last_step, jax.ShapeDtypeStruct((rank, rows + 2 * columns), f32), 6 * one, 2 * block
    )(sums, delta_main, delta_late)
    right = lax.ppermute(own, "blk", to_left)
    left_done = kernel_call(update_left, matrix, 6 * one, 2 * block)(main, late, own)
    new_params, next_warm = kernel_call(
        update_right,
        (jax.ShapeDtypeStruct(params.shape, f32), jax.ShapeDtypeStruct(warm.shape, f32)),
        6 * one, 2 * block, out_specs=(hbm, hbm),
        scratch_shapes=[pltpu.VMEM(matrix.shape, f32), factor_scratch, sems],
    )(left_done, right)
    return new_params, next_warm


def solution(mesh):
    spec = P("blk", None, "tp")
    return jax.shard_map(
        per_device, mesh=mesh, in_specs=(spec, spec), out_specs=(spec, spec), check_vma=False
    )
```

```python
import jax
import jax.numpy as jnp
from jax import lax
from jax.experimental import pallas as pl
from jax.experimental.pallas import tpu as pltpu
from jax.sharding import PartitionSpec as P

GOSSIP_RATE = 0.5
TILES = 4
LATE = 1
RUNS = 2


def kernel_call(body, out_shape, flops, moved, **blocks):
    return pl.pallas_call(
        body,
        out_shape=out_shape,
        **blocks,
        compiler_params=pltpu.CompilerParams(vmem_limit_bytes=24 << 20),
        cost_estimate=pl.CostEstimate(flops=flops, bytes_accessed=moved, transcendentals=0),
    )


def three_parts(value):
    high = value.astype(jnp.bfloat16)
    rest = value - high.astype(jnp.float32)
    middle = rest.astype(jnp.bfloat16)
    low = (rest - middle.astype(jnp.float32)).astype(jnp.bfloat16)
    return high, middle, low


def stack(parts):
    return jnp.concatenate([p.astype(jnp.float32) for p in parts], axis=0).astype(jnp.bfloat16)


def bf16_dot(a, b, a_dim, b_dim):
    return lax.dot_general(
        a, b, (((a_dim,), (b_dim,)), ((), ())), preferred_element_type=jnp.float32
    )


def split_product(rows, parts, contract):
    rank = rows.shape[0]
    stacked = stack(three_parts(rows))
    total = None
    for taken, part in reversed(list(zip((3, 2, 1), parts))):
        products = bf16_dot(stacked[:taken * rank], part, 1, contract)
        for index in reversed(range(taken)):
            term = products[index * rank:(index + 1) * rank]
            total = term if total is None else total + term
    return total


def gram_of(rows):
    rank = rows.shape[0]
    stacked = stack(three_parts(rows))
    products = bf16_dot(stacked, stacked, 1, 1)
    total = None
    for i, j in ((1, 1), (0, 2), (2, 0), (0, 1), (1, 0), (0, 0)):
        term = products[i * rank:(i + 1) * rank, j * rank:(j + 1) * rank]
        total = term if total is None else total + term
    return total


def outer_product(values, weights):
    left, right = three_parts(values), three_parts(weights)
    pairs = ((1, 1), (0, 2), (2, 0), (0, 1), (1, 0), (0, 0))
    return bf16_dot(stack([left[i] for i, _ in pairs]), stack([right[j] for _, j in pairs]), 0, 0)


def factorize(gram, shape):
    rank = gram.shape[0]
    row_index = lax.broadcasted_iota(jnp.int32, shape, 0)
    columns = [jnp.broadcast_to(gram[:, k:k + 1], shape) for k in range(rank)]
    pivots = jnp.ones(shape, jnp.float32)
    ratios = []
    for k in range(rank):
        pivot = columns[k][k:k + 1, :]
        pivots = jnp.where(row_index == k, pivot, pivots)
        if k + 1 < rank:
            ratio = jnp.where(row_index > k, columns[k] * (1.0 / pivot), 0.0)
            ratios.append(ratio)
            for j in range(k + 1, rank):
                columns[j] = columns[j] - ratio * columns[j][k:k + 1, :]
    return pivots, ratios


def forward_substitute(ratios, value):
    for k, ratio in enumerate(ratios):
        value = value - ratio * value[k:k + 1, :]
    return value


def back_substitute(ratios, value):
    row_index = lax.broadcasted_iota(jnp.int32, value.shape, 0)
    for k in reversed(range(len(ratios))):
        below = jnp.sum(ratios[k] * value, axis=0, keepdims=True)
        value = jnp.where(row_index == k, value - below, value)
    return value


def own_product(q_hbm, matrix_hbm, packed_ref, parts_ref, main_ref, late_ref, q_vmem, sems):
    split = main_ref.shape[0]
    rows = split + late_ref.shape[0]
    pieces = [(split, rows), (0, split)]
    places = [late_ref, main_ref]
    copies = [pltpu.make_async_copy(q_hbm.at[0], q_vmem, sems.at[TILES])]
    for index, (start, end) in enumerate(pieces):
        piece = pl.ds(start, end - start)
        copies.append(pltpu.make_async_copy(matrix_hbm.at[0, piece], places[index], sems.at[index]))
    for copy in copies:
        copy.start()
    copies[0].wait()
    q = q_vmem[...]
    packed_ref[:, rows:] = q
    for index, (start, end) in enumerate(pieces):
        copies[index + 1].wait()
        parts = three_parts(places[index][...].T)
        for number, part in enumerate(parts):
            parts_ref[number, :, start:end] = part
        packed_ref[:, start:end] = split_product(q, parts, 0)


def spread_first(packed_ref, parts_ref, out_ref):
    rows = parts_ref.shape[2]
    mine = split_product(packed_ref[:, rows:], [parts_ref[i] for i in range(3)], 0)
    part = packed_ref[:, :rows] - mine
    for peer in range(out_ref.shape[0]):
        out_ref[peer] = part


def total_of(sums_ref):
    value = sums_ref[0]
    for peer in range(1, sums_ref.shape[0]):
        value = value + sums_ref[peer]
    return value


def add_up(sums_ref, out_ref):
    out_ref[...] = total_of(sums_ref)


def split_difference(mine_ref, left_ref, delta_ref, turned_ref):
    difference = left_ref[...] - mine_ref[...]
    for index, part in enumerate(three_parts(difference)):
        delta_ref[index] = part
    for index, part in enumerate(three_parts(difference.T)):
        turned_ref[index] = part


def middle_main(sum_ref, other_ref, main_ref, value_ref, image_ref, scale_ref, ratios_ref):
    split = main_ref.shape[1]
    value = sum_ref[...] + other_ref[...]
    value_ref[...] = value[:, split:]
    image_ref[...] = split_product(value[:, :split], [main_ref[i] for i in range(3)], 0)
    pivots, ratios = factorize(gram_of(value), image_ref.shape)
    scale_ref[...] = 1.0 / jnp.sqrt(pivots)
    for index, ratio in enumerate(ratios):
        ratios_ref[index] = ratio


def middle_late(value_ref, image_ref, scale_ref, ratios_ref, turned_ref, mine_ref, left_ref, late_ref, out_ref):
    split = turned_ref.shape[2]
    late = three_parts(left_ref[...] - mine_ref[...])
    for index, part in enumerate(late):
        late_ref[index] = part
    image = image_ref[...] + split_product(value_ref[...], late, 0)
    factor = forward_substitute([ratios_ref[k] for k in range(ratios_ref.shape[0])], image) * scale_ref[...]
    first = split_product(factor, [turned_ref[i] for i in range(3)], 0)
    last = split_product(factor, late, 1)
    for peer in range(out_ref.shape[0]):
        out_ref[peer, :, :split] = first
        out_ref[peer, :, split:] = last


def last_step(sums_ref, main_ref, late_ref, packed_ref):
    _, rank, rows = sums_ref.shape
    columns = main_ref.shape[2]
    value = total_of(sums_ref)
    packed_ref[:, :rows] = value
    image = split_product(
        value, [jnp.concatenate([main_ref[i], late_ref[i]], axis=0) for i in range(3)], 0
    )
    pivots, ratios = factorize(gram_of(value), image.shape)
    image = forward_substitute(ratios, image)
    packed_ref[:, rows:rows + columns] = back_substitute(ratios, image * (1.0 / pivots))
    packed_ref[:, rows + columns:] = image * (1.0 / jnp.sqrt(pivots))


def update_left(main_ref, late_ref, packed_ref, new_ref):
    rows, columns = new_ref.shape
    weights = GOSSIP_RATE * packed_ref[:, rows:rows + columns]
    start = 0
    for matrix_ref in (main_ref, late_ref):
        piece = pl.ds(start, matrix_ref.shape[0])
        new_ref[piece] = matrix_ref[...] + outer_product(packed_ref[:, piece], weights)
        start += matrix_ref.shape[0]


def update_right(matrix_ref, packed_ref, new_hbm, warm_hbm, new_vmem, warm_vmem, sems):
    rows, columns = matrix_ref.shape
    tile = rows // TILES
    warm_vmem[...] = packed_ref[:, rows + columns:]
    copies = [pltpu.make_async_copy(warm_vmem, warm_hbm.at[0], sems.at[TILES])]
    copies[0].start()
    weights = -GOSSIP_RATE * packed_ref[:, rows:rows + columns]
    for index in range(TILES):
        piece = pl.ds(index * tile, tile)
        new_vmem[piece] = matrix_ref[piece] + outer_product(packed_ref[:, piece], weights)
        copy = pltpu.make_async_copy(new_vmem.at[piece], new_hbm.at[0, piece], sems.at[index])
        copy.start()
        copies.append(copy)
    for copy in copies:
        copy.wait()


def sum_over_y(spread):
    peers = lax.axis_size("tp")
    groups = [list(range(start, peers, 2)) for start in range(2)]
    spread = lax.all_to_all(spread, "tp", 0, 0, axis_index_groups=groups)
    _, rank, rows = spread.shape
    return kernel_call(
        add_up, jax.ShapeDtypeStruct((rank, rows), jnp.float32), spread.size, 4 * spread.size
    )(spread)


def per_device(params, warm):
    _, rows, columns = params.shape
    rank = warm.shape[1]
    peers = lax.axis_size("tp")
    count = lax.axis_size("blk")
    one = rank * rows * columns * 2
    block = rows * columns * 4
    f32 = jnp.float32
    to_right = [(i, (i + 1) % count) for i in range(count)]
    to_left = [(i, (i - 1) % count) for i in range(count)]
    split_at = rows - rows // TILES * LATE
    run = count // RUNS
    ends = [run * (i + 1) - 1 for i in range(RUNS)]
    swap_ends = [(i, i) for i in range(count) if i not in ends]
    swap_ends += [(end, ends[index - 1]) for index, end in enumerate(ends)]
    in_run = [(i, i // run * run + (i + 1) % run) for i in range(count)]

    def spread(peers):
        return jax.ShapeDtypeStruct((peers, rank, rows), f32)

    def split(rows):
        return jax.ShapeDtypeStruct((3, rows, columns), jnp.bfloat16)

    def turned(rows):
        return jax.ShapeDtypeStruct((3, columns, rows), jnp.bfloat16)

    matrix = jax.ShapeDtypeStruct((rows, columns), f32)
    hbm = pl.BlockSpec(memory_space=pltpu.HBM)
    factor_scratch = pltpu.VMEM((rank, columns), f32)
    sems = pltpu.SemaphoreType.DMA((TILES + 1,))

    packed, parts, main, late = kernel_call(
        own_product,
        (
            jax.ShapeDtypeStruct((rank, rows + columns), f32), turned(rows),
            jax.ShapeDtypeStruct((split_at, columns), f32),
            jax.ShapeDtypeStruct((rows - split_at, columns), f32),
        ),
        6 * one, 2 * block, in_specs=[hbm, hbm], scratch_shapes=[factor_scratch, sems],
    )(pltpu.with_memory_space_constraint(warm, pltpu.HBM), pltpu.with_memory_space_constraint(params, pltpu.HBM))
    packed = lax.ppermute(packed, "blk", to_right)
    left_main = lax.ppermute(main, "blk", to_right)
    carried = lax.ppermute(late, "blk", swap_ends)
    sums = kernel_call(spread_first, spread(peers // 2), 750 * one, block)(packed, parts)
    sums = sum_over_y(sums)
    carried, sums = lax.optimization_barrier((carried, sums))
    left_late = lax.ppermute(carried, "blk", in_run)
    other = lax.ppermute(sums, "tp", [(i, i ^ 1) for i in range(peers)])
    delta_main, delta_turned = kernel_call(
        split_difference, (split(split_at), turned(split_at)), one // 64, 3 * block
    )(main, left_main)
    factor_shape = jax.ShapeDtypeStruct((rank, columns), f32)
    value, image, scale, ratios = kernel_call(
        middle_main,
        (
            jax.ShapeDtypeStruct((rank, rows - split_at), f32), factor_shape, factor_shape,
            jax.ShapeDtypeStruct((rank - 1, rank, columns), f32),
        ),
        6 * one, 2 * block,
    )(sums, other, delta_main)
    delta_late, sums = kernel_call(middle_late, (split(rows - split_at), spread(peers)), 6 * one, 2 * block)(
        value, image, scale, ratios, delta_turned, late, left_late
    )
    sums = lax.all_to_all(sums, "tp", 0, 0)
    own = kernel_call(
        last_step, jax.ShapeDtypeStruct((rank, rows + 2 * columns), f32), 6 * one, 2 * block
    )(sums, delta_main, delta_late)
    right = lax.ppermute(own, "blk", to_left)
    left_done = kernel_call(update_left, matrix, 6 * one, 2 * block)(main, late, own)
    new_params, next_warm = kernel_call(
        update_right,
        (jax.ShapeDtypeStruct(params.shape, f32), jax.ShapeDtypeStruct(warm.shape, f32)),
        6 * one, 2 * block, out_specs=(hbm, hbm),
        scratch_shapes=[pltpu.VMEM(matrix.shape, f32), factor_scratch, sems],
    )(left_done, right)
    return new_params, next_warm


def solution(mesh):
    spec = P("blk", None, "tp")
    return jax.shard_map(
        per_device, mesh=mesh, in_specs=(spec, spec), out_specs=(spec, spec), check_vma=False
    )
```

```python
import jax
import jax.numpy as jnp
from jax import lax
from jax.experimental import pallas as pl
from jax.experimental.pallas import tpu as pltpu
from jax.sharding import PartitionSpec as P

GOSSIP_RATE = 0.5
TILES = 4
SIXTEENTHS = 11
RUNS = 2


def kernel_call(body, out_shape, flops, moved, **blocks):
    return pl.pallas_call(
        body,
        out_shape=out_shape,
        **blocks,
        compiler_params=pltpu.CompilerParams(vmem_limit_bytes=24 << 20),
        cost_estimate=pl.CostEstimate(flops=flops, bytes_accessed=moved, transcendentals=0),
    )


def three_parts(value):
    high = value.astype(jnp.bfloat16)
    rest = value - high.astype(jnp.float32)
    middle = rest.astype(jnp.bfloat16)
    low = (rest - middle.astype(jnp.float32)).astype(jnp.bfloat16)
    return high, middle, low


def stack(parts):
    return jnp.concatenate([p.astype(jnp.float32) for p in parts], axis=0).astype(jnp.bfloat16)


def bf16_dot(a, b, a_dim, b_dim):
    return lax.dot_general(
        a, b, (((a_dim,), (b_dim,)), ((), ())), preferred_element_type=jnp.float32
    )


def split_product(rows, parts, contract):
    rank = rows.shape[0]
    stacked = stack(three_parts(rows))
    total = None
    for taken, part in reversed(list(zip((3, 2, 1), parts))):
        products = bf16_dot(stacked[:taken * rank], part, 1, contract)
        for index in reversed(range(taken)):
            term = products[index * rank:(index + 1) * rank]
            total = term if total is None else total + term
    return total


def gram_of(rows):
    rank = rows.shape[0]
    stacked = stack(three_parts(rows))
    products = bf16_dot(stacked, stacked, 1, 1)
    total = None
    for i, j in ((1, 1), (0, 2), (2, 0), (0, 1), (1, 0), (0, 0)):
        term = products[i * rank:(i + 1) * rank, j * rank:(j + 1) * rank]
        total = term if total is None else total + term
    return total


def outer_product(values, weights):
    left, right = three_parts(values), three_parts(weights)
    pairs = ((1, 1), (0, 2), (2, 0), (0, 1), (1, 0), (0, 0))
    return bf16_dot(stack([left[i] for i, _ in pairs]), stack([right[j] for _, j in pairs]), 0, 0)


def factorize(gram, shape):
    rank = gram.shape[0]
    row_index = lax.broadcasted_iota(jnp.int32, shape, 0)
    columns = [jnp.broadcast_to(gram[:, k:k + 1], shape) for k in range(rank)]
    pivots = jnp.ones(shape, jnp.float32)
    ratios = []
    for k in range(rank):
        pivot = columns[k][k:k + 1, :]
        pivots = jnp.where(row_index == k, pivot, pivots)
        if k + 1 < rank:
            ratio = jnp.where(row_index > k, columns[k] * (1.0 / pivot), 0.0)
            ratios.append(ratio)
            for j in range(k + 1, rank):
                columns[j] = columns[j] - ratio * columns[j][k:k + 1, :]
    return pivots, ratios


def forward_substitute(ratios, value):
    for k, ratio in enumerate(ratios):
        value = value - ratio * value[k:k + 1, :]
    return value


def back_substitute(ratios, value):
    row_index = lax.broadcasted_iota(jnp.int32, value.shape, 0)
    for k in reversed(range(len(ratios))):
        below = jnp.sum(ratios[k] * value, axis=0, keepdims=True)
        value = jnp.where(row_index == k, value - below, value)
    return value


def own_product(q_hbm, matrix_hbm, packed_ref, parts_ref, main_ref, late_ref, q_vmem, sems):
    split = main_ref.shape[0]
    rows = split + late_ref.shape[0]
    pieces = [(split, rows), (0, split)]
    places = [late_ref, main_ref]
    copies = [pltpu.make_async_copy(q_hbm.at[0], q_vmem, sems.at[TILES])]
    for index, (start, end) in enumerate(pieces):
        piece = pl.ds(start, end - start)
        copies.append(pltpu.make_async_copy(matrix_hbm.at[0, piece], places[index], sems.at[index]))
    for copy in copies:
        copy.start()
    copies[0].wait()
    q = q_vmem[...]
    packed_ref[:, rows:] = q
    for index, (start, end) in enumerate(pieces):
        copies[index + 1].wait()
        parts = three_parts(places[index][...].T)
        for number, part in enumerate(parts):
            parts_ref[number, :, start:end] = part
        packed_ref[:, start:end] = split_product(q, parts, 0)


def spread_first(packed_ref, parts_ref, out_ref):
    rows = parts_ref.shape[2]
    mine = split_product(packed_ref[:, rows:], [parts_ref[i] for i in range(3)], 0)
    part = packed_ref[:, :rows] - mine
    for peer in range(out_ref.shape[0]):
        out_ref[peer] = part


def total_of(sums_ref):
    value = sums_ref[0]
    for peer in range(1, sums_ref.shape[0]):
        value = value + sums_ref[peer]
    return value


def add_up(sums_ref, out_ref):
    out_ref[...] = total_of(sums_ref)


def split_difference(mine_ref, left_ref, delta_ref, turned_ref):
    difference = left_ref[...] - mine_ref[...]
    for index, part in enumerate(three_parts(difference)):
        delta_ref[index] = part
    for index, part in enumerate(three_parts(difference.T)):
        turned_ref[index] = part


def middle_main(sum_ref, other_ref, main_ref, value_ref, image_ref, scale_ref, ratios_ref):
    split = main_ref.shape[1]
    value = sum_ref[...] + other_ref[...]
    value_ref[...] = value[:, split:]
    image_ref[...] = split_product(value[:, :split], [main_ref[i] for i in range(3)], 0)
    pivots, ratios = factorize(gram_of(value), image_ref.shape)
    scale_ref[...] = 1.0 / jnp.sqrt(pivots)
    for index, ratio in enumerate(ratios):
        ratios_ref[index] = ratio


def middle_late(value_ref, image_ref, scale_ref, ratios_ref, turned_ref, mine_ref, left_ref, late_ref, out_ref):
    split = turned_ref.shape[2]
    late = three_parts(left_ref[...] - mine_ref[...])
    for index, part in enumerate(late):
        late_ref[index] = part
    image = image_ref[...] + split_product(value_ref[...], late, 0)
    factor = forward_substitute([ratios_ref[k] for k in range(ratios_ref.shape[0])], image) * scale_ref[...]
    first = split_product(factor, [turned_ref[i] for i in range(3)], 0)
    last = split_product(factor, late, 1)
    for peer in range(out_ref.shape[0]):
        out_ref[peer, :, :split] = first
        out_ref[peer, :, split:] = last


def last_step(sums_ref, main_ref, late_ref, packed_ref):
    _, rank, rows = sums_ref.shape
    columns = main_ref.shape[2]
    value = total_of(sums_ref)
    packed_ref[:, :rows] = value
    image = split_product(
        value, [jnp.concatenate([main_ref[i], late_ref[i]], axis=0) for i in range(3)], 0
    )
    pivots, ratios = factorize(gram_of(value), image.shape)
    image = forward_substitute(ratios, image)
    packed_ref[:, rows:rows + columns] = back_substitute(ratios, image * (1.0 / pivots))
    packed_ref[:, rows + columns:] = image * (1.0 / jnp.sqrt(pivots))


def update_left(main_ref, late_ref, packed_ref, new_ref):
    rows, columns = new_ref.shape
    weights = GOSSIP_RATE * packed_ref[:, rows:rows + columns]
    start = 0
    for matrix_ref in (main_ref, late_ref):
        piece = pl.ds(start, matrix_ref.shape[0])
        new_ref[piece] = matrix_ref[...] + outer_product(packed_ref[:, piece], weights)
        start += matrix_ref.shape[0]


def update_right(matrix_ref, packed_ref, new_hbm, warm_hbm, new_vmem, warm_vmem, sems):
    rows, columns = matrix_ref.shape
    tile = rows // TILES
    warm_vmem[...] = packed_ref[:, rows + columns:]
    copies = [pltpu.make_async_copy(warm_vmem, warm_hbm.at[0], sems.at[TILES])]
    copies[0].start()
    weights = -GOSSIP_RATE * packed_ref[:, rows:rows + columns]
    for index in range(TILES):
        piece = pl.ds(index * tile, tile)
        new_vmem[piece] = matrix_ref[piece] + outer_product(packed_ref[:, piece], weights)
        copy = pltpu.make_async_copy(new_vmem.at[piece], new_hbm.at[0, piece], sems.at[index])
        copy.start()
        copies.append(copy)
    for copy in copies:
        copy.wait()


def sum_over_y(spread):
    peers = lax.axis_size("tp")
    groups = [list(range(start, peers, 2)) for start in range(2)]
    spread = lax.all_to_all(spread, "tp", 0, 0, axis_index_groups=groups)
    _, rank, rows = spread.shape
    return kernel_call(
        add_up, jax.ShapeDtypeStruct((rank, rows), jnp.float32), spread.size, 4 * spread.size
    )(spread)


def per_device(params, warm):
    _, rows, columns = params.shape
    rank = warm.shape[1]
    peers = lax.axis_size("tp")
    count = lax.axis_size("blk")
    one = rank * rows * columns * 2
    block = rows * columns * 4
    f32 = jnp.float32
    to_right = [(i, (i + 1) % count) for i in range(count)]
    to_left = [(i, (i - 1) % count) for i in range(count)]
    split_at = rows // 16 * SIXTEENTHS
    run = count // RUNS
    ends = [run * (i + 1) - 1 for i in range(RUNS)]
    swap_ends = [(i, i) for i in range(count) if i not in ends]
    swap_ends += [(end, ends[index - 1]) for index, end in enumerate(ends)]
    in_run = [(i, i // run * run + (i + 1) % run) for i in range(count)]

    def spread(peers):
        return jax.ShapeDtypeStruct((peers, rank, rows), f32)

    def split(rows):
        return jax.ShapeDtypeStruct((3, rows, columns), jnp.bfloat16)

    def turned(rows):
        return jax.ShapeDtypeStruct((3, columns, rows), jnp.bfloat16)

    matrix = jax.ShapeDtypeStruct((rows, columns), f32)
    hbm = pl.BlockSpec(memory_space=pltpu.HBM)
    factor_scratch = pltpu.VMEM((rank, columns), f32)
    sems = pltpu.SemaphoreType.DMA((TILES + 1,))

    packed, parts, main, late = kernel_call(
        own_product,
        (
            jax.ShapeDtypeStruct((rank, rows + columns), f32), turned(rows),
            jax.ShapeDtypeStruct((split_at, columns), f32),
            jax.ShapeDtypeStruct((rows - split_at, columns), f32),
        ),
        6 * one, 2 * block, in_specs=[hbm, hbm], scratch_shapes=[factor_scratch, sems],
    )(pltpu.with_memory_space_constraint(warm, pltpu.HBM), pltpu.with_memory_space_constraint(params, pltpu.HBM))
    packed = lax.ppermute(packed, "blk", to_right)
    left_main = lax.ppermute(main, "blk", to_right)
    carried = lax.ppermute(late, "blk", swap_ends)
    sums = kernel_call(spread_first, spread(peers // 2), 450 * one, block)(packed, parts)
    sums = sum_over_y(sums)
    carried, sums = lax.optimization_barrier((carried, sums))
    left_late = lax.ppermute(carried, "blk", in_run)
    other = lax.ppermute(sums, "tp", [(i, i ^ 1) for i in range(peers)])
    delta_main, delta_turned = kernel_call(
        split_difference, (split(split_at), turned(split_at)), one // 64, 3 * block
    )(main, left_main)
    factor_shape = jax.ShapeDtypeStruct((rank, columns), f32)
    value, image, scale, ratios = kernel_call(
        middle_main,
        (
            jax.ShapeDtypeStruct((rank, rows - split_at), f32), factor_shape, factor_shape,
            jax.ShapeDtypeStruct((rank - 1, rank, columns), f32),
        ),
        6 * one, 2 * block,
    )(sums, other, delta_main)
    delta_late, sums = kernel_call(middle_late, (split(rows - split_at), spread(peers)), 6 * one, 2 * block)(
        value, image, scale, ratios, delta_turned, late, left_late
    )
    sums = lax.all_to_all(sums, "tp", 0, 0)
    own = kernel_call(
        last_step, jax.ShapeDtypeStruct((rank, rows + 2 * columns), f32), 6 * one, 2 * block
    )(sums, delta_main, delta_late)
    right = lax.ppermute(own, "blk", to_left)
    left_done = kernel_call(update_left, matrix, 6 * one, 2 * block)(main, late, own)
    new_params, next_warm = kernel_call(
        update_right,
        (jax.ShapeDtypeStruct(params.shape, f32), jax.ShapeDtypeStruct(warm.shape, f32)),
        6 * one, 2 * block, out_specs=(hbm, hbm),
        scratch_shapes=[pltpu.VMEM(matrix.shape, f32), factor_scratch, sems],
    )(left_done, right)
    return new_params, next_warm


def solution(mesh):
    spec = P("blk", None, "tp")
    return jax.shard_map(
        per_device, mesh=mesh, in_specs=(spec, spec), out_specs=(spec, spec), check_vma=False
    )
```

```python
import jax
import jax.numpy as jnp
from jax import lax
from jax.experimental import pallas as pl
from jax.experimental.pallas import tpu as pltpu
from jax.sharding import PartitionSpec as P

GOSSIP_RATE = 0.5
TILES = 4
CARRIED = (4, 2)
RUNS = 2


def kernel_call(body, out_shape, flops, moved, **blocks):
    return pl.pallas_call(
        body,
        out_shape=out_shape,
        **blocks,
        compiler_params=pltpu.CompilerParams(vmem_limit_bytes=24 << 20),
        cost_estimate=pl.CostEstimate(flops=flops, bytes_accessed=moved, transcendentals=0),
    )


def three_parts(value):
    high = value.astype(jnp.bfloat16)
    rest = value - high.astype(jnp.float32)
    middle = rest.astype(jnp.bfloat16)
    low = (rest - middle.astype(jnp.float32)).astype(jnp.bfloat16)
    return high, middle, low


def stack(parts):
    return jnp.concatenate([p.astype(jnp.float32) for p in parts], axis=0).astype(jnp.bfloat16)


def bf16_dot(a, b, a_dim, b_dim):
    return lax.dot_general(
        a, b, (((a_dim,), (b_dim,)), ((), ())), preferred_element_type=jnp.float32
    )


def split_product(rows, parts, contract):
    rank = rows.shape[0]
    stacked = stack(three_parts(rows))
    total = None
    for taken, part in reversed(list(zip((3, 2, 1), parts))):
        products = bf16_dot(stacked[:taken * rank], part, 1, contract)
        for index in reversed(range(taken)):
            term = products[index * rank:(index + 1) * rank]
            total = term if total is None else total + term
    return total


def gram_of(rows):
    rank = rows.shape[0]
    stacked = stack(three_parts(rows))
    products = bf16_dot(stacked, stacked, 1, 1)
    total = None
    for i, j in ((1, 1), (0, 2), (2, 0), (0, 1), (1, 0), (0, 0)):
        term = products[i * rank:(i + 1) * rank, j * rank:(j + 1) * rank]
        total = term if total is None else total + term
    return total


def outer_product(values, weights):
    left, right = three_parts(values), three_parts(weights)
    pairs = ((1, 1), (0, 2), (2, 0), (0, 1), (1, 0), (0, 0))
    return bf16_dot(stack([left[i] for i, _ in pairs]), stack([right[j] for _, j in pairs]), 0, 0)


def factorize(gram, shape):
    rank = gram.shape[0]
    row_index = lax.broadcasted_iota(jnp.int32, shape, 0)
    columns = [jnp.broadcast_to(gram[:, k:k + 1], shape) for k in range(rank)]
    pivots = jnp.ones(shape, jnp.float32)
    ratios = []
    for k in range(rank):
        pivot = columns[k][k:k + 1, :]
        pivots = jnp.where(row_index == k, pivot, pivots)
        if k + 1 < rank:
            ratio = jnp.where(row_index > k, columns[k] * (1.0 / pivot), 0.0)
            ratios.append(ratio)
            for j in range(k + 1, rank):
                columns[j] = columns[j] - ratio * columns[j][k:k + 1, :]
    return pivots, ratios


def forward_substitute(ratios, value):
    for k, ratio in enumerate(ratios):
        value = value - ratio * value[k:k + 1, :]
    return value


def back_substitute(ratios, value):
    row_index = lax.broadcasted_iota(jnp.int32, value.shape, 0)
    for k in reversed(range(len(ratios))):
        below = jnp.sum(ratios[k] * value, axis=0, keepdims=True)
        value = jnp.where(row_index == k, value - below, value)
    return value


def own_product(q_hbm, matrix_hbm, packed_ref, parts_ref, main_ref, late_ref, last_ref, q_vmem, sems):
    split, middle = main_ref.shape[0], main_ref.shape[0] + late_ref.shape[0]
    rows = middle + last_ref.shape[0]
    copies = [pltpu.make_async_copy(q_hbm.at[0], q_vmem, sems.at[TILES])]
    for index, (start, place) in enumerate([(split, late_ref), (middle, last_ref), (0, main_ref)]):
        piece = pl.ds(start, place.shape[0])
        copies.append(pltpu.make_async_copy(matrix_hbm.at[0, piece], place, sems.at[index]))
    for copy in copies:
        copy.start()
    copies[0].wait()
    q = q_vmem[...]
    packed_ref[:, rows:] = q

    def multiply(start, matrix):
        end = start + matrix.shape[0]
        parts = three_parts(matrix.T)
        for number, part in enumerate(parts):
            parts_ref[number, :, start:end] = part
        packed_ref[:, start:end] = split_product(q, parts, 0)

    copies[1].wait()
    copies[2].wait()
    multiply(split, jnp.concatenate([late_ref[...], last_ref[...]], axis=0))
    copies[3].wait()
    multiply(0, main_ref[...])


def spread_first(packed_ref, parts_ref, out_ref):
    rows = parts_ref.shape[2]
    mine = split_product(packed_ref[:, rows:], [parts_ref[i] for i in range(3)], 0)
    part = packed_ref[:, :rows] - mine
    for peer in range(out_ref.shape[0]):
        out_ref[peer] = part


def total_of(sums_ref):
    value = sums_ref[0]
    for peer in range(1, sums_ref.shape[0]):
        value = value + sums_ref[peer]
    return value


def add_up(sums_ref, out_ref):
    out_ref[...] = total_of(sums_ref)


def split_difference(mine_ref, left_ref, delta_ref, turned_ref):
    difference = left_ref[...] - mine_ref[...]
    for index, part in enumerate(three_parts(difference)):
        delta_ref[index] = part
    for index, part in enumerate(three_parts(difference.T)):
        turned_ref[index] = part


def middle_main(sum_ref, other_ref, main_ref, value_ref, image_ref, scale_ref, ratios_ref):
    split = main_ref.shape[1]
    value = sum_ref[...] + other_ref[...]
    value_ref[...] = value[:, split:]
    image_ref[...] = split_product(value[:, :split], [main_ref[i] for i in range(3)], 0)
    pivots, ratios = factorize(gram_of(value), image_ref.shape)
    scale_ref[...] = 1.0 / jnp.sqrt(pivots)
    for index, ratio in enumerate(ratios):
        ratios_ref[index] = ratio


def middle_late(value_ref, image_ref, scale_ref, ratios_ref, turned_ref, *refs):
    mine_refs, left_refs, (late_ref, out_ref) = refs[:2], refs[2:4], refs[4:]
    split = turned_ref.shape[2]
    late = three_parts(jnp.concatenate(
        [left_ref[...] - mine_ref[...] for left_ref, mine_ref in zip(left_refs, mine_refs)], axis=0
    ))
    for index, part in enumerate(late):
        late_ref[index] = part
    image = image_ref[...] + split_product(value_ref[...], late, 0)
    factor = forward_substitute([ratios_ref[k] for k in range(ratios_ref.shape[0])], image) * scale_ref[...]
    first = split_product(factor, [turned_ref[i] for i in range(3)], 0)
    last = split_product(factor, late, 1)
    for peer in range(out_ref.shape[0]):
        out_ref[peer, :, :split] = first
        out_ref[peer, :, split:] = last


def last_step(sums_ref, main_ref, late_ref, packed_ref):
    _, rank, rows = sums_ref.shape
    columns = main_ref.shape[2]
    value = total_of(sums_ref)
    packed_ref[:, :rows] = value
    image = split_product(
        value, [jnp.concatenate([main_ref[i], late_ref[i]], axis=0) for i in range(3)], 0
    )
    pivots, ratios = factorize(gram_of(value), image.shape)
    image = forward_substitute(ratios, image)
    packed_ref[:, rows:rows + columns] = back_substitute(ratios, image * (1.0 / pivots))
    packed_ref[:, rows + columns:] = image * (1.0 / jnp.sqrt(pivots))


def update_left(*refs):
    piece_refs, (packed_ref, new_ref) = refs[:-2], refs[-2:]
    rows, columns = new_ref.shape
    weights = GOSSIP_RATE * packed_ref[:, rows:rows + columns]
    start = 0
    for matrix_ref in piece_refs:
        piece = pl.ds(start, matrix_ref.shape[0])
        new_ref[piece] = matrix_ref[...] + outer_product(packed_ref[:, piece], weights)
        start += matrix_ref.shape[0]


def update_right(matrix_ref, packed_ref, new_hbm, warm_hbm, new_vmem, warm_vmem, sems):
    rows, columns = matrix_ref.shape
    tile = rows // TILES
    warm_vmem[...] = packed_ref[:, rows + columns:]
    copies = [pltpu.make_async_copy(warm_vmem, warm_hbm.at[0], sems.at[TILES])]
    copies[0].start()
    weights = -GOSSIP_RATE * packed_ref[:, rows:rows + columns]
    for index in range(TILES):
        piece = pl.ds(index * tile, tile)
        new_vmem[piece] = matrix_ref[piece] + outer_product(packed_ref[:, piece], weights)
        copy = pltpu.make_async_copy(new_vmem.at[piece], new_hbm.at[0, piece], sems.at[index])
        copy.start()
        copies.append(copy)
    for copy in copies:
        copy.wait()


def sum_over_y(spread):
    peers = lax.axis_size("tp")
    groups = [list(range(start, peers, 2)) for start in range(2)]
    spread = lax.all_to_all(spread, "tp", 0, 0, axis_index_groups=groups)
    _, rank, rows = spread.shape
    return kernel_call(
        add_up, jax.ShapeDtypeStruct((rank, rows), jnp.float32), spread.size, 4 * spread.size
    )(spread)


def per_device(params, warm):
    _, rows, columns = params.shape
    rank = warm.shape[1]
    peers = lax.axis_size("tp")
    count = lax.axis_size("blk")
    one = rank * rows * columns * 2
    block = rows * columns * 4
    f32 = jnp.float32
    to_right = [(i, (i + 1) % count) for i in range(count)]
    to_left = [(i, (i - 1) % count) for i in range(count)]
    carried_rows = [rows // 16 * part for part in CARRIED]
    split_at = rows - sum(carried_rows)
    run = count // RUNS
    ends = [run * (i + 1) - 1 for i in range(RUNS)]
    swap_ends = [(i, i) for i in range(count) if i not in ends]
    swap_ends += [(end, ends[index - 1]) for index, end in enumerate(ends)]
    in_run = [(i, i // run * run + (i + 1) % run) for i in range(count)]

    def spread(peers):
        return jax.ShapeDtypeStruct((peers, rank, rows), f32)

    def split(rows):
        return jax.ShapeDtypeStruct((3, rows, columns), jnp.bfloat16)

    def turned(rows):
        return jax.ShapeDtypeStruct((3, columns, rows), jnp.bfloat16)

    matrix = jax.ShapeDtypeStruct((rows, columns), f32)
    hbm = pl.BlockSpec(memory_space=pltpu.HBM)
    factor_scratch = pltpu.VMEM((rank, columns), f32)
    sems = pltpu.SemaphoreType.DMA((TILES + 1,))

    packed, parts, main, *late = kernel_call(
        own_product,
        (
            jax.ShapeDtypeStruct((rank, rows + columns), f32), turned(rows),
            jax.ShapeDtypeStruct((split_at, columns), f32),
            *[jax.ShapeDtypeStruct((part, columns), f32) for part in carried_rows],
        ),
        6 * one, 2 * block, in_specs=[hbm, hbm], scratch_shapes=[factor_scratch, sems],
    )(pltpu.with_memory_space_constraint(warm, pltpu.HBM), pltpu.with_memory_space_constraint(params, pltpu.HBM))
    packed = lax.ppermute(packed, "blk", to_right)
    left_main = lax.ppermute(main, "blk", to_right)
    carried = [lax.ppermute(part, "blk", swap_ends) for part in late]
    sums = kernel_call(spread_first, spread(peers // 2), 400 * one, block)(packed, parts)
    sums = sum_over_y(sums)
    carried, sums = lax.optimization_barrier((carried, sums))
    left_late = [lax.ppermute(part, "blk", in_run) for part in carried]
    other = lax.ppermute(sums, "tp", [(i, i ^ 1) for i in range(peers)])
    delta_main, delta_turned = kernel_call(
        split_difference, (split(split_at), turned(split_at)), one // 64, 3 * block
    )(main, left_main)
    factor_shape = jax.ShapeDtypeStruct((rank, columns), f32)
    value, image, scale, ratios = kernel_call(
        middle_main,
        (
            jax.ShapeDtypeStruct((rank, rows - split_at), f32), factor_shape, factor_shape,
            jax.ShapeDtypeStruct((rank - 1, rank, columns), f32),
        ),
        6 * one, 2 * block,
    )(sums, other, delta_main)
    delta_late, sums = kernel_call(middle_late, (split(rows - split_at), spread(peers)), 6 * one, 2 * block)(
        value, image, scale, ratios, delta_turned, *late, *left_late
    )
    sums = lax.all_to_all(sums, "tp", 0, 0)
    own = kernel_call(
        last_step, jax.ShapeDtypeStruct((rank, rows + 2 * columns), f32), 6 * one, 2 * block
    )(sums, delta_main, delta_late)
    right = lax.ppermute(own, "blk", to_left)
    left_done = kernel_call(update_left, matrix, 6 * one, 2 * block)(main, *late, own)
    new_params, next_warm = kernel_call(
        update_right,
        (jax.ShapeDtypeStruct(params.shape, f32), jax.ShapeDtypeStruct(warm.shape, f32)),
        6 * one, 2 * block, out_specs=(hbm, hbm),
        scratch_shapes=[pltpu.VMEM(matrix.shape, f32), factor_scratch, sems],
    )(left_done, right)
    return new_params, next_warm


def solution(mesh):
    spec = P("blk", None, "tp")
    return jax.shard_map(
        per_device, mesh=mesh, in_specs=(spec, spec), out_specs=(spec, spec), check_vma=False
    )
```

```python
import jax
import jax.numpy as jnp
from jax import lax
from jax.experimental import pallas as pl
from jax.experimental.pallas import tpu as pltpu
from jax.sharding import PartitionSpec as P

GOSSIP_RATE = 0.5
TILES = 4
SIXTEENTHS = 11
RUNS = 2


def kernel_call(body, out_shape, flops, moved, **blocks):
    return pl.pallas_call(
        body,
        out_shape=out_shape,
        **blocks,
        compiler_params=pltpu.CompilerParams(vmem_limit_bytes=24 << 20),
        cost_estimate=pl.CostEstimate(flops=flops, bytes_accessed=moved, transcendentals=0),
    )


def three_parts(value):
    high = value.astype(jnp.bfloat16)
    rest = value - high.astype(jnp.float32)
    middle = rest.astype(jnp.bfloat16)
    low = (rest - middle.astype(jnp.float32)).astype(jnp.bfloat16)
    return high, middle, low


def stack(parts):
    return jnp.concatenate([p.astype(jnp.float32) for p in parts], axis=0).astype(jnp.bfloat16)


def bf16_dot(a, b, a_dim, b_dim):
    return lax.dot_general(
        a, b, (((a_dim,), (b_dim,)), ((), ())), preferred_element_type=jnp.float32
    )


def split_product(rows, parts, contract):
    rank = rows.shape[0]
    stacked = stack(three_parts(rows))
    total = None
    for taken, part in reversed(list(zip((3, 2, 1), parts))):
        products = bf16_dot(stacked[:taken * rank], part, 1, contract)
        for index in reversed(range(taken)):
            term = products[index * rank:(index + 1) * rank]
            total = term if total is None else total + term
    return total


def gram_of(rows):
    rank = rows.shape[0]
    stacked = stack(three_parts(rows))
    products = bf16_dot(stacked, stacked, 1, 1)
    total = None
    for i, j in ((1, 1), (0, 2), (2, 0), (0, 1), (1, 0), (0, 0)):
        term = products[i * rank:(i + 1) * rank, j * rank:(j + 1) * rank]
        total = term if total is None else total + term
    return total


def outer_product(values, weights):
    left, right = three_parts(values), three_parts(weights)
    pairs = ((1, 1), (0, 2), (2, 0), (0, 1), (1, 0), (0, 0))
    return bf16_dot(stack([left[i] for i, _ in pairs]), stack([right[j] for _, j in pairs]), 0, 0)


def factorize(gram, shape):
    rank = gram.shape[0]
    row_index = lax.broadcasted_iota(jnp.int32, shape, 0)
    columns = [jnp.broadcast_to(gram[:, k:k + 1], shape) for k in range(rank)]
    pivots = jnp.ones(shape, jnp.float32)
    ratios = []
    for k in range(rank):
        pivot = columns[k][k:k + 1, :]
        pivots = jnp.where(row_index == k, pivot, pivots)
        if k + 1 < rank:
            ratio = jnp.where(row_index > k, columns[k] * (1.0 / pivot), 0.0)
            ratios.append(ratio)
            for j in range(k + 1, rank):
                columns[j] = columns[j] - ratio * columns[j][k:k + 1, :]
    return pivots, ratios


def forward_substitute(ratios, value):
    for k, ratio in enumerate(ratios):
        value = value - ratio * value[k:k + 1, :]
    return value


def back_substitute(ratios, value):
    row_index = lax.broadcasted_iota(jnp.int32, value.shape, 0)
    for k in reversed(range(len(ratios))):
        below = jnp.sum(ratios[k] * value, axis=0, keepdims=True)
        value = jnp.where(row_index == k, value - below, value)
    return value


def own_product(q_hbm, matrix_hbm, packed_ref, parts_ref, main_ref, late_ref, q_vmem, sems):
    split = main_ref.shape[0]
    rows = split + late_ref.shape[0]
    pieces = [(split, rows), (0, split)]
    places = [late_ref, main_ref]
    copies = [pltpu.make_async_copy(q_hbm.at[0], q_vmem, sems.at[TILES])]
    for index, (start, end) in enumerate(pieces):
        piece = pl.ds(start, end - start)
        copies.append(pltpu.make_async_copy(matrix_hbm.at[0, piece], places[index], sems.at[index]))
    for copy in copies:
        copy.start()
    copies[0].wait()
    q = q_vmem[...]
    packed_ref[:, rows:] = q
    for index, (start, end) in enumerate(pieces):
        copies[index + 1].wait()
        parts = three_parts(places[index][...].T)
        for number, part in enumerate(parts):
            parts_ref[number, :, start:end] = part
        packed_ref[:, start:end] = split_product(q, parts, 0)


def spread_first(packed_ref, parts_ref, out_ref):
    rows = parts_ref.shape[2]
    mine = split_product(packed_ref[:, rows:], [parts_ref[i] for i in range(3)], 0)
    part = packed_ref[:, :rows] - mine
    for peer in range(out_ref.shape[0]):
        out_ref[peer] = part


def total_of(sums_ref):
    value = sums_ref[0]
    for peer in range(1, sums_ref.shape[0]):
        value = value + sums_ref[peer]
    return value


def add_up(sums_ref, out_ref):
    out_ref[...] = total_of(sums_ref)


def split_difference(mine_ref, left_ref, delta_ref, turned_ref):
    difference = left_ref[...] - mine_ref[...]
    for index, part in enumerate(three_parts(difference)):
        delta_ref[index] = part
    for index, part in enumerate(three_parts(difference.T)):
        turned_ref[index] = part


def middle_main(sum_ref, other_ref, main_ref, value_ref, image_ref, scale_ref, ratios_ref):
    split = main_ref.shape[1]
    value = sum_ref[...] + other_ref[...]
    value_ref[...] = value[:, split:]
    image_ref[...] = split_product(value[:, :split], [main_ref[i] for i in range(3)], 0)
    pivots, ratios = factorize(gram_of(value), image_ref.shape)
    scale_ref[...] = 1.0 / jnp.sqrt(pivots)
    for index, ratio in enumerate(ratios):
        ratios_ref[index] = ratio


def middle_late(value_ref, image_ref, scale_ref, ratios_ref, turned_ref, mine_ref, left_ref, late_ref, out_ref):
    split = turned_ref.shape[2]
    late = three_parts(left_ref[...] - mine_ref[...])
    for index, part in enumerate(late):
        late_ref[index] = part
    image = image_ref[...] + split_product(value_ref[...], late, 0)
    factor = forward_substitute([ratios_ref[k] for k in range(ratios_ref.shape[0])], image) * scale_ref[...]
    first = split_product(factor, [turned_ref[i] for i in range(3)], 0)
    last = split_product(factor, late, 1)
    for peer in range(out_ref.shape[0]):
        out_ref[peer, :, :split] = first
        out_ref[peer, :, split:] = last


def last_step(sums_ref, main_ref, late_ref, packed_ref):
    _, rank, rows = sums_ref.shape
    columns = main_ref.shape[2]
    value = total_of(sums_ref)
    packed_ref[:, :rows] = value
    image = split_product(
        value, [jnp.concatenate([main_ref[i], late_ref[i]], axis=0) for i in range(3)], 0
    )
    pivots, ratios = factorize(gram_of(value), image.shape)
    image = forward_substitute(ratios, image)
    packed_ref[:, rows:rows + columns] = back_substitute(ratios, image * (1.0 / pivots))
    packed_ref[:, rows + columns:] = image * (1.0 / jnp.sqrt(pivots))


def update_left(main_ref, late_ref, packed_ref, new_ref):
    rows, columns = new_ref.shape
    weights = GOSSIP_RATE * packed_ref[:, rows:rows + columns]
    start = 0
    for matrix_ref in (main_ref, late_ref):
        piece = pl.ds(start, matrix_ref.shape[0])
        new_ref[piece] = matrix_ref[...] + outer_product(packed_ref[:, piece], weights)
        start += matrix_ref.shape[0]


def update_right(matrix_ref, packed_ref, new_hbm, warm_hbm, new_vmem, warm_vmem, sems):
    rows, columns = matrix_ref.shape
    bounds = (0, rows // 8, rows // 2, rows)
    warm_vmem[...] = packed_ref[:, rows + columns:]
    copies = [pltpu.make_async_copy(warm_vmem, warm_hbm.at[0], sems.at[TILES])]
    copies[0].start()
    weights = -GOSSIP_RATE * packed_ref[:, rows:rows + columns]
    for index, (start, end) in enumerate(zip(bounds, bounds[1:])):
        piece = pl.ds(start, end - start)
        new_vmem[piece] = matrix_ref[piece] + outer_product(packed_ref[:, piece], weights)
        copy = pltpu.make_async_copy(new_vmem.at[piece], new_hbm.at[0, piece], sems.at[index])
        copy.start()
        copies.append(copy)
    for copy in copies:
        copy.wait()


def sum_over_y(spread):
    peers = lax.axis_size("tp")
    groups = [list(range(start, peers, 2)) for start in range(2)]
    spread = lax.all_to_all(spread, "tp", 0, 0, axis_index_groups=groups)
    _, rank, rows = spread.shape
    return kernel_call(
        add_up, jax.ShapeDtypeStruct((rank, rows), jnp.float32), spread.size, 4 * spread.size
    )(spread)


def per_device(params, warm):
    _, rows, columns = params.shape
    rank = warm.shape[1]
    peers = lax.axis_size("tp")
    count = lax.axis_size("blk")
    one = rank * rows * columns * 2
    block = rows * columns * 4
    f32 = jnp.float32
    to_right = [(i, (i + 1) % count) for i in range(count)]
    to_left = [(i, (i - 1) % count) for i in range(count)]
    split_at = rows // 16 * SIXTEENTHS
    run = count // RUNS
    ends = [run * (i + 1) - 1 for i in range(RUNS)]
    swap_ends = [(i, i) for i in range(count) if i not in ends]
    swap_ends += [(end, ends[index - 1]) for index, end in enumerate(ends)]
    in_run = [(i, i // run * run + (i + 1) % run) for i in range(count)]

    def spread(peers):
        return jax.ShapeDtypeStruct((peers, rank, rows), f32)

    def split(rows):
        return jax.ShapeDtypeStruct((3, rows, columns), jnp.bfloat16)

    def turned(rows):
        return jax.ShapeDtypeStruct((3, columns, rows), jnp.bfloat16)

    matrix = jax.ShapeDtypeStruct((rows, columns), f32)
    hbm = pl.BlockSpec(memory_space=pltpu.HBM)
    factor_scratch = pltpu.VMEM((rank, columns), f32)
    sems = pltpu.SemaphoreType.DMA((TILES + 1,))

    packed, parts, main, late = kernel_call(
        own_product,
        (
            jax.ShapeDtypeStruct((rank, rows + columns), f32), turned(rows),
            jax.ShapeDtypeStruct((split_at, columns), f32),
            jax.ShapeDtypeStruct((rows - split_at, columns), f32),
        ),
        6 * one, 2 * block, in_specs=[hbm, hbm], scratch_shapes=[factor_scratch, sems],
    )(pltpu.with_memory_space_constraint(warm, pltpu.HBM), pltpu.with_memory_space_constraint(params, pltpu.HBM))
    packed = lax.ppermute(packed, "blk", to_right)
    left_main = lax.ppermute(main, "blk", to_right)
    carried = lax.ppermute(late, "blk", swap_ends)
    sums = kernel_call(spread_first, spread(peers // 2), 450 * one, block)(packed, parts)
    sums = sum_over_y(sums)
    carried, sums = lax.optimization_barrier((carried, sums))
    left_late = lax.ppermute(carried, "blk", in_run)
    other = lax.ppermute(sums, "tp", [(i, i ^ 1) for i in range(peers)])
    delta_main, delta_turned = kernel_call(
        split_difference, (split(split_at), turned(split_at)), one // 64, 3 * block
    )(main, left_main)
    factor_shape = jax.ShapeDtypeStruct((rank, columns), f32)
    value, image, scale, ratios = kernel_call(
        middle_main,
        (
            jax.ShapeDtypeStruct((rank, rows - split_at), f32), factor_shape, factor_shape,
            jax.ShapeDtypeStruct((rank - 1, rank, columns), f32),
        ),
        6 * one, 2 * block,
    )(sums, other, delta_main)
    delta_late, sums = kernel_call(middle_late, (split(rows - split_at), spread(peers)), 6 * one, 2 * block)(
        value, image, scale, ratios, delta_turned, late, left_late
    )
    sums = lax.all_to_all(sums, "tp", 0, 0)
    own = kernel_call(
        last_step, jax.ShapeDtypeStruct((rank, rows + 2 * columns), f32), 6 * one, 2 * block
    )(sums, delta_main, delta_late)
    right = lax.ppermute(own, "blk", to_left)
    left_done = kernel_call(update_left, matrix, 6 * one, 2 * block)(main, late, own)
    new_params, next_warm = kernel_call(
        update_right,
        (jax.ShapeDtypeStruct(params.shape, f32), jax.ShapeDtypeStruct(warm.shape, f32)),
        6 * one, 2 * block, out_specs=(hbm, hbm),
        scratch_shapes=[pltpu.VMEM(matrix.shape, f32), factor_scratch, sems],
    )(left_done, right)
    return new_params, next_warm


def solution(mesh):
    spec = P("blk", None, "tp")
    return jax.shard_map(
        per_device, mesh=mesh, in_specs=(spec, spec), out_specs=(spec, spec), check_vma=False
    )
```

```python
import jax
import jax.numpy as jnp
from jax import lax
from jax.experimental import pallas as pl
from jax.experimental.pallas import tpu as pltpu
from jax.sharding import PartitionSpec as P

GOSSIP_RATE = 0.5
TILES = 4
DIRECT = 23
RUNS = 2


def kernel_call(body, out_shape, flops, moved, **blocks):
    return pl.pallas_call(
        body,
        out_shape=out_shape,
        **blocks,
        compiler_params=pltpu.CompilerParams(vmem_limit_bytes=24 << 20),
        cost_estimate=pl.CostEstimate(flops=flops, bytes_accessed=moved, transcendentals=0),
    )


def three_parts(value):
    high = value.astype(jnp.bfloat16)
    rest = value - high.astype(jnp.float32)
    middle = rest.astype(jnp.bfloat16)
    low = (rest - middle.astype(jnp.float32)).astype(jnp.bfloat16)
    return high, middle, low


def stack(parts):
    return jnp.concatenate([p.astype(jnp.float32) for p in parts], axis=0).astype(jnp.bfloat16)


def bf16_dot(a, b, a_dim, b_dim):
    return lax.dot_general(
        a, b, (((a_dim,), (b_dim,)), ((), ())), preferred_element_type=jnp.float32
    )


def split_product(rows, parts, contract):
    rank = rows.shape[0]
    stacked = stack(three_parts(rows))
    total = None
    for taken, part in reversed(list(zip((3, 2, 1), parts))):
        products = bf16_dot(stacked[:taken * rank], part, 1, contract)
        for index in reversed(range(taken)):
            term = products[index * rank:(index + 1) * rank]
            total = term if total is None else total + term
    return total


def gram_of(rows):
    rank = rows.shape[0]
    stacked = stack(three_parts(rows))
    products = bf16_dot(stacked, stacked, 1, 1)
    total = None
    for i, j in ((1, 1), (0, 2), (2, 0), (0, 1), (1, 0), (0, 0)):
        term = products[i * rank:(i + 1) * rank, j * rank:(j + 1) * rank]
        total = term if total is None else total + term
    return total


def outer_product(values, weights):
    left, right = three_parts(values), three_parts(weights)
    pairs = ((1, 1), (0, 2), (2, 0), (0, 1), (1, 0), (0, 0))
    return bf16_dot(stack([left[i] for i, _ in pairs]), stack([right[j] for _, j in pairs]), 0, 0)


def factorize(gram, shape):
    rank = gram.shape[0]
    row_index = lax.broadcasted_iota(jnp.int32, shape, 0)
    columns = [jnp.broadcast_to(gram[:, k:k + 1], shape) for k in range(rank)]
    pivots = jnp.ones(shape, jnp.float32)
    ratios = []
    for k in range(rank):
        pivot = columns[k][k:k + 1, :]
        pivots = jnp.where(row_index == k, pivot, pivots)
        if k + 1 < rank:
            ratio = jnp.where(row_index > k, columns[k] * (1.0 / pivot), 0.0)
            ratios.append(ratio)
            for j in range(k + 1, rank):
                columns[j] = columns[j] - ratio * columns[j][k:k + 1, :]
    return pivots, ratios


def forward_substitute(ratios, value):
    for k, ratio in enumerate(ratios):
        value = value - ratio * value[k:k + 1, :]
    return value


def back_substitute(ratios, value):
    row_index = lax.broadcasted_iota(jnp.int32, value.shape, 0)
    for k in reversed(range(len(ratios))):
        below = jnp.sum(ratios[k] * value, axis=0, keepdims=True)
        value = jnp.where(row_index == k, value - below, value)
    return value


def own_product(q_hbm, matrix_hbm, packed_ref, parts_ref, main_ref, late_ref, q_vmem, sems):
    split = main_ref.shape[0]
    rows = split + late_ref.shape[0]
    pieces = [(split, rows), (0, split)]
    places = [late_ref, main_ref]
    copies = [pltpu.make_async_copy(q_hbm.at[0], q_vmem, sems.at[TILES])]
    for index, (start, end) in enumerate(pieces):
        piece = pl.ds(start, end - start)
        copies.append(pltpu.make_async_copy(matrix_hbm.at[0, piece], places[index], sems.at[index]))
    for copy in copies:
        copy.start()
    copies[0].wait()
    q = q_vmem[...]
    packed_ref[:, rows:] = q
    for index, (start, end) in enumerate(pieces):
        copies[index + 1].wait()
        parts = three_parts(places[index][...].T)
        for number, part in enumerate(parts):
            parts_ref[number, :, start:end] = part
        packed_ref[:, start:end] = split_product(q, parts, 0)


def spread_first(packed_ref, parts_ref, out_ref):
    rows = parts_ref.shape[2]
    mine = split_product(packed_ref[:, rows:], [parts_ref[i] for i in range(3)], 0)
    part = packed_ref[:, :rows] - mine
    for peer in range(out_ref.shape[0]):
        out_ref[peer] = part


def total_of(sums_ref):
    value = sums_ref[0]
    for peer in range(1, sums_ref.shape[0]):
        value = value + sums_ref[peer]
    return value


def add_up(sums_ref, out_ref):
    out_ref[...] = total_of(sums_ref)


def split_difference(mine_ref, left_ref, delta_ref, turned_ref):
    difference = left_ref[...] - mine_ref[...]
    for index, part in enumerate(three_parts(difference)):
        delta_ref[index] = part
    for index, part in enumerate(three_parts(difference.T)):
        turned_ref[index] = part


def middle_main(sum_ref, other_ref, main_ref, value_ref, image_ref, scale_ref, ratios_ref):
    split = main_ref.shape[1]
    value = sum_ref[...] + other_ref[...]
    value_ref[...] = value[:, split:]
    image_ref[...] = split_product(value[:, :split], [main_ref[i] for i in range(3)], 0)
    pivots, ratios = factorize(gram_of(value), image_ref.shape)
    scale_ref[...] = 1.0 / jnp.sqrt(pivots)
    for index, ratio in enumerate(ratios):
        ratios_ref[index] = ratio


def middle_late(value_ref, image_ref, scale_ref, ratios_ref, turned_ref, mine_ref, left_ref, late_ref, out_ref):
    split = turned_ref.shape[2]
    late = three_parts(left_ref[...] - mine_ref[...])
    for index, part in enumerate(late):
        late_ref[index] = part
    image = image_ref[...] + split_product(value_ref[...], late, 0)
    factor = forward_substitute([ratios_ref[k] for k in range(ratios_ref.shape[0])], image) * scale_ref[...]
    first = split_product(factor, [turned_ref[i] for i in range(3)], 0)
    last = split_product(factor, late, 1)
    for peer in range(out_ref.shape[0]):
        out_ref[peer, :, :split] = first
        out_ref[peer, :, split:] = last


def last_step(sums_ref, main_ref, late_ref, packed_ref):
    _, rank, rows = sums_ref.shape
    columns = main_ref.shape[2]
    value = total_of(sums_ref)
    packed_ref[:, :rows] = value
    image = split_product(
        value, [jnp.concatenate([main_ref[i], late_ref[i]], axis=0) for i in range(3)], 0
    )
    pivots, ratios = factorize(gram_of(value), image.shape)
    image = forward_substitute(ratios, image)
    packed_ref[:, rows:rows + columns] = back_substitute(ratios, image * (1.0 / pivots))
    packed_ref[:, rows + columns:] = image * (1.0 / jnp.sqrt(pivots))


def update_left(main_ref, late_ref, packed_ref, new_ref):
    rows, columns = new_ref.shape
    weights = GOSSIP_RATE * packed_ref[:, rows:rows + columns]
    start = 0
    for matrix_ref in (main_ref, late_ref):
        piece = pl.ds(start, matrix_ref.shape[0])
        new_ref[piece] = matrix_ref[...] + outer_product(packed_ref[:, piece], weights)
        start += matrix_ref.shape[0]


def update_right(matrix_ref, packed_ref, new_hbm, warm_hbm, new_vmem, warm_vmem, sems):
    rows, columns = matrix_ref.shape
    tile = rows // TILES
    warm_vmem[...] = packed_ref[:, rows + columns:]
    copies = [pltpu.make_async_copy(warm_vmem, warm_hbm.at[0], sems.at[TILES])]
    copies[0].start()
    weights = -GOSSIP_RATE * packed_ref[:, rows:rows + columns]
    for index in range(TILES):
        piece = pl.ds(index * tile, tile)
        new_vmem[piece] = matrix_ref[piece] + outer_product(packed_ref[:, piece], weights)
        copy = pltpu.make_async_copy(new_vmem.at[piece], new_hbm.at[0, piece], sems.at[index])
        copy.start()
        copies.append(copy)
    for copy in copies:
        copy.wait()


def sum_over_y(spread):
    peers = lax.axis_size("tp")
    groups = [list(range(start, peers, 2)) for start in range(2)]
    spread = lax.all_to_all(spread, "tp", 0, 0, axis_index_groups=groups)
    _, rank, rows = spread.shape
    return kernel_call(
        add_up, jax.ShapeDtypeStruct((rank, rows), jnp.float32), spread.size, 4 * spread.size
    )(spread)


def per_device(params, warm):
    _, rows, columns = params.shape
    rank = warm.shape[1]
    peers = lax.axis_size("tp")
    count = lax.axis_size("blk")
    one = rank * rows * columns * 2
    block = rows * columns * 4
    f32 = jnp.float32
    to_right = [(i, (i + 1) % count) for i in range(count)]
    to_left = [(i, (i - 1) % count) for i in range(count)]
    split_at = rows // 32 * DIRECT
    run = count // RUNS
    ends = [run * (i + 1) - 1 for i in range(RUNS)]
    swap_ends = [(i, i) for i in range(count) if i not in ends]
    swap_ends += [(end, ends[index - 1]) for index, end in enumerate(ends)]
    in_run = [(i, i // run * run + (i + 1) % run) for i in range(count)]

    def spread(peers):
        return jax.ShapeDtypeStruct((peers, rank, rows), f32)

    def split(rows):
        return jax.ShapeDtypeStruct((3, rows, columns), jnp.bfloat16)

    def turned(rows):
        return jax.ShapeDtypeStruct((3, columns, rows), jnp.bfloat16)

    matrix = jax.ShapeDtypeStruct((rows, columns), f32)
    hbm = pl.BlockSpec(memory_space=pltpu.HBM)
    factor_scratch = pltpu.VMEM((rank, columns), f32)
    sems = pltpu.SemaphoreType.DMA((TILES + 1,))

    packed, parts, main, late = kernel_call(
        own_product,
        (
            jax.ShapeDtypeStruct((rank, rows + columns), f32), turned(rows),
            jax.ShapeDtypeStruct((split_at, columns), f32),
            jax.ShapeDtypeStruct((rows - split_at, columns), f32),
        ),
        6 * one, 2 * block, in_specs=[hbm, hbm], scratch_shapes=[factor_scratch, sems],
    )(pltpu.with_memory_space_constraint(warm, pltpu.HBM), pltpu.with_memory_space_constraint(params, pltpu.HBM))
    packed = lax.ppermute(packed, "blk", to_right)
    left_main = lax.ppermute(main, "blk", to_right)
    carried = lax.ppermute(late, "blk", swap_ends)
    sums = kernel_call(spread_first, spread(peers // 2), 600 * one, block)(packed, parts)
    sums = sum_over_y(sums)
    carried, sums = lax.optimization_barrier((carried, sums))
    left_late = lax.ppermute(carried, "blk", in_run)
    other = lax.ppermute(sums, "tp", [(i, i ^ 1) for i in range(peers)])
    delta_main, delta_turned = kernel_call(
        split_difference, (split(split_at), turned(split_at)), one // 64, 3 * block
    )(main, left_main)
    factor_shape = jax.ShapeDtypeStruct((rank, columns), f32)
    value, image, scale, ratios = kernel_call(
        middle_main,
        (
            jax.ShapeDtypeStruct((rank, rows - split_at), f32), factor_shape, factor_shape,
            jax.ShapeDtypeStruct((rank - 1, rank, columns), f32),
        ),
        6 * one, 2 * block,
    )(sums, other, delta_main)
    delta_late, sums = kernel_call(middle_late, (split(rows - split_at), spread(peers)), 6 * one, 2 * block)(
        value, image, scale, ratios, delta_turned, late, left_late
    )
    sums = lax.all_to_all(sums, "tp", 0, 0)
    own = kernel_call(
        last_step, jax.ShapeDtypeStruct((rank, rows + 2 * columns), f32), 6 * one, 2 * block
    )(sums, delta_main, delta_late)
    right = lax.ppermute(own, "blk", to_left)
    left_done = kernel_call(update_left, matrix, 6 * one, 2 * block)(main, late, own)
    new_params, next_warm = kernel_call(
        update_right,
        (jax.ShapeDtypeStruct(params.shape, f32), jax.ShapeDtypeStruct(warm.shape, f32)),
        6 * one, 2 * block, out_specs=(hbm, hbm),
        scratch_shapes=[pltpu.VMEM(matrix.shape, f32), factor_scratch, sems],
    )(left_done, right)
    return new_params, next_warm


def solution(mesh):
    spec = P("blk", None, "tp")
    return jax.shard_map(
        per_device, mesh=mesh, in_specs=(spec, spec), out_specs=(spec, spec), check_vma=False
    )
```

```python
import jax
import jax.numpy as jnp
from jax import lax
from jax.experimental import pallas as pl
from jax.experimental.pallas import tpu as pltpu
from jax.sharding import PartitionSpec as P

GOSSIP_RATE = 0.5
TILES = 4
SIXTEENTHS = 11
RUNS = 2


def kernel_call(body, out_shape, flops, moved, **blocks):
    return pl.pallas_call(
        body,
        out_shape=out_shape,
        **blocks,
        compiler_params=pltpu.CompilerParams(vmem_limit_bytes=24 << 20),
        cost_estimate=pl.CostEstimate(flops=flops, bytes_accessed=moved, transcendentals=0),
    )


def three_parts(value):
    high = value.astype(jnp.bfloat16)
    rest = value - high.astype(jnp.float32)
    middle = rest.astype(jnp.bfloat16)
    low = (rest - middle.astype(jnp.float32)).astype(jnp.bfloat16)
    return high, middle, low


def stack(parts):
    return jnp.concatenate([p.astype(jnp.float32) for p in parts], axis=0).astype(jnp.bfloat16)


def bf16_dot(a, b, a_dim, b_dim):
    return lax.dot_general(
        a, b, (((a_dim,), (b_dim,)), ((), ())), preferred_element_type=jnp.float32
    )


def split_product(rows, parts, contract):
    rank = rows.shape[0]
    stacked = stack(three_parts(rows))
    total = None
    for taken, part in reversed(list(zip((3, 2, 1), parts))):
        products = bf16_dot(stacked[:taken * rank], part, 1, contract)
        for index in reversed(range(taken)):
            term = products[index * rank:(index + 1) * rank]
            total = term if total is None else total + term
    return total


def gram_of(rows):
    rank = rows.shape[0]
    stacked = stack(three_parts(rows))
    products = bf16_dot(stacked, stacked, 1, 1)
    total = None
    for i, j in ((1, 1), (0, 2), (2, 0), (0, 1), (1, 0), (0, 0)):
        term = products[i * rank:(i + 1) * rank, j * rank:(j + 1) * rank]
        total = term if total is None else total + term
    return total


def outer_product(values, weights):
    left, right = three_parts(values), three_parts(weights)
    pairs = ((1, 1), (0, 2), (2, 0), (0, 1), (1, 0), (0, 0))
    return bf16_dot(stack([left[i] for i, _ in pairs]), stack([right[j] for _, j in pairs]), 0, 0)


def factorize(gram, shape):
    rank = gram.shape[0]
    row_index = lax.broadcasted_iota(jnp.int32, shape, 0)
    columns = [jnp.broadcast_to(gram[:, k:k + 1], shape) for k in range(rank)]
    pivots = jnp.ones(shape, jnp.float32)
    ratios = []
    for k in range(rank):
        pivot = columns[k][k:k + 1, :]
        pivots = jnp.where(row_index == k, pivot, pivots)
        if k + 1 < rank:
            ratio = jnp.where(row_index > k, columns[k] * (1.0 / pivot), 0.0)
            ratios.append(ratio)
            for j in range(k + 1, rank):
                columns[j] = columns[j] - ratio * columns[j][k:k + 1, :]
    return pivots, ratios


def forward_substitute(ratios, value):
    for k, ratio in enumerate(ratios):
        value = value - ratio * value[k:k + 1, :]
    return value


def back_substitute(ratios, value):
    row_index = lax.broadcasted_iota(jnp.int32, value.shape, 0)
    for k in reversed(range(len(ratios))):
        below = jnp.sum(ratios[k] * value, axis=0, keepdims=True)
        value = jnp.where(row_index == k, value - below, value)
    return value


def own_product(q_hbm, matrix_hbm, packed_ref, parts_ref, main_ref, late_ref, q_vmem, sems):
    split = main_ref.shape[0]
    rows = split + late_ref.shape[0]
    pieces = [(split, rows), (0, split)]
    places = [late_ref, main_ref]
    copies = [pltpu.make_async_copy(q_hbm.at[0], q_vmem, sems.at[TILES])]
    for index, (start, end) in enumerate(pieces):
        piece = pl.ds(start, end - start)
        copies.append(pltpu.make_async_copy(matrix_hbm.at[0, piece], places[index], sems.at[index]))
    for copy in copies:
        copy.start()
    copies[0].wait()
    q = q_vmem[...]
    packed_ref[:, rows:] = q
    for index, (start, end) in enumerate(pieces):
        copies[index + 1].wait()
        parts = three_parts(places[index][...].T)
        for number, part in enumerate(parts):
            parts_ref[number, :, start:end] = part
        packed_ref[:, start:end] = split_product(q, parts, 0)


def spread_first(packed_ref, parts_ref, out_ref):
    rows = parts_ref.shape[2]
    mine = split_product(packed_ref[:, rows:], [parts_ref[i] for i in range(3)], 0)
    part = packed_ref[:, :rows] - mine
    for peer in range(out_ref.shape[0]):
        out_ref[peer] = part


def total_of(sums_ref):
    value = sums_ref[0]
    for peer in range(1, sums_ref.shape[0]):
        value = value + sums_ref[peer]
    return value


def add_up(sums_ref, out_ref):
    out_ref[...] = total_of(sums_ref)


def split_difference(mine_ref, left_ref, delta_ref, turned_ref):
    difference = left_ref[...] - mine_ref[...]
    for index, part in enumerate(three_parts(difference)):
        delta_ref[index] = part
    for index, part in enumerate(three_parts(difference.T)):
        turned_ref[index] = part


def middle_main(sum_ref, other_ref, main_ref, value_ref, image_ref, scale_ref, ratios_ref):
    split = main_ref.shape[1]
    value = sum_ref[...] + other_ref[...]
    value_ref[...] = value[:, split:]
    image_ref[...] = split_product(value[:, :split], [main_ref[i] for i in range(3)], 0)
    pivots, ratios = factorize(gram_of(value), image_ref.shape)
    scale_ref[...] = 1.0 / jnp.sqrt(pivots)
    for index, ratio in enumerate(ratios):
        ratios_ref[index] = ratio


def middle_late(value_ref, image_ref, scale_ref, ratios_ref, turned_ref, mine_ref, left_ref, late_ref, out_ref):
    split = turned_ref.shape[2]
    late = three_parts(left_ref[...] - mine_ref[...])
    for index, part in enumerate(late):
        late_ref[index] = part
    image = image_ref[...] + split_product(value_ref[...], late, 0)
    factor = forward_substitute([ratios_ref[k] for k in range(ratios_ref.shape[0])], image) * scale_ref[...]
    first = split_product(factor, [turned_ref[i] for i in range(3)], 0)
    last = split_product(factor, late, 1)
    for peer in range(out_ref.shape[0]):
        out_ref[peer, :, :split] = first
        out_ref[peer, :, split:] = last


def last_step(sums_ref, main_ref, late_ref, packed_ref):
    _, rank, rows = sums_ref.shape
    columns = main_ref.shape[2]
    value = total_of(sums_ref)
    packed_ref[:, :rows] = value
    image = split_product(
        value, [jnp.concatenate([main_ref[i], late_ref[i]], axis=0) for i in range(3)], 0
    )
    pivots, ratios = factorize(gram_of(value), image.shape)
    image = forward_substitute(ratios, image)
    packed_ref[:, rows:rows + columns] = back_substitute(ratios, image * (1.0 / pivots))
    packed_ref[:, rows + columns:] = image * (1.0 / jnp.sqrt(pivots))


def update_left(main_ref, late_ref, packed_ref, new_ref):
    rows, columns = new_ref.shape
    weights = GOSSIP_RATE * packed_ref[:, rows:rows + columns]
    start = 0
    for matrix_ref in (main_ref, late_ref):
        piece = pl.ds(start, matrix_ref.shape[0])
        new_ref[piece] = matrix_ref[...] + outer_product(packed_ref[:, piece], weights)
        start += matrix_ref.shape[0]


def update_right(matrix_ref, packed_ref, new_hbm, warm_hbm, new_vmem, warm_vmem, sems):
    rows, columns = matrix_ref.shape
    tile = rows // TILES
    warm_vmem[...] = packed_ref[:, rows + columns:]
    copies = [pltpu.make_async_copy(warm_vmem, warm_hbm.at[0], sems.at[TILES])]
    copies[0].start()
    weights = -GOSSIP_RATE * packed_ref[:, rows:rows + columns]
    for index in range(TILES):
        piece = pl.ds(index * tile, tile)
        new_vmem[piece] = matrix_ref[piece] + outer_product(packed_ref[:, piece], weights)
        copy = pltpu.make_async_copy(new_vmem.at[piece], new_hbm.at[0, piece], sems.at[index])
        copy.start()
        copies.append(copy)
    for copy in copies:
        copy.wait()


def sum_over_y(spread, carried):
    peers = lax.axis_size("tp")
    groups = [list(range(start, peers, 2)) for start in range(2)]
    spread = lax.all_to_all(spread, "tp", 0, 0, axis_index_groups=groups)
    carried, spread = lax.optimization_barrier((carried, spread))
    _, rank, rows = spread.shape
    total = kernel_call(
        add_up, jax.ShapeDtypeStruct((rank, rows), jnp.float32), spread.size, 4 * spread.size
    )(spread)
    return total, carried


def per_device(params, warm):
    _, rows, columns = params.shape
    rank = warm.shape[1]
    peers = lax.axis_size("tp")
    count = lax.axis_size("blk")
    one = rank * rows * columns * 2
    block = rows * columns * 4
    f32 = jnp.float32
    to_right = [(i, (i + 1) % count) for i in range(count)]
    to_left = [(i, (i - 1) % count) for i in range(count)]
    split_at = rows // 16 * SIXTEENTHS
    run = count // RUNS
    ends = [run * (i + 1) - 1 for i in range(RUNS)]
    swap_ends = [(i, i) for i in range(count) if i not in ends]
    swap_ends += [(end, ends[index - 1]) for index, end in enumerate(ends)]
    in_run = [(i, i // run * run + (i + 1) % run) for i in range(count)]

    def spread(peers):
        return jax.ShapeDtypeStruct((peers, rank, rows), f32)

    def split(rows):
        return jax.ShapeDtypeStruct((3, rows, columns), jnp.bfloat16)

    def turned(rows):
        return jax.ShapeDtypeStruct((3, columns, rows), jnp.bfloat16)

    matrix = jax.ShapeDtypeStruct((rows, columns), f32)
    hbm = pl.BlockSpec(memory_space=pltpu.HBM)
    factor_scratch = pltpu.VMEM((rank, columns), f32)
    sems = pltpu.SemaphoreType.DMA((TILES + 1,))

    packed, parts, main, late = kernel_call(
        own_product,
        (
            jax.ShapeDtypeStruct((rank, rows + columns), f32), turned(rows),
            jax.ShapeDtypeStruct((split_at, columns), f32),
            jax.ShapeDtypeStruct((rows - split_at, columns), f32),
        ),
        6 * one, 2 * block, in_specs=[hbm, hbm], scratch_shapes=[factor_scratch, sems],
    )(pltpu.with_memory_space_constraint(warm, pltpu.HBM), pltpu.with_memory_space_constraint(params, pltpu.HBM))
    packed = lax.ppermute(packed, "blk", to_right)
    left_main = lax.ppermute(main, "blk", to_right)
    carried = lax.ppermute(late, "blk", swap_ends)
    sums = kernel_call(spread_first, spread(peers // 2), 450 * one, block)(packed, parts)
    sums, carried = sum_over_y(sums, carried)
    left_late = lax.ppermute(carried, "blk", in_run)
    other = lax.ppermute(sums, "tp", [(i, i ^ 1) for i in range(peers)])
    delta_main, delta_turned = kernel_call(
        split_difference, (split(split_at), turned(split_at)), one // 64, 3 * block
    )(main, left_main)
    factor_shape = jax.ShapeDtypeStruct((rank, columns), f32)
    value, image, scale, ratios = kernel_call(
        middle_main,
        (
            jax.ShapeDtypeStruct((rank, rows - split_at), f32), factor_shape, factor_shape,
            jax.ShapeDtypeStruct((rank - 1, rank, columns), f32),
        ),
        6 * one, 2 * block,
    )(sums, other, delta_main)
    delta_late, sums = kernel_call(middle_late, (split(rows - split_at), spread(peers)), 6 * one, 2 * block)(
        value, image, scale, ratios, delta_turned, late, left_late
    )
    sums = lax.all_to_all(sums, "tp", 0, 0)
    own = kernel_call(
        last_step, jax.ShapeDtypeStruct((rank, rows + 2 * columns), f32), 6 * one, 2 * block
    )(sums, delta_main, delta_late)
    right = lax.ppermute(own, "blk", to_left)
    left_done = kernel_call(update_left, matrix, 6 * one, 2 * block)(main, late, own)
    new_params, next_warm = kernel_call(
        update_right,
        (jax.ShapeDtypeStruct(params.shape, f32), jax.ShapeDtypeStruct(warm.shape, f32)),
        6 * one, 2 * block, out_specs=(hbm, hbm),
        scratch_shapes=[pltpu.VMEM(matrix.shape, f32), factor_scratch, sems],
    )(left_done, right)
    return new_params, next_warm


def solution(mesh):
    spec = P("blk", None, "tp")
    return jax.shard_map(
        per_device, mesh=mesh, in_specs=(spec, spec), out_specs=(spec, spec), check_vma=False
    )
```
